1024 devices in a mesh: stream: 32 (over x, y, core), cross: 32 (over z).
Axes of the slice: x: 4, y: 4, z: 32, core: 2. Of those that a mesh axis runs over, the one named last changes fastest.
Arguments:
- sources: float32 [2, 32, 32, 8, 8, 128], P(None, 'stream', 'cross'), may hold values from -6 to 6
Outputs:
- correction: float32 [2, 32, 32, 8, 8, 128], P(None, 'stream', 'cross')
The draws below stay inside these ranges and needn't reach their ends.
All inputs are finite; a program needn't handle non-finite values.
Results may differ from the reference program's by a relative error of at most 0.00011.
Values sent between devices are 32-bit elements; how exact they have to be, the bound alone decides.
A program may use at most 64 MiB of HBM per device.

```python
import math
import jax
import jax.numpy as jnp
import numpy as np
from jax import lax

ORDER = 7
MID_ORDER = 3
RHS = 2
EZ = 16
NXE = 32
NYE = 32


def shard_levels(key, dims, cuts, smallest, top_value):
    gain, own = 1.0, jax.random.fold_in(key, 6)
    for dim, parts in cuts:
        steps = jnp.exp(jax.random.uniform(jax.random.fold_in(own, dim), (parts,), jnp.float32, smallest / len(cuts), top_value / len(cuts)))
        gain = gain * jnp.repeat(steps, dims[dim] // parts).reshape([-1 if axis == dim else 1 for axis in range(len(dims))])
    return gain


def noise(own_key, extent, scale, limit, split=(), kind=jnp.bfloat16):
    entries = scale * jax.random.normal(own_key, extent, jnp.float32)
    if split:
        entries = entries * shard_levels(own_key, extent, split, -0.22, 0.18)
    return jnp.clip(entries, -limit, limit).astype(kind)


def setup_inputs(seed: int = 0) -> dict:
    key_of = jax.random.split(jax.random.key(seed), 2)
    sources = noise(key_of[0], (RHS, NXE, NYE, ORDER + 1, ORDER + 1, EZ * (ORDER + 1)), 1.0, 6.0, ((1, 32), (2, 32)), jnp.float32)
    return {"sources": sources}


PRECISE = lax.Precision.HIGHEST

def legendre_pair(degree, points):
    below_poly = np.ones(points.shape)
    top_poly = points.copy()
    for order_step in range(2, degree + 1):
        below_poly, top_poly = (top_poly, ((2 * order_step - 1) * points * top_poly - (order_step - 1) * below_poly) / order_step)
    return (below_poly, top_poly)

def gll_tables(degree):
    gll_nodes = -np.cos(np.pi * np.arange(degree + 1) / degree)
    for newton_step in range(100):
        below_poly, top_poly = legendre_pair(degree, gll_nodes)
        gll_nodes = gll_nodes - (gll_nodes * top_poly - below_poly) / ((degree + 1) * top_poly)
    at_nodes = legendre_pair(degree, gll_nodes)[1]
    weights = 2.0 / (degree * (degree + 1) * at_nodes ** 2)
    node_count = degree + 1
    derivative = np.zeros((node_count, node_count))
    for target in range(node_count):
        for source in range(node_count):
            if target != source:
                derivative[target, source] = at_nodes[target] / (at_nodes[source] * (gll_nodes[target] - gll_nodes[source]))
    derivative[0, 0] = -degree * (degree + 1) / 4.0
    derivative[degree, degree] = degree * (degree + 1) / 4.0
    stiffness = derivative.T @ (weights[:, None] * derivative)
    return (gll_nodes, weights, stiffness)

def lagrange_matrix(fine_degree, coarse_degree):
    fine_nodes = gll_tables(fine_degree)[0]
    coarse_nodes = gll_tables(coarse_degree)[0]
    lagrange_table = np.ones((fine_degree + 1, coarse_degree + 1))
    for column in range(coarse_degree + 1):
        for other_node in range(coarse_degree + 1):
            if other_node != column:
                lagrange_table[:, column] *= (fine_nodes - coarse_nodes[other_node]) / (coarse_nodes[column] - coarse_nodes[other_node])
    return jnp.asarray(lagrange_table, jnp.float32)

def smoother_bounds(degree):
    stiffness = gll_tables(degree)[2]
    elements = 6
    size_total = elements * degree
    assembled = np.zeros((size_total, size_total))
    for element in range(elements):
        for local_row in range(degree + 1):
            for local_col in range(degree + 1):
                assembled[(element * degree + local_row) % size_total, (element * degree + local_col) % size_total] += stiffness[local_row, local_col]
    diagonal = np.sqrt(assembled[np.arange(size_total), np.arange(size_total)])
    scaled = assembled / diagonal[:, None] / diagonal[None, :]
    positions = np.arange(size_total)
    vector = np.where(positions % 2 == 0, 1.0, -1.0) * (1.0 + positions / size_total)
    for power_step in range(2000):
        vector = scaled @ vector
        vector = vector / np.sqrt(np.sum(vector * vector))
    upper_bound = float(np.sum(vector * (scaled @ vector)) / np.sum(vector * vector))
    return (0.1 * upper_bound, upper_bound)

def static_tables(degree, span_blocks):
    weights, stiffness = gll_tables(degree)[1:]
    stiff_sum = np.array([stiffness[index, index] for index in range(degree + 1)])
    stiff_sum[0] = stiffness[0, 0] + stiffness[degree, degree]
    stiff_sum[degree] = stiffness[0, 0] + stiffness[degree, degree]
    mass_sum = weights.copy()
    mass_sum[0] = weights[0] + weights[degree]
    mass_sum[degree] = weights[0] + weights[degree]
    shared = np.ones(degree + 1)
    shared[0] = 2.0
    shared[degree] = 2.0
    diagonal = stiff_sum[:, None, None] * mass_sum[None, :, None] * mass_sum[None, None, :] + mass_sum[:, None, None] * stiff_sum[None, :, None] * mass_sum[None, None, :] + mass_sum[:, None, None] * mass_sum[None, :, None] * stiff_sum[None, None, :]
    inverse_share = 1.0 / (shared[:, None, None] * shared[None, :, None] * shared[None, None, :])
    diag_tile = jnp.asarray(np.tile(1.0 / diagonal, (1, 1, span_blocks)), jnp.float32)
    share_tile = jnp.asarray(np.tile(inverse_share, (1, 1, span_blocks)), jnp.float32)
    return (jnp.asarray(stiffness, jnp.float32), jnp.asarray(weights, jnp.float32), diag_tile, share_tile)

def wall_mask(row_total, node_count):
    element_rows = jnp.arange(row_total, dtype=jnp.int32)
    node_rows = jnp.arange(node_count, dtype=jnp.int32)
    bottom = (element_rows[:, None] == 0) & (node_rows[None, :] == 0)
    top_wall = (element_rows[:, None] == row_total - 1) & (node_rows[None, :] == node_count - 1)
    wall_keep = jnp.where(bottom | top_wall, 0.0, 1.0).astype(jnp.float32)
    return wall_keep[None, None, :, None, :, None]

def build_level(degree, span_blocks, row_total):
    stiffness, weights, diag_tile, share_tile = static_tables(degree, span_blocks)
    lower_bound, upper_bound = smoother_bounds(degree) if degree > 1 else (1.0, 2.0)
    return (degree + 1, stiffness, weights, diag_tile, share_tile, wall_mask(row_total, degree + 1), lower_bound, upper_bound)

def local_apply(nodal_field, stiffness, weights):
    node_count = stiffness.shape[0]
    blocks = nodal_field.reshape(nodal_field.shape[:5] + (nodal_field.shape[5] // node_count, node_count))
    along_first = jnp.einsum('ai,rxyijzk->rxyajzk', stiffness, blocks, precision=PRECISE)
    along_second = jnp.einsum('bj,rxyijzk->rxyibzk', stiffness, blocks, precision=PRECISE)
    along_third = jnp.einsum('ck,rxyijzk->rxyijzc', stiffness, blocks, precision=PRECISE)
    weight_first = weights[:, None, None, None]
    weight_second = weights[None, :, None, None]
    weight_third = weights[None, None, None, :]
    total_sum = along_first * weight_second * weight_third + along_second * weight_first * weight_third + along_third * weight_first * weight_second
    return total_sum.reshape(nodal_field.shape)

def sum_spanwise(nodal_field, node_count):
    blocks = nodal_field.reshape(nodal_field.shape[:5] + (nodal_field.shape[5] // node_count, node_count))
    joined = blocks[..., node_count - 1] + jnp.roll(blocks[..., 0], -1, axis=5)
    blocks = blocks.at[..., node_count - 1].set(joined)
    blocks = blocks.at[..., 0].set(jnp.roll(joined, 1, axis=5))
    return blocks.reshape(nodal_field.shape)

def sum_streamwise(nodal_field, node_count):
    final_node = node_count - 1
    first_face = nodal_field[:, :, :, 0]
    last_face = nodal_field[:, :, :, final_node]
    before = jnp.roll(last_face, 1, axis=1)
    following = jnp.roll(first_face, -1, axis=1)
    nodal_field = nodal_field.at[:, :, :, 0].set(first_face + before)
    return nodal_field.at[:, :, :, final_node].set(last_face + following)

def sum_wallnormal(nodal_field, node_count):
    final_node = node_count - 1
    first_face = nodal_field[:, :, :, :, 0]
    last_face = nodal_field[:, :, :, :, final_node]
    zero_row = jnp.zeros_like(first_face[:, :, :1])
    before = jnp.concatenate([zero_row, last_face[:, :, :-1]], axis=2)
    following = jnp.concatenate([first_face[:, :, 1:], zero_row], axis=2)
    nodal_field = nodal_field.at[:, :, :, :, 0].set(first_face + before)
    return nodal_field.at[:, :, :, :, final_node].set(last_face + following)

def assemble(nodal_field, node_count):
    return sum_wallnormal(sum_streamwise(sum_spanwise(nodal_field, node_count), node_count), node_count)

def operate(nodal_field, level_data):
    return level_data[5] * assemble(local_apply(nodal_field, level_data[1], level_data[2]), level_data[0])

def chebyshev(approx, residual, level_data, keep_residual):
    lower_bound = level_data[6]
    upper_bound = level_data[7]
    center = 0.5 * (upper_bound + lower_bound)
    spread = 0.5 * (upper_bound - lower_bound)
    sigma_ratio = center / spread
    rho_first = 1.0 / sigma_ratio
    rho_second = 1.0 / (2.0 * sigma_ratio - rho_first)
    scaling = level_data[5] * level_data[3]
    update = scaling * residual / center
    approx = approx + update
    residual = residual - operate(update, level_data)
    update = rho_second * rho_first * update + 2.0 * rho_second / spread * scaling * residual
    approx = approx + update
    if keep_residual:
        residual = residual - operate(update, level_data)
    return (approx, residual)

def restrict(nodal_field, lagrange_table):
    fine_count, coarse_count = lagrange_table.shape
    blocks = nodal_field.reshape(nodal_field.shape[:5] + (nodal_field.shape[5] // fine_count, fine_count))
    reduced = jnp.einsum('ia,jb,kc,rxyijzk->rxyabzc', lagrange_table, lagrange_table, lagrange_table, blocks, precision=PRECISE)
    return reduced.reshape(nodal_field.shape[:3] + (coarse_count, coarse_count, reduced.shape[5] * coarse_count))

def prolong(coarse_values, lagrange_table):
    fine_count, coarse_count = lagrange_table.shape
    blocks = coarse_values.reshape(coarse_values.shape[:5] + (coarse_values.shape[5] // coarse_count, coarse_count))
    expanded = jnp.einsum('ia,jb,kc,rxyabzc->rxyijzk', lagrange_table, lagrange_table, lagrange_table, blocks, precision=PRECISE)
    return expanded.reshape(coarse_values.shape[:3] + (fine_count, fine_count, expanded.shape[5] * fine_count))

def fourier_rows(row_index, point_index, total_count):
    half_size = total_count // 2
    frequency = jnp.where(row_index <= half_size, row_index, row_index - half_size)
    phase_angle = 2.0 * jnp.pi * (frequency * point_index % total_count).astype(jnp.float32) / total_count
    row_scale = jnp.where((row_index == 0) | (row_index == half_size), math.sqrt(1.0 / total_count), math.sqrt(2.0 / total_count))
    return row_scale * jnp.where(row_index <= half_size, jnp.cos(phase_angle), jnp.sin(phase_angle))

def sine_rows(mode_index, point_index, total_count):
    product = mode_index * point_index % (2 * total_count)
    inside = (mode_index > 0) & (mode_index < total_count) & (point_index > 0) & (point_index < total_count)
    values = math.sqrt(2.0 / total_count) * jnp.sin(jnp.pi * product.astype(jnp.float32) / total_count)
    return jnp.where(inside, values, 0.0).astype(jnp.float32)

def gap_table(wall_index, span_index, wall_total, span_total):
    wall_angle = 0.5 * jnp.pi * wall_index.astype(jnp.float32) / wall_total
    wall_gap = 2.0 * jnp.sin(wall_angle) ** 2 + jnp.where(wall_index == 0, 1.0, 0.0)
    half_size = span_total // 2
    frequency = jnp.where(span_index <= half_size, span_index, span_index - half_size)
    span_gap = 2.0 * jnp.sin(jnp.pi * frequency.astype(jnp.float32) / span_total) ** 2
    return (wall_gap[:, None] + span_gap[None, :]).astype(jnp.float32)

def green_values(distance, half_gap, length):
    sinh_part = jnp.sqrt(half_gap * (2.0 + half_gap))
    decay_rate = jnp.log1p(half_gap + sinh_part)
    numerator = jnp.exp(-decay_rate * distance) + jnp.exp(-decay_rate * (length - distance))
    return numerator / (4.0 * sinh_part * -jnp.expm1(-decay_rate * length))

def expand_coarse(window, stream_blocks, wall_blocks):
    stream_parts = []
    for stream_shift in range(2):
        wall_parts = []
        for wall_shift in range(2):
            base_block = window[:, stream_shift:stream_shift + stream_blocks, wall_shift:wall_shift + wall_blocks]
            span_pair = jnp.stack([base_block, jnp.roll(base_block, -1, axis=3)], axis=4)
            wall_parts.append(span_pair.reshape(base_block.shape[:3] + (base_block.shape[3] * 2,)))
        stream_parts.append(jnp.stack(wall_parts, axis=3))
    return jnp.stack(stream_parts, axis=3)

def coarse_solve(coarse_field):
    values = coarse_field[:, :, :, 0, 0, 0::2]
    nx_total = values.shape[1]
    ny_total = values.shape[2]
    nz_total = values.shape[3]
    span_index = jnp.arange(nz_total, dtype=jnp.int32)
    fourier_table = fourier_rows(span_index[:, None], span_index[None, :], nz_total)
    spectral = jnp.einsum('kz,rxyz->rxyk', fourier_table, values, precision=PRECISE)
    wall_index = jnp.arange(ny_total, dtype=jnp.int32)
    sine_table = sine_rows(wall_index[:, None], wall_index[None, :], ny_total)
    modal_part = jnp.einsum('ay,rxyk->rxak', sine_table, spectral, precision=PRECISE)
    gap_all = gap_table(wall_index, span_index, ny_total, nz_total)
    stream_index = jnp.arange(nx_total, dtype=jnp.int32)
    distance = ((stream_index[:, None] - stream_index[None, :]) % nx_total).astype(jnp.float32)
    kernel = green_values(distance[:, :, None, None], gap_all[None, None], nx_total)
    solved = jnp.einsum('txak,rxak->rtak', kernel, modal_part, precision=PRECISE)
    window_rows = jnp.arange(ny_total + 1, dtype=jnp.int32)
    sine_back = sine_rows(wall_index[:, None], window_rows[None, :], ny_total)
    physical = jnp.einsum('aq,rtak->rtqk', sine_back, solved, precision=PRECISE)
    node_values = jnp.einsum('kz,rtqk->rtqz', fourier_table, physical, precision=PRECISE)
    window = jnp.concatenate([node_values, node_values[:, :1]], axis=1)
    return expand_coarse(window, nx_total, ny_total)

def vcycle(sources):
    row_total = sources.shape[2]
    span_blocks = sources.shape[5] // (ORDER + 1)
    fine = build_level(ORDER, span_blocks, row_total)
    middle = build_level(MID_ORDER, span_blocks, row_total)
    coarse_keep = wall_mask(row_total, 2)
    fine_to_mid = lagrange_matrix(ORDER, MID_ORDER)
    mid_to_coarse = lagrange_matrix(MID_ORDER, 1)
    forcing = fine[5] * assemble(sources, ORDER + 1)
    fine_approx, fine_resid = chebyshev(jnp.zeros_like(forcing), forcing, fine, True)
    mid_forcing = middle[5] * assemble(restrict(fine[4] * fine_resid, fine_to_mid), MID_ORDER + 1)
    mid_approx, mid_resid = chebyshev(jnp.zeros_like(mid_forcing), mid_forcing, middle, True)
    coarse_forcing = coarse_keep * assemble(restrict(middle[4] * mid_resid, mid_to_coarse), 2)
    coarse_values = coarse_solve(coarse_forcing)
    mid_approx = mid_approx + prolong(coarse_values, mid_to_coarse)
    mid_approx = chebyshev(mid_approx, mid_forcing - operate(mid_approx, middle), middle, False)[0]
    fine_approx = fine_approx + prolong(mid_approx, fine_to_mid)
    return chebyshev(fine_approx, forcing - operate(fine_approx, fine), fine, False)[0]

def reference(sources):
    outputs = []
    for source_index in range(RHS):
        outputs.append(vcycle(sources[source_index:source_index + 1]))
    return jnp.concatenate(outputs, axis=0)
```

```python
import functools
import math

import jax
import jax.numpy as jnp
import numpy as np
from jax import lax
from jax.experimental import pallas as pl
from jax.experimental.pallas import tpu as pltpu
from jax.sharding import PartitionSpec as P

ORDER = 7
MID_ORDER = 3
EZ = 16
LANES = 128
MODES = 32
EXACT = lax.Precision.HIGHEST
MESH_ID = pl.DeviceIdType.MESH


def legendre_pair(degree, points):
    below_poly = np.ones(points.shape)
    top_poly = points.copy()
    for step in range(2, degree + 1):
        below_poly, top_poly = (
            top_poly,
            ((2 * step - 1) * points * top_poly - (step - 1) * below_poly) / step,
        )
    return (below_poly, top_poly)


@functools.lru_cache(None)
def gll_tables(degree):
    nodes = -np.cos(np.pi * np.arange(degree + 1) / degree)
    for _ in range(100):
        below_poly, top_poly = legendre_pair(degree, nodes)
        nodes = nodes - (nodes * top_poly - below_poly) / ((degree + 1) * top_poly)
    at_nodes = legendre_pair(degree, nodes)[1]
    weights = 2.0 / (degree * (degree + 1) * at_nodes**2)
    count = degree + 1
    derivative = np.zeros((count, count))
    for target in range(count):
        for source in range(count):
            if target != source:
                derivative[target, source] = at_nodes[target] / (
                    at_nodes[source] * (nodes[target] - nodes[source])
                )
    derivative[0, 0] = -degree * (degree + 1) / 4.0
    derivative[degree, degree] = degree * (degree + 1) / 4.0
    stiffness = derivative.T @ (weights[:, None] * derivative)
    return (nodes, weights, stiffness)


def lagrange_matrix(fine_degree, coarse_degree):
    fine_nodes = gll_tables(fine_degree)[0]
    coarse_nodes = gll_tables(coarse_degree)[0]
    table = np.ones((fine_degree + 1, coarse_degree + 1))
    for column in range(coarse_degree + 1):
        for other in range(coarse_degree + 1):
            if other != column:
                table[:, column] *= (fine_nodes - coarse_nodes[other]) / (
                    coarse_nodes[column] - coarse_nodes[other]
                )
    return table


@functools.lru_cache(None)
def smoother(degree):
    stiffness = gll_tables(degree)[2]
    elements = 6
    size = elements * degree
    assembled = np.zeros((size, size))
    for element in range(elements):
        for row in range(degree + 1):
            for col in range(degree + 1):
                assembled[(element * degree + row) % size, (element * degree + col) % size] += (
                    stiffness[row, col]
                )
    diagonal = np.sqrt(np.diagonal(assembled))
    scaled = assembled / diagonal[:, None] / diagonal[None, :]
    positions = np.arange(size)
    vector = np.where(positions % 2 == 0, 1.0, -1.0) * (1.0 + positions / size)
    for _ in range(2000):
        vector = scaled @ vector
        vector = vector / np.sqrt(np.sum(vector * vector))
    high = float(np.sum(vector * (scaled @ vector)) / np.sum(vector * vector))
    low = 0.1 * high
    theta, delta = 0.5 * (high + low), 0.5 * (high - low)
    sigma = theta / delta
    rho1 = 1.0 / sigma
    rho2 = 1.0 / (2.0 * sigma - rho1)
    return theta, rho2 * rho1, 2.0 * rho2 / delta * theta


def level(degree):
    _, w, k = gll_tables(degree)
    t = w.copy()
    t[0] = t[-1] = w[0] + w[-1]
    s = np.diagonal(k).copy()
    s[0] = s[-1] = k[0, 0] + k[-1, -1]
    c = np.ones(degree + 1)
    c[0] = c[-1] = 0.5
    diag = (
        s[:, None, None] * t[None, :, None] * t[None, None, :]
        + t[:, None, None] * s[None, :, None] * t[None, None, :]
        + t[:, None, None] * t[None, :, None] * s[None, None, :]
    )
    return w, k, t, c, 1.0 / (diag * smoother(degree)[0])


def join_z(count):
    size = EZ * count
    m = np.eye(size)
    for e in range(EZ):
        a, b = e * count + count - 1, ((e + 1) % EZ) * count
        m[a, b] += 1.0
        m[b, a] += 1.0
    return m


def two(m):
    return np.kron(np.eye(2), m)


def lanes(values):
    return np.broadcast_to(values[None, :], (8, LANES))


def rows(values):
    return np.broadcast_to(np.asarray(values)[..., None], np.shape(values) + (LANES,))


def fourier_rows(total):
    k, n = np.meshgrid(np.arange(total), np.arange(total), indexing="ij")
    half = total // 2
    freq = np.where(k <= half, k, k - half)
    angle = 2.0 * np.pi * (freq * n % total) / total
    scale = np.where((k == 0) | (k == half), math.sqrt(1.0 / total), math.sqrt(2.0 / total))
    return scale * np.where(k <= half, np.cos(angle), np.sin(angle))


def sine_rows(mode, point, total):
    product = mode * point % (2 * total)
    inside = (mode > 0) & (mode < total) & (point > 0) & (point < total)
    return np.where(inside, math.sqrt(2.0 / total) * np.sin(np.pi * product / total), 0.0)


def green_table(nx, ny):
    mode = np.arange(MODES)
    wall_gap = 2.0 * np.sin(0.5 * np.pi * mode / ny) ** 2 + np.where(mode % ny == 0, 1.0, 0.0)
    freq = np.arange(EZ)
    freq = np.where(freq <= EZ // 2, freq, freq - EZ // 2)
    span_gap = 2.0 * np.sin(np.pi * freq / EZ) ** 2
    half_gap = wall_gap[:, None] + span_gap[None, :]
    root = np.sqrt(half_gap * (2.0 + half_gap))
    rate = np.log1p(half_gap + root)
    d = np.arange(nx)[:, None, None]
    top = np.exp(-rate * d) + np.exp(-rate * (nx - d))
    return top / (4.0 * root * -np.expm1(-rate * nx))


def modal(values):
    v = values.reshape(values.shape[:-2] + (MODES // 8, 8, EZ))
    v = np.stack([v, v], axis=-2)
    v = np.moveaxis(v, -4, -3)
    return v.reshape(v.shape[:-3] + (LANES,))


def assembled_1d(local_cols, window):
    count = local_cols.shape[0]
    out = np.zeros((count, window))
    out[:, 1:3] += local_cols
    out[0, 0:2] += local_cols[-1]
    out[-1, 2:4] += local_cols[0]
    return out


@functools.lru_cache(None)
def build_tables(nx, ny):
    f, q = ORDER + 1, MID_ORDER + 1
    w7, k7, t7, c7, e7 = level(ORDER)
    w3, k3, t3, c3, e3 = level(MID_ORDER)
    j73 = lagrange_matrix(ORDER, MID_ORDER)
    j31 = lagrange_matrix(MID_ORDER, 1)
    tile = {}
    tk = np.tile(t7, EZ)
    ones = np.ones((8, LANES))
    tile["kx"] = np.stack(
        [np.stack([k7[i, a] * t7[:, None] * tk[None, :] for i in range(f)]) for a in range(f)]
    ).reshape(f * f, 8, LANES)
    roll = np.stack([[k7[j, (j - s) % f] for j in range(f)] for s in range(f)])
    tile["ky"] = roll[:, :, None] * tk[None, None, :]
    tile["e7"] = np.tile(e7, (1, 1, EZ))
    tile["ti"] = np.stack([t * ones for t in t7])
    tile["tij"] = np.stack([t * rows(t7) for t in t7])
    tile["cj"] = rows(c7)[None]
    tile["ci"] = np.stack([c * ones for c in c7])
    tile["jx"] = np.stack([j73[i, a] * ones for i in range(f) for a in range(q)])
    tile["jb"] = np.stack([rows(j73[:, b]) for b in range(q)])
    tile["ji"] = np.stack([j73[i, a] * ones for a in range(q) for i in range(f)])
    green = modal(green_table(nx, ny))
    tile["green"] = green[(np.arange(nx + 3) - 1) % nx]
    point = np.arange(-2, ny + 4)
    tile["sine"] = modal(
        np.broadcast_to(
            sine_rows(np.arange(MODES)[None, :], point[:, None], ny)[:, :, None],
            (len(point), MODES, EZ),
        )
    )
    row = {}
    mid = [(a, b) for a in range(q) for b in range(q)]
    tc = np.tile(np.tile(t3, EZ), 2)

    def left(matrix, scale=None):
        scale = np.ones(LANES) if scale is None else scale
        return matrix.T[:, :, None] * scale[None, None, :]

    row["jy"] = left(
        np.array([[(a == a2) * j73[j, b] for a2 in range(q) for j in range(f)] for a, b in mid])
    )
    row["lx"] = left(np.kron(k3, np.diag(t3)), tc)
    row["ly"] = left(np.kron(np.diag(t3), k3), tc)
    row["e3"] = np.stack([np.tile(np.tile(e3[a, b], EZ), 2) for a, b in mid])[None]
    row["tab"] = rows([t3[a] * t3[b] for a, b in mid])[None]
    row["ca"] = rows([c3[a] for a, b in mid])[None]
    row["cb"] = rows([c3[b] for a, b in mid])[None]
    groups = [np.array([j31[a, x] * j31[b, y] for a, b in mid]) for x in (0, 1) for y in (0, 1)]
    row["jj"] = np.repeat(np.stack(groups, axis=1), MODES, axis=1)[None]
    own = np.zeros((q, 4))
    own[:, 1:3] = j31
    stiff = assembled_1d(k3 @ j31, 4)
    mass = t3[:, None] * own
    row["pj"] = left(np.kron(own, own))
    row["kt"] = left(np.kron(stiff, mass) + np.kron(mass, stiff), tc)
    row["tt"] = left(np.kron(mass, mass))

    mat = {}
    az7 = (join_z(f) @ np.kron(np.eye(EZ), k7)).T
    az3 = two((join_z(q) @ np.kron(np.eye(EZ), k3)).T)
    down = (join_z(q) @ np.kron(np.eye(EZ), j73.T) @ np.diag(np.tile(c7, EZ))).T
    zero = np.zeros_like(down)
    mat["az7"] = az7
    mat["down"] = np.concatenate(
        [np.concatenate([down, zero], axis=1), np.concatenate([zero, down], axis=1)], axis=0
    )
    mat["az3"] = az3
    up = np.kron(np.eye(EZ), j73).T
    mat["up"] = two(up)
    gather = np.zeros((EZ, EZ * q))
    for e in range(EZ):
        for node in (0, 1):
            gather[(e + node) % EZ, e * q : (e + 1) * q] += j31[:, node] * c3
    b1 = two((fourier_rows(EZ) @ gather).T)
    b1 = np.tile(b1, (1, 4))
    mat["b12"] = np.concatenate([b1, az3 @ b1], axis=0)
    spread = np.zeros((EZ * q, EZ))
    for e in range(EZ):
        for node in (0, 1):
            spread[e * q : (e + 1) * q, (e + node) % EZ] += j31[:, node]
    back = two((spread @ fourier_rows(EZ).T).T)
    back = np.tile(back, (4, 1))
    mat["back"] = np.concatenate([back, back @ az3], axis=1)
    mode, here = np.arange(MODES)[:, None], np.arange(32)[None, :]
    s0 = np.where(here < ny, sine_rows(mode, here, ny), 0.0)
    s1 = np.where(here < ny, sine_rows(mode, here + 1, ny), 0.0)
    mat["sin"] = np.concatenate([s0, s1], axis=0)
    packed, where = [], {}
    at = 0
    for name, value in tile.items():
        where[name] = (at, value.shape[0])
        packed.append(value)
        at += value.shape[0]
    tiles = np.concatenate(packed).astype(np.float32)
    packed, at = [], 0
    for name, value in row.items():
        where[name] = (at, value.shape[0])
        packed.append(value)
        at += value.shape[0]
    row16 = np.concatenate(packed).astype(np.float32)
    mats = {name: value.astype(np.float32) for name, value in mat.items()}
    return tiles, row16, mats, where


MATS = ("az7", "down", "az3", "up", "b12", "back", "sin")
N_LINKS = 8 + 4 + 4 + 4 + 4 + 8 + 4 + 4 + 4


def kernel(nx, ny, where, x_ref, tile_ref, row_ref, *rest):
    mat = dict(zip(MATS, rest[: len(MATS)]))
    (out_ref, fine_send, fine_recv, mid_send, mid_recv, line_send, line_recv, mode_send, mode_recv,
     send_sem, recv_sem, line_ss, line_rs, mode_ss, mode_rs) = rest[len(MATS) :]
    sx, cx = lax.axis_index("stream"), lax.axis_index("cross")

    def at(dx, dy):
        return {"stream": lax.rem(sx + (nx + dx), nx), "cross": lax.rem(cx + (ny + dy), ny)}

    def tab(name):
        start, size = where[name]
        return tile_ref[start : start + size]

    def rtab(name):
        start, size = where[name]
        return row_ref[start : start + size]

    bar = pltpu.get_barrier_semaphore()
    corners = ((1, 1), (1, -1), (-1, 1), (-1, -1))
    faces = ((1, 0), (-1, 0), (0, 1), (0, -1))
    for d in corners:
        pl.semaphore_signal(bar, inc=1, device_id=at(*d), device_id_type=MESH_ID)

    def greet_stream(d, carry):
        pl.semaphore_signal(bar, inc=1, device_id={"stream": lax.rem(sx + d, nx)},
                            device_id_type=MESH_ID)
        return carry

    def greet_cross(d, carry):
        pl.semaphore_signal(bar, inc=1, device_id={"cross": lax.rem(cx + d, ny)},
                            device_id_type=MESH_ID)
        return carry

    lax.fori_loop(1, nx, greet_stream, 0)
    lax.fori_loop(1, ny, greet_cross, 0)

    links = [0]
    sent = []

    def start(src, dst, to):
        n = links[0]
        links[0] += 1
        copy = pltpu.make_async_remote_copy(
            src, dst, send_sem.at[n], recv_sem.at[n], device_id=at(*to), device_id_type=MESH_ID)
        copy.start()
        sent.append(copy)
        return copy

    jrow = lax.broadcasted_iota(jnp.int32, (8, LANES), 0)
    lane = lax.broadcasted_iota(jnp.int32, (8, LANES), 1)
    low_wall = jnp.where(cx == 0, 0, -1)
    high_wall = jnp.where(cx == ny - 1, ORDER, -1)
    keep7 = jnp.where((jrow == low_wall) | (jrow == high_wall), 0.0, 1.0)
    mrow = lax.broadcasted_iota(jnp.int32, (16, LANES), 0)
    brow = lax.rem(mrow, 4)
    high_wall3 = jnp.where(cx == ny - 1, MID_ORDER, -1)
    keep3 = jnp.where((brow == low_wall) | (brow == high_wall3), 0.0, 1.0)
    e7 = tab("e7") * keep7[None]
    e3 = rtab("e3")[0] * keep3
    _, keep_f, gain_f = smoother(ORDER)
    _, keep_m, gain_m = smoother(MID_ORDER)

    def dot(a, b):
        return jnp.dot(a, b, preferred_element_type=jnp.float32, precision=EXACT)

    def fine_xy(u):
        kx = tab("kx").reshape(8, 8, 8, LANES)
        ax = kx[0][None] * u[:, 0:1]
        for a in range(1, 8):
            ax = ax + kx[a][None] * u[:, a : a + 1]
        ky = tab("ky")
        flat = u.reshape(16, 8, LANES)
        ay = ky[0][None] * flat
        for s in range(1, 8):
            ay = ay + ky[s][None] * pltpu.roll(flat, s, 1)
        return ax, ay.reshape(2, 8, 8, LANES) * tab("ti")[None]

    def fine_z(u):
        az = dot(u.reshape(128, LANES), mat["az7"][...])
        return az.reshape(2, 8, 8, LANES) * tab("tij")[None]

    def fine_send_faces(n, ax, ay):
        fine_send[n, 0] = ax[:, 7].reshape(16, LANES)
        fine_send[n, 1] = ax[:, 0].reshape(16, LANES)
        flat = ay.reshape(16, 8, LANES)
        fine_send[n, 2] = flat[:, 7, :]
        fine_send[n, 3] = flat[:, 0, :]
        return [start(fine_send.at[n, d], fine_recv.at[n, d], faces[d]) for d in range(4)]

    def add_x(field, low, high):
        return jnp.concatenate(
            [field[:, 0:1] + low.reshape(2, 1, 8, LANES), field[:, 1:7],
             field[:, 7:8] + high.reshape(2, 1, 8, LANES)], axis=1)

    def add_y(field, low, high):
        flat = field.reshape(16, 8, LANES)
        flat = flat + jnp.where(jrow[None] == 0, low[:, None, :], 0.0)
        flat = flat + jnp.where(jrow[None] == 7, high[:, None, :], 0.0)
        return flat.reshape(2, 8, 8, LANES)

    def fine_join(n, copies, field):
        for copy in copies:
            copy.wait_recv()
        field = add_x(field, fine_recv[n, 0], fine_recv[n, 1])
        return add_y(field, fine_recv[n, 2], fine_recv[n, 3])

    def left(name, v):
        start_row, size = where[name]
        acc = row_ref[start_row] * v[0:1]
        for c in range(1, size):
            acc = acc + row_ref[start_row + c] * v[c : c + 1]
        return acc

    def mid_start(n, ax, ay):
        mid_send[n, 0] = ax
        mid_send[n, 1] = ay
        return [start(mid_send.at[n, d // 2], mid_recv.at[n, d], faces[d]) for d in range(4)]

    def shifted(v, shift, mask):
        return jnp.where(mask, pltpu.roll(v, shift, 0), 0.0)

    def mid_join(n, copies, field):
        for copy in copies:
            copy.wait_recv()
        field = field + shifted(mid_recv[n, 0], 4, mrow < 4)
        field = field + shifted(mid_recv[n, 1], 12, mrow >= 12)
        field = field + shifted(mid_recv[n, 2], 13, brow == 0)
        return field + shifted(mid_recv[n, 3], 3, brow == 3)

    src = x_ref[...].reshape(16, 8, LANES)
    knode = lax.rem(lane, 8)
    src = (src + jnp.where(knode[None] == 7, pltpu.roll(src, LANES - 1, 2), 0.0)
           + jnp.where(knode[None] == 0, pltpu.roll(src, 1, 2), 0.0))
    fine_send[0, 2] = src[:, 7, :]
    fine_send[0, 3] = src[:, 0, :]
    src = src.reshape(2, 8, 8, LANES)
    fine_send[0, 0] = src[:, 7].reshape(16, LANES)
    fine_send[0, 1] = src[:, 0].reshape(16, LANES)
    pl.semaphore_wait(bar, 4 + nx - 1 + ny - 1)
    copies = [start(fine_send.at[0, 2 if d[1] > 0 else 3], fine_recv.at[5, n], d)
              for n, d in enumerate(corners)]
    copies += [start(fine_send.at[0, d], fine_recv.at[0, d], faces[d]) for d in range(4)]
    for copy in copies:
        copy.wait_recv()
    irow = jrow[None]

    def end(n, shift, row):
        line = fine_recv[5, n].reshape(2, 8, LANES)
        return jnp.where(irow == row, pltpu.roll(line, shift, 1), 0.0).reshape(16, LANES)

    low = fine_recv[0, 2] + end(0, 1, 0) + end(2, 7, 7)
    high = fine_recv[0, 3] + end(1, 1, 0) + end(3, 7, 7)
    b7 = add_y(add_x(src, fine_recv[0, 0], fine_recv[0, 1]), low, high)

    u1 = e7[None] * b7
    ax, ay = fine_xy(u1)
    copies = fine_send_faces(1, ax, ay)
    az = fine_z(u1)
    r1 = b7 - fine_join(1, copies, ax + ay + az)
    x7 = (1.0 + keep_f) * u1 + gain_f * (e7[None] * r1)
    ax, ay = fine_xy(x7)
    side7 = fine_send_faces(2, ax, ay)
    az = fine_z(x7)
    local7 = ax + ay + az
    ci = tab("ci")[None]
    rest7 = (src - tab("cj")[None] * (ax + ci * az) - ci * ay) * keep7[None, None]
    jx = tab("jx").reshape(8, 4, 8, LANES)
    g = jx[0][None] * rest7[:, 0:1]
    for i in range(1, 8):
        g = g + jx[i][None] * rest7[:, i : i + 1]
    g = jnp.concatenate([g[0].reshape(32, LANES), g[1].reshape(32, LANES)], axis=1)
    g3 = left("jy", dot(g, mat["down"][...]))
    mid_send[3, 0] = g3
    around = faces + corners
    copies = [start(mid_send.at[3, 0], mid_recv.at[3 + n // 4, n % 4], d)
              for n, d in enumerate(around)]
    rest7 = b7 - fine_join(2, side7, local7)
    for copy in copies:
        copy.wait_recv()
    shifts = ((4, mrow < 4), (12, mrow >= 12), (13, brow == 0), (3, brow == 3),
              (1, mrow == 0), (7, mrow == 3), (9, mrow == 12), (15, mrow == 15))
    b3 = g3
    for n, (shift, mask) in enumerate(shifts):
        b3 = b3 + shifted(mid_recv[3 + n // 4, n % 4], shift, mask)

    tab3 = rtab("tab")[0]

    def mid_z(v):
        return tab3 * dot(v, mat["az3"][...])

    v1 = e3 * b3
    ax, ay = left("lx", v1), left("ly", v1)
    copies = mid_start(0, ax, ay)
    az = mid_z(v1)
    r1 = b3 - mid_join(0, copies, ax + ay + az)
    x3 = (1.0 + keep_m) * v1 + gain_m * (e3 * r1)
    ax, ay = left("lx", x3), left("ly", x3)
    ca, cb = rtab("ca")[0], rtab("cb")[0]
    part = keep3 * (g3 - cb * ax - ca * ay)
    other = keep3 * (ca * cb * tab3) * x3
    line = dot(jnp.concatenate([part, -other], axis=1), mat["b12"][...])
    line = jnp.sum(rtab("jj")[0] * line, axis=0, keepdims=True)
    line_send[0] = line

    def line_copy(d, slot, to):
        return pltpu.make_async_remote_copy(
            line_send.at[0], line_recv.at[slot], line_ss.at[d], line_rs.at[d],
            device_id={"cross": to}, device_id_type=MESH_ID)

    def line_out(d, carry):
        line_copy(d, cx, lax.rem(cx + d, ny)).start()
        return carry

    lax.fori_loop(1, ny, line_out, 0)
    line_recv[cx] = line
    side3 = mid_start(1, ax, ay)
    if ny < 32:
        line_recv[ny:] = jnp.zeros((32 - ny, 1, LANES), jnp.float32)
    rest3 = b3 - mid_join(1, side3, ax + ay + mid_z(x3))

    def line_in(d, carry):
        line_copy(d, lax.rem(cx + ny - d, ny), cx).wait()
        return carry

    lax.fori_loop(1, ny, line_in, 0)
    spectrum = dot(mat["sin"][...], line_recv[:, 0, :])
    group = lax.div(lane, 32)
    for alpha in range(2):
        total = jnp.zeros((8, LANES), jnp.float32)
        for hi in range(4):
            for beta in range(2):
                piece = spectrum[(beta * 4 + hi) * 8 : (beta * 4 + hi + 1) * 8]
                shift = 32 * (hi - 2 * alpha - beta) % LANES
                if shift:
                    piece = pltpu.roll(piece, shift, 1)
                total = total + jnp.where(group == hi, piece, 0.0)
        mode_send[alpha] = total

    def mode_copy(d, to):
        return pltpu.make_async_remote_copy(
            mode_send, mode_recv.at[d], mode_ss.at[d], mode_rs.at[d],
            device_id={"stream": to}, device_id_type=MESH_ID)

    def mode_out(d, carry):
        mode_copy(d, lax.rem(sx + d, nx)).start()
        return carry

    def mode_in(d, carry):
        mode_copy(d, sx).wait()
        return carry

    lax.fori_loop(1, nx, mode_out, 0)
    mode_recv[0] = mode_send[...]
    lax.fori_loop(1, nx, mode_in, 0)
    first = mode_recv[:, 0]
    second = mode_recv[:, 1]
    nodes = first + jnp.concatenate([second[1:], second[:1]], axis=0)
    start_g = where["green"][0]
    solved = [jnp.sum(tile_ref[start_g + n : start_g + n + nx] * nodes, axis=0) for n in range(4)]
    sine = tile_ref[pl.ds(where["sine"][0] + cx + 1, 4)]
    window = [jnp.sum(sine * s[None], axis=1) for s in solved]
    window = jnp.concatenate(window, axis=0)
    window = dot(window, mat["back"][...])
    zval, zstiff = window[:, :LANES], window[:, LANES:]

    x3 = x3 + left("pj", zval)
    r0 = rest3 - left("kt", zval) - left("tt", zstiff)
    w1 = e3 * r0
    ax, ay = left("lx", w1), left("ly", w1)
    copies = mid_start(2, ax, ay)
    r1 = r0 - mid_join(2, copies, ax + ay + mid_z(w1))
    x3 = x3 + (1.0 + keep_m) * w1 + gain_m * (e3 * r1)

    jb, ji = tab("jb"), tab("ji").reshape(4, 8, 8, LANES)
    halves = dot(x3, mat["up"][...])
    parts = []
    for r in range(2):
        half = halves[:, r * LANES : (r + 1) * LANES]
        cols = []
        for a in range(4):
            acc = jb[0] * half[4 * a : 4 * a + 1]
            for b in range(1, 4):
                acc = acc + jb[b] * half[4 * a + b : 4 * a + b + 1]
            cols.append(acc)
        acc = ji[0] * cols[0][None]
        for a in range(1, 4):
            acc = acc + ji[a] * cols[a][None]
        parts.append(acc)
    px = jnp.stack(parts, axis=0)
    ax, ay = fine_xy(px)
    copies = fine_send_faces(3, ax, ay)
    r0 = rest7 - fine_join(3, copies, ax + ay + fine_z(px))
    u1 = e7[None] * r0
    ax, ay = fine_xy(u1)
    copies = fine_send_faces(4, ax, ay)
    r1 = r0 - fine_join(4, copies, ax + ay + fine_z(u1))
    out = x7 + px + (1.0 + keep_f) * u1 + gain_f * (e7[None] * r1)
    out_ref[...] = out.reshape(128, LANES)
    for copy in sent:
        copy.wait_send()


def solution(mesh):
    nx, ny = mesh.shape["stream"], mesh.shape["cross"]
    tiles, row16, mats, where = build_tables(nx, ny)
    vmem = pl.BlockSpec(memory_space=pltpu.VMEM)

    def body(sources):
        flat = sources.reshape(128, LANES)
        operands = [flat, jnp.asarray(tiles), jnp.asarray(row16)]
        operands += [jnp.asarray(mats[name]) for name in MATS]
        out = pl.pallas_call(
            functools.partial(kernel, nx, ny, where),
            out_shape=jax.ShapeDtypeStruct((128, LANES), jnp.float32),
            in_specs=[vmem] * len(operands),
            out_specs=vmem,
            scratch_shapes=[
                pltpu.VMEM((5, 4, 16, LANES), jnp.float32),
                pltpu.VMEM((6, 4, 16, LANES), jnp.float32),
                pltpu.VMEM((4, 2, 16, LANES), jnp.float32),
                pltpu.VMEM((5, 4, 16, LANES), jnp.float32),
                pltpu.VMEM((1, 1, LANES), jnp.float32),
                pltpu.VMEM((32, 1, LANES), jnp.float32),
                pltpu.VMEM((2, 8, LANES), jnp.float32),
                pltpu.VMEM((nx, 2, 8, LANES), jnp.float32),
                pltpu.SemaphoreType.DMA((N_LINKS,)),
                pltpu.SemaphoreType.DMA((N_LINKS,)),
                pltpu.SemaphoreType.DMA((ny,)),
                pltpu.SemaphoreType.DMA((ny,)),
                pltpu.SemaphoreType.DMA((nx,)),
                pltpu.SemaphoreType.DMA((nx,)),
            ],
            compiler_params=pltpu.CompilerParams(
                collective_id=0, has_side_effects=True, vmem_limit_bytes=32 * 1024 * 1024),
            name="vcycle",
        )(*operands)
        return out.reshape(sources.shape)

    spec = P(None, "stream", "cross", None, None, None)
    return jax.shard_map(body, mesh=mesh, in_specs=(spec,), out_specs=spec, check_vma=False)
```

```python
import functools
import math

import jax
import jax.numpy as jnp
import numpy as np
from jax import lax
from jax.experimental import pallas as pl
from jax.experimental.pallas import tpu as pltpu
from jax.sharding import PartitionSpec as P

ORDER = 7
MID_ORDER = 3
EZ = 16
LANES = 128
MODES = 32
EXACT = lax.Precision.HIGHEST
MESH_ID = pl.DeviceIdType.MESH


def legendre_pair(degree, points):
    below_poly = np.ones(points.shape)
    top_poly = points.copy()
    for step in range(2, degree + 1):
        below_poly, top_poly = (
            top_poly,
            ((2 * step - 1) * points * top_poly - (step - 1) * below_poly) / step,
        )
    return (below_poly, top_poly)


@functools.lru_cache(None)
def gll_tables(degree):
    nodes = -np.cos(np.pi * np.arange(degree + 1) / degree)
    for _ in range(100):
        below_poly, top_poly = legendre_pair(degree, nodes)
        nodes = nodes - (nodes * top_poly - below_poly) / ((degree + 1) * top_poly)
    at_nodes = legendre_pair(degree, nodes)[1]
    weights = 2.0 / (degree * (degree + 1) * at_nodes**2)
    count = degree + 1
    derivative = np.zeros((count, count))
    for target in range(count):
        for source in range(count):
            if target != source:
                derivative[target, source] = at_nodes[target] / (
                    at_nodes[source] * (nodes[target] - nodes[source])
                )
    derivative[0, 0] = -degree * (degree + 1) / 4.0
    derivative[degree, degree] = degree * (degree + 1) / 4.0
    stiffness = derivative.T @ (weights[:, None] * derivative)
    return (nodes, weights, stiffness)


def lagrange_matrix(fine_degree, coarse_degree):
    fine_nodes = gll_tables(fine_degree)[0]
    coarse_nodes = gll_tables(coarse_degree)[0]
    table = np.ones((fine_degree + 1, coarse_degree + 1))
    for column in range(coarse_degree + 1):
        for other in range(coarse_degree + 1):
            if other != column:
                table[:, column] *= (fine_nodes - coarse_nodes[other]) / (
                    coarse_nodes[column] - coarse_nodes[other]
                )
    return table


@functools.lru_cache(None)
def smoother(degree):
    stiffness = gll_tables(degree)[2]
    elements = 6
    size = elements * degree
    assembled = np.zeros((size, size))
    for element in range(elements):
        for row in range(degree + 1):
            for col in range(degree + 1):
                assembled[(element * degree + row) % size, (element * degree + col) % size] += (
                    stiffness[row, col]
                )
    diagonal = np.sqrt(np.diagonal(assembled))
    scaled = assembled / diagonal[:, None] / diagonal[None, :]
    positions = np.arange(size)
    vector = np.where(positions % 2 == 0, 1.0, -1.0) * (1.0 + positions / size)
    for _ in range(2000):
        vector = scaled @ vector
        vector = vector / np.sqrt(np.sum(vector * vector))
    high = float(np.sum(vector * (scaled @ vector)) / np.sum(vector * vector))
    low = 0.1 * high
    theta, delta = 0.5 * (high + low), 0.5 * (high - low)
    sigma = theta / delta
    rho1 = 1.0 / sigma
    rho2 = 1.0 / (2.0 * sigma - rho1)
    return theta, rho2 * rho1, 2.0 * rho2 / delta * theta


def level(degree):
    _, w, k = gll_tables(degree)
    t = w.copy()
    t[0] = t[-1] = w[0] + w[-1]
    s = np.diagonal(k).copy()
    s[0] = s[-1] = k[0, 0] + k[-1, -1]
    c = np.ones(degree + 1)
    c[0] = c[-1] = 0.5
    diag = (
        s[:, None, None] * t[None, :, None] * t[None, None, :]
        + t[:, None, None] * s[None, :, None] * t[None, None, :]
        + t[:, None, None] * t[None, :, None] * s[None, None, :]
    )
    return w, k, t, c, 1.0 / (diag * smoother(degree)[0])


def join_z(count):
    size = EZ * count
    m = np.eye(size)
    for e in range(EZ):
        a, b = e * count + count - 1, ((e + 1) % EZ) * count
        m[a, b] += 1.0
        m[b, a] += 1.0
    return m


def two(m):
    return np.kron(np.eye(2), m)


def lanes(values):
    return np.broadcast_to(values[None, :], (8, LANES))


def rows(values):
    return np.broadcast_to(np.asarray(values)[..., None], np.shape(values) + (LANES,))


def fourier_rows(total):
    k, n = np.meshgrid(np.arange(total), np.arange(total), indexing="ij")
    half = total // 2
    freq = np.where(k <= half, k, k - half)
    angle = 2.0 * np.pi * (freq * n % total) / total
    scale = np.where((k == 0) | (k == half), math.sqrt(1.0 / total), math.sqrt(2.0 / total))
    return scale * np.where(k <= half, np.cos(angle), np.sin(angle))


def sine_rows(mode, point, total):
    product = mode * point % (2 * total)
    inside = (mode > 0) & (mode < total) & (point > 0) & (point < total)
    return np.where(inside, math.sqrt(2.0 / total) * np.sin(np.pi * product / total), 0.0)


def green_table(nx, ny):
    mode = np.arange(MODES)
    wall_gap = 2.0 * np.sin(0.5 * np.pi * mode / ny) ** 2 + np.where(mode % ny == 0, 1.0, 0.0)
    freq = np.arange(EZ)
    freq = np.where(freq <= EZ // 2, freq, freq - EZ // 2)
    span_gap = 2.0 * np.sin(np.pi * freq / EZ) ** 2
    half_gap = wall_gap[:, None] + span_gap[None, :]
    root = np.sqrt(half_gap * (2.0 + half_gap))
    rate = np.log1p(half_gap + root)
    d = np.arange(nx)[:, None, None]
    top = np.exp(-rate * d) + np.exp(-rate * (nx - d))
    return top / (4.0 * root * -np.expm1(-rate * nx))


def modal(values):
    v = values.reshape(values.shape[:-2] + (MODES // 8, 8, EZ))
    v = np.stack([v, v], axis=-2)
    v = np.moveaxis(v, -4, -3)
    return v.reshape(v.shape[:-3] + (LANES,))


def assembled_1d(local_cols, window):
    count = local_cols.shape[0]
    out = np.zeros((count, window))
    out[:, 1:3] += local_cols
    out[0, 0:2] += local_cols[-1]
    out[-1, 2:4] += local_cols[0]
    return out


@functools.lru_cache(None)
def build_tables(nx, ny):
    f, q = ORDER + 1, MID_ORDER + 1
    w7, k7, t7, c7, e7 = level(ORDER)
    w3, k3, t3, c3, e3 = level(MID_ORDER)
    j73 = lagrange_matrix(ORDER, MID_ORDER)
    j31 = lagrange_matrix(MID_ORDER, 1)
    tile = {}
    tk = np.tile(t7, EZ)
    ones = np.ones((8, LANES))
    tile["kx"] = np.stack(
        [np.stack([k7[i, a] * t7[:, None] * tk[None, :] for i in range(f)]) for a in range(f)]
    ).reshape(f * f, 8, LANES)
    roll = np.stack([[k7[j, (j - s) % f] for j in range(f)] for s in range(f)])
    tile["ky"] = roll[:, :, None] * tk[None, None, :]
    tile["e7"] = np.tile(e7, (1, 1, EZ))
    tile["ti"] = np.stack([t * ones for t in t7])
    tile["tij"] = np.stack([t * rows(t7) for t in t7])
    tile["cj"] = rows(c7)[None]
    tile["ci"] = np.stack([c * ones for c in c7])
    tile["jx"] = np.stack([j73[i, a] * ones for i in range(f) for a in range(q)])
    tile["jb"] = np.stack([rows(j73[:, b]) for b in range(q)])
    tile["ji"] = np.stack([j73[i, a] * ones for a in range(q) for i in range(f)])
    green = modal(green_table(nx, ny))
    tile["green"] = green[(np.arange(nx + 3) - 1) % nx]
    point = np.arange(-2, ny + 4)
    tile["sine"] = modal(
        np.broadcast_to(
            sine_rows(np.arange(MODES)[None, :], point[:, None], ny)[:, :, None],
            (len(point), MODES, EZ),
        )
    )
    row = {}
    mid = [(a, b) for a in range(q) for b in range(q)]
    tc = np.tile(np.tile(t3, EZ), 2)

    def left(matrix, scale=None):
        scale = np.ones(LANES) if scale is None else scale
        return matrix.T[:, :, None] * scale[None, None, :]

    row["jy"] = left(
        np.array([[(a == a2) * j73[j, b] for a2 in range(q) for j in range(f)] for a, b in mid])
    )
    row["lx"] = left(np.kron(k3, np.diag(t3)), tc)
    row["ly"] = left(np.kron(np.diag(t3), k3), tc)
    row["e3"] = np.stack([np.tile(np.tile(e3[a, b], EZ), 2) for a, b in mid])[None]
    row["tab"] = rows([t3[a] * t3[b] for a, b in mid])[None]
    row["ca"] = rows([c3[a] for a, b in mid])[None]
    row["cb"] = rows([c3[b] for a, b in mid])[None]
    groups = [np.array([j31[a, x] * j31[b, y] for a, b in mid]) for x in (0, 1) for y in (0, 1)]
    row["jj"] = np.repeat(np.stack(groups, axis=1), MODES, axis=1)[None]
    own = np.zeros((q, 4))
    own[:, 1:3] = j31
    stiff = assembled_1d(k3 @ j31, 4)
    mass = t3[:, None] * own
    row["pj"] = left(np.kron(own, own))
    row["kt"] = left(np.kron(stiff, mass) + np.kron(mass, stiff), tc)
    row["tt"] = left(np.kron(mass, mass))

    mat = {}
    az7 = (join_z(f) @ np.kron(np.eye(EZ), k7)).T
    az3 = two((join_z(q) @ np.kron(np.eye(EZ), k3)).T)
    down = (join_z(q) @ np.kron(np.eye(EZ), j73.T) @ np.diag(np.tile(c7, EZ))).T
    zero = np.zeros_like(down)
    mat["az7"] = az7
    mat["down"] = np.concatenate(
        [np.concatenate([down, zero], axis=1), np.concatenate([zero, down], axis=1)], axis=0
    )
    mat["az3"] = az3
    up = np.kron(np.eye(EZ), j73).T
    mat["up"] = two(up)
    gather = np.zeros((EZ, EZ * q))
    for e in range(EZ):
        for node in (0, 1):
            gather[(e + node) % EZ, e * q : (e + 1) * q] += j31[:, node] * c3
    b1 = two((fourier_rows(EZ) @ gather).T)
    b1 = np.tile(b1, (1, 4))
    mat["b12"] = np.concatenate([b1, az3 @ b1], axis=0)
    spread = np.zeros((EZ * q, EZ))
    for e in range(EZ):
        for node in (0, 1):
            spread[e * q : (e + 1) * q, (e + node) % EZ] += j31[:, node]
    back = two((spread @ fourier_rows(EZ).T).T)
    back = np.tile(back, (4, 1))
    mat["back"] = np.concatenate([back, back @ az3], axis=1)
    mode, here = np.arange(MODES)[:, None], np.arange(32)[None, :]
    s0 = np.where(here < ny, sine_rows(mode, here, ny), 0.0)
    s1 = np.where(here < ny, sine_rows(mode, here + 1, ny), 0.0)
    mat["sin"] = np.concatenate([s0, s1], axis=0)
    packed, where = [], {}
    at = 0
    for name, value in tile.items():
        where[name] = (at, value.shape[0])
        packed.append(value)
        at += value.shape[0]
    tiles = np.concatenate(packed).astype(np.float32)
    packed, at = [], 0
    for name, value in row.items():
        where[name] = (at, value.shape[0])
        packed.append(value)
        at += value.shape[0]
    row16 = np.concatenate(packed).astype(np.float32)
    mats = {name: value.astype(np.float32) for name, value in mat.items()}
    return tiles, row16, mats, where


MATS = ("az7", "down", "az3", "up", "b12", "back", "sin")
N_LINKS = 8 + 4 + 4 + 4 + 4 + 8 + 4 + 4 + 4


def reach(n):
    base = max(n // 8, 1)
    known, hops = base, []
    while known < n // 2:
        hops.append(known)
        known *= 2
    return range(1, base + 1), hops


def kernel(nx, ny, where, *refs):
    names = ("x", "tiles", "rows") + MATS
    count = len(names)
    hbm, out_ref, vmem = refs[:count], refs[count], refs[count + 1 : 2 * count + 1]
    (fine_send, fine_recv, mid_send, mid_recv, line_send, line_recv, mode_send, mode_recv,
     load_sem, send_sem, recv_sem, line_ss, line_rs, mode_ss, mode_rs, known) = refs[2 * count + 1 :]
    sx, cx = lax.axis_index("stream"), lax.axis_index("cross")
    tile_ref, row_ref = vmem[1], vmem[2]
    mat = dict(zip(MATS, vmem[3:]))

    def at(dx, dy):
        return {"stream": lax.rem(sx + (nx + dx), nx), "cross": lax.rem(cx + (ny + dy), ny)}

    def tab(name):
        start, size = where[name]
        return tile_ref[start : start + size]

    def rtab(name):
        start, size = where[name]
        return row_ref[start : start + size]

    bar = pltpu.get_barrier_semaphore()
    corners = ((1, 1), (1, -1), (-1, 1), (-1, -1))
    faces = ((1, 0), (-1, 0), (0, 1), (0, -1))
    near_x, hops_x = reach(nx)
    near_y, hops_y = reach(ny)
    near = [(s * d, 0) for d in near_x for s in (1, -1)]
    near += [(0, s * d) for d in near_y for s in (1, -1)]
    near += corners
    for d in near:
        pl.semaphore_signal(bar, inc=1, device_id=at(*d), device_id_type=MESH_ID)
    loads = {}
    for n, name in enumerate(names):
        loads[name] = pltpu.make_async_copy(hbm[n], vmem[n], load_sem.at[n])
        loads[name].start()

    def need(*wanted):
        for name in wanted:
            if name in loads:
                loads.pop(name).wait()

    def tell(step):
        for n, hops in enumerate((hops_x, hops_y)):
            if step < len(hops):
                for s in (1, -1):
                    d = (s * hops[step], 0) if n == 0 else (0, s * hops[step])
                    pl.semaphore_signal(
                        known.at[step, n], inc=1, device_id=at(*d), device_id_type=MESH_ID)

    def told(step):
        for n, hops in enumerate((hops_x, hops_y)):
            if step < len(hops):
                pl.semaphore_wait(known.at[step, n], 2)

    links = [0]
    sent = []

    def start(src, dst, to):
        n = links[0]
        links[0] += 1
        copy = pltpu.make_async_remote_copy(
            src, dst, send_sem.at[n], recv_sem.at[n], device_id=at(*to), device_id_type=MESH_ID)
        copy.start()
        sent.append(copy)
        return copy

    jrow = lax.broadcasted_iota(jnp.int32, (8, LANES), 0)
    lane = lax.broadcasted_iota(jnp.int32, (8, LANES), 1)
    low_wall = jnp.where(cx == 0, 0, -1)
    high_wall = jnp.where(cx == ny - 1, ORDER, -1)
    keep7 = jnp.where((jrow == low_wall) | (jrow == high_wall), 0.0, 1.0)
    mrow = lax.broadcasted_iota(jnp.int32, (16, LANES), 0)
    brow = lax.rem(mrow, 4)
    high_wall3 = jnp.where(cx == ny - 1, MID_ORDER, -1)
    keep3 = jnp.where((brow == low_wall) | (brow == high_wall3), 0.0, 1.0)
    _, keep_f, gain_f = smoother(ORDER)
    _, keep_m, gain_m = smoother(MID_ORDER)

    def dot(a, b):
        return jnp.dot(a, b, preferred_element_type=jnp.float32, precision=EXACT)

    def fine_xy(u):
        kx = tab("kx").reshape(8, 8, 8, LANES)
        ax = kx[0][None] * u[:, 0:1]
        for a in range(1, 8):
            ax = ax + kx[a][None] * u[:, a : a + 1]
        ky = tab("ky")
        flat = u.reshape(16, 8, LANES)
        ay = ky[0][None] * flat
        for s in range(1, 8):
            ay = ay + ky[s][None] * pltpu.roll(flat, s, 1)
        return ax, ay.reshape(2, 8, 8, LANES) * tab("ti")[None]

    def fine_z(u):
        az = dot(u.reshape(128, LANES), mat["az7"][...])
        return az.reshape(2, 8, 8, LANES) * tab("tij")[None]

    def fine_send_faces(n, ax, ay):
        fine_send[n, 0] = ax[:, 7].reshape(16, LANES)
        fine_send[n, 1] = ax[:, 0].reshape(16, LANES)
        flat = ay.reshape(16, 8, LANES)
        fine_send[n, 2] = flat[:, 7, :]
        fine_send[n, 3] = flat[:, 0, :]
        return [start(fine_send.at[n, d], fine_recv.at[n, d], faces[d]) for d in range(4)]

    def add_x(field, low, high):
        return jnp.concatenate(
            [field[:, 0:1] + low.reshape(2, 1, 8, LANES), field[:, 1:7],
             field[:, 7:8] + high.reshape(2, 1, 8, LANES)], axis=1)

    def add_y(field, low, high):
        flat = field.reshape(16, 8, LANES)
        flat = flat + jnp.where(jrow[None] == 0, low[:, None, :], 0.0)
        flat = flat + jnp.where(jrow[None] == 7, high[:, None, :], 0.0)
        return flat.reshape(2, 8, 8, LANES)

    def fine_join(n, copies, field):
        for copy in copies:
            copy.wait_recv()
        field = add_x(field, fine_recv[n, 0], fine_recv[n, 1])
        return add_y(field, fine_recv[n, 2], fine_recv[n, 3])

    def left(name, v):
        start_row, size = where[name]
        acc = row_ref[start_row] * v[0:1]
        for c in range(1, size):
            acc = acc + row_ref[start_row + c] * v[c : c + 1]
        return acc

    def mid_start(n, ax, ay):
        mid_send[n, 0] = ax
        mid_send[n, 1] = ay
        return [start(mid_send.at[n, d // 2], mid_recv.at[n, d], faces[d]) for d in range(4)]

    def shifted(v, shift, mask):
        return jnp.where(mask, pltpu.roll(v, shift, 0), 0.0)

    def mid_join(n, copies, field):
        for copy in copies:
            copy.wait_recv()
        field = field + shifted(mid_recv[n, 0], 4, mrow < 4)
        field = field + shifted(mid_recv[n, 1], 12, mrow >= 12)
        field = field + shifted(mid_recv[n, 2], 13, brow == 0)
        return field + shifted(mid_recv[n, 3], 3, brow == 3)

    need("x")
    src = vmem[0][...].reshape(16, 8, LANES)
    knode = lax.rem(lane, 8)
    src = (src + jnp.where(knode[None] == 7, pltpu.roll(src, LANES - 1, 2), 0.0)
           + jnp.where(knode[None] == 0, pltpu.roll(src, 1, 2), 0.0))
    fine_send[0, 2] = src[:, 7, :]
    fine_send[0, 3] = src[:, 0, :]
    src = src.reshape(2, 8, 8, LANES)
    fine_send[0, 0] = src[:, 7].reshape(16, LANES)
    fine_send[0, 1] = src[:, 0].reshape(16, LANES)
    pl.semaphore_wait(bar, len(near))
    tell(0)
    copies = [start(fine_send.at[0, 2 if d[1] > 0 else 3], fine_recv.at[5, n], d)
              for n, d in enumerate(corners)]
    copies += [start(fine_send.at[0, d], fine_recv.at[0, d], faces[d]) for d in range(4)]
    need("tiles", "az7")
    e7 = tab("e7") * keep7[None]
    for copy in copies:
        copy.wait_recv()
    told(0)
    tell(1)
    irow = jrow[None]

    def end(n, shift, row):
        line = fine_recv[5, n].reshape(2, 8, LANES)
        return jnp.where(irow == row, pltpu.roll(line, shift, 1), 0.0).reshape(16, LANES)

    low = fine_recv[0, 2] + end(0, 1, 0) + end(2, 7, 7)
    high = fine_recv[0, 3] + end(1, 1, 0) + end(3, 7, 7)
    b7 = add_y(add_x(src, fine_recv[0, 0], fine_recv[0, 1]), low, high)

    u1 = e7[None] * b7
    ax, ay = fine_xy(u1)
    copies = fine_send_faces(1, ax, ay)
    az = fine_z(u1)
    r1 = b7 - fine_join(1, copies, ax + ay + az)
    x7 = (1.0 + keep_f) * u1 + gain_f * (e7[None] * r1)
    ax, ay = fine_xy(x7)
    side7 = fine_send_faces(2, ax, ay)
    az = fine_z(x7)
    local7 = ax + ay + az
    ci = tab("ci")[None]
    rest7 = (src - tab("cj")[None] * (ax + ci * az) - ci * ay) * keep7[None, None]
    need("rows", "down")
    jx = tab("jx").reshape(8, 4, 8, LANES)
    g = jx[0][None] * rest7[:, 0:1]
    for i in range(1, 8):
        g = g + jx[i][None] * rest7[:, i : i + 1]
    g = jnp.concatenate([g[0].reshape(32, LANES), g[1].reshape(32, LANES)], axis=1)
    g3 = left("jy", dot(g, mat["down"][...]))
    mid_send[3, 0] = g3
    around = faces + corners
    copies = [start(mid_send.at[3, 0], mid_recv.at[3 + n // 4, n % 4], d)
              for n, d in enumerate(around)]
    rest7 = b7 - fine_join(2, side7, local7)
    for copy in copies:
        copy.wait_recv()
    shifts = ((4, mrow < 4), (12, mrow >= 12), (13, brow == 0), (3, brow == 3),
              (1, mrow == 0), (7, mrow == 3), (9, mrow == 12), (15, mrow == 15))
    b3 = g3
    for n, (shift, mask) in enumerate(shifts):
        b3 = b3 + shifted(mid_recv[3 + n // 4, n % 4], shift, mask)

    need("az3", "b12", "sin", "back", "up")
    told(1)
    e3 = rtab("e3")[0] * keep3
    tab3 = rtab("tab")[0]

    def mid_z(v):
        return tab3 * dot(v, mat["az3"][...])

    v1 = e3 * b3
    ax, ay = left("lx", v1), left("ly", v1)
    copies = mid_start(0, ax, ay)
    az = mid_z(v1)
    r1 = b3 - mid_join(0, copies, ax + ay + az)
    x3 = (1.0 + keep_m) * v1 + gain_m * (e3 * r1)
    ax, ay = left("lx", x3), left("ly", x3)
    ca, cb = rtab("ca")[0], rtab("cb")[0]
    part = keep3 * (g3 - cb * ax - ca * ay)
    other = keep3 * (ca * cb * tab3) * x3
    line = dot(jnp.concatenate([part, -other], axis=1), mat["b12"][...])
    line = jnp.sum(rtab("jj")[0] * line, axis=0, keepdims=True)
    line_send[0] = line

    def line_copy(d, slot, to):
        return pltpu.make_async_remote_copy(
            line_send.at[0], line_recv.at[slot], line_ss.at[d], line_rs.at[d],
            device_id={"cross": to}, device_id_type=MESH_ID)

    def line_out(d, carry):
        line_copy(d, cx, lax.rem(cx + d, ny)).start()
        return carry

    lax.fori_loop(1, ny, line_out, 0)
    line_recv[cx] = line
    side3 = mid_start(1, ax, ay)
    if ny < 32:
        line_recv[ny:] = jnp.zeros((32 - ny, 1, LANES), jnp.float32)
    rest3 = b3 - mid_join(1, side3, ax + ay + mid_z(x3))

    def line_in(d, carry):
        line_copy(d, lax.rem(cx + ny - d, ny), cx).wait()
        return carry

    lax.fori_loop(1, ny, line_in, 0)
    spectrum = dot(mat["sin"][...], line_recv[:, 0, :])
    group = lax.div(lane, 32)
    for alpha in range(2):
        total = jnp.zeros((8, LANES), jnp.float32)
        for hi in range(4):
            for beta in range(2):
                piece = spectrum[(beta * 4 + hi) * 8 : (beta * 4 + hi + 1) * 8]
                shift = 32 * (hi - 2 * alpha - beta) % LANES
                if shift:
                    piece = pltpu.roll(piece, shift, 1)
                total = total + jnp.where(group == hi, piece, 0.0)
        mode_send[alpha] = total

    def mode_copy(d, to):
        return pltpu.make_async_remote_copy(
            mode_send, mode_recv.at[d], mode_ss.at[d], mode_rs.at[d],
            device_id={"stream": to}, device_id_type=MESH_ID)

    def mode_out(d, carry):
        mode_copy(d, lax.rem(sx + d, nx)).start()
        return carry

    def mode_in(d, carry):
        mode_copy(d, sx).wait()
        return carry

    lax.fori_loop(1, nx, mode_out, 0)
    mode_recv[0] = mode_send[...]
    lax.fori_loop(1, nx, mode_in, 0)
    first = mode_recv[:, 0]
    second = mode_recv[:, 1]
    nodes = first + jnp.concatenate([second[1:], second[:1]], axis=0)
    start_g = where["green"][0]
    solved = [jnp.sum(tile_ref[start_g + n : start_g + n + nx] * nodes, axis=0) for n in range(4)]
    sine = tile_ref[pl.ds(where["sine"][0] + cx + 1, 4)]
    window = [jnp.sum(sine * s[None], axis=1) for s in solved]
    window = jnp.concatenate(window, axis=0)
    window = dot(window, mat["back"][...])
    zval, zstiff = window[:, :LANES], window[:, LANES:]

    x3 = x3 + left("pj", zval)
    r0 = rest3 - left("kt", zval) - left("tt", zstiff)
    w1 = e3 * r0
    ax, ay = left("lx", w1), left("ly", w1)
    copies = mid_start(2, ax, ay)
    r1 = r0 - mid_join(2, copies, ax + ay + mid_z(w1))
    x3 = x3 + (1.0 + keep_m) * w1 + gain_m * (e3 * r1)

    jb, ji = tab("jb"), tab("ji").reshape(4, 8, 8, LANES)
    halves = dot(x3, mat["up"][...])
    parts = []
    for r in range(2):
        half = halves[:, r * LANES : (r + 1) * LANES]
        cols = []
        for a in range(4):
            acc = jb[0] * half[4 * a : 4 * a + 1]
            for b in range(1, 4):
                acc = acc + jb[b] * half[4 * a + b : 4 * a + b + 1]
            cols.append(acc)
        acc = ji[0] * cols[0][None]
        for a in range(1, 4):
            acc = acc + ji[a] * cols[a][None]
        parts.append(acc)
    px = jnp.stack(parts, axis=0)
    ax, ay = fine_xy(px)
    copies = fine_send_faces(3, ax, ay)
    r0 = rest7 - fine_join(3, copies, ax + ay + fine_z(px))
    u1 = e7[None] * r0
    ax, ay = fine_xy(u1)
    copies = fine_send_faces(4, ax, ay)
    r1 = r0 - fine_join(4, copies, ax + ay + fine_z(u1))
    out = x7 + px + (1.0 + keep_f) * u1 + gain_f * (e7[None] * r1)
    out_ref[...] = out.reshape(128, LANES)
    for copy in sent:
        copy.wait_send()


def solution(mesh):
    nx, ny = mesh.shape["stream"], mesh.shape["cross"]
    tiles, row16, mats, where = build_tables(nx, ny)

    def body(sources):
        flat = sources.reshape(128, LANES)
        operands = [flat, jnp.asarray(tiles), jnp.asarray(row16)]
        operands += [jnp.asarray(mats[name]) for name in MATS]
        links, f32 = pltpu.SemaphoreType.DMA, jnp.float32
        out = pl.pallas_call(
            functools.partial(kernel, nx, ny, where),
            out_shape=jax.ShapeDtypeStruct((128, LANES), jnp.float32),
            in_specs=[pl.BlockSpec(memory_space=pl.ANY)] * len(operands),
            out_specs=pl.BlockSpec(memory_space=pltpu.VMEM),
            scratch_shapes=[pltpu.VMEM(o.shape, f32) for o in operands]
            + [
                pltpu.VMEM((5, 4, 16, LANES), f32),
                pltpu.VMEM((6, 4, 16, LANES), f32),
                pltpu.VMEM((4, 2, 16, LANES), f32),
                pltpu.VMEM((5, 4, 16, LANES), f32),
                pltpu.VMEM((1, 1, LANES), f32),
                pltpu.VMEM((32, 1, LANES), f32),
                pltpu.VMEM((2, 8, LANES), f32),
                pltpu.VMEM((nx, 2, 8, LANES), f32),
                links((len(operands),)),
                links((N_LINKS,)),
                links((N_LINKS,)),
                links((ny,)),
                links((ny,)),
                links((nx,)),
                links((nx,)),
                pltpu.SemaphoreType.REGULAR((2, 2)),
            ],
            compiler_params=pltpu.CompilerParams(collective_id=0, has_side_effects=True),
            name="vcycle",
        )(*operands)
        return out.reshape(sources.shape)

    spec = P(None, "stream", "cross", None, None, None)
    return jax.shard_map(body, mesh=mesh, in_specs=(spec,), out_specs=spec, check_vma=False)
```

```python
import functools
import math

import jax
import jax.numpy as jnp
import numpy as np
from jax import lax
from jax.experimental import pallas as pl
from jax.experimental.pallas import tpu as pltpu
from jax.sharding import PartitionSpec as P

ORDER = 7
MID_ORDER = 3
EZ = 16
LANES = 128
MODES = 32
EXACT = lax.Precision.HIGHEST
MESH_ID = pl.DeviceIdType.MESH
FACES = ((1, 0), (-1, 0), (0, 1), (0, -1))
WIDE, SPAN, PAD = 4, 10, 16


def legendre_pair(degree, points):
    below_poly = np.ones(points.shape)
    top_poly = points.copy()
    for step in range(2, degree + 1):
        below_poly, top_poly = (
            top_poly,
            ((2 * step - 1) * points * top_poly - (step - 1) * below_poly) / step,
        )
    return (below_poly, top_poly)


@functools.lru_cache(None)
def gll_tables(degree):
    nodes = -np.cos(np.pi * np.arange(degree + 1) / degree)
    for _ in range(100):
        below_poly, top_poly = legendre_pair(degree, nodes)
        nodes = nodes - (nodes * top_poly - below_poly) / ((degree + 1) * top_poly)
    at_nodes = legendre_pair(degree, nodes)[1]
    weights = 2.0 / (degree * (degree + 1) * at_nodes**2)
    count = degree + 1
    derivative = np.zeros((count, count))
    for target in range(count):
        for source in range(count):
            if target != source:
                derivative[target, source] = at_nodes[target] / (
                    at_nodes[source] * (nodes[target] - nodes[source])
                )
    derivative[0, 0] = -degree * (degree + 1) / 4.0
    derivative[degree, degree] = degree * (degree + 1) / 4.0
    stiffness = derivative.T @ (weights[:, None] * derivative)
    return (nodes, weights, stiffness)


def lagrange_matrix(fine_degree, coarse_degree):
    fine_nodes = gll_tables(fine_degree)[0]
    coarse_nodes = gll_tables(coarse_degree)[0]
    table = np.ones((fine_degree + 1, coarse_degree + 1))
    for column in range(coarse_degree + 1):
        for other in range(coarse_degree + 1):
            if other != column:
                table[:, column] *= (fine_nodes - coarse_nodes[other]) / (
                    coarse_nodes[column] - coarse_nodes[other]
                )
    return table


@functools.lru_cache(None)
def smoother(degree):
    stiffness = gll_tables(degree)[2]
    elements = 6
    size = elements * degree
    assembled = np.zeros((size, size))
    for element in range(elements):
        for row in range(degree + 1):
            for col in range(degree + 1):
                assembled[(element * degree + row) % size, (element * degree + col) % size] += (
                    stiffness[row, col]
                )
    diagonal = np.sqrt(np.diagonal(assembled))
    scaled = assembled / diagonal[:, None] / diagonal[None, :]
    positions = np.arange(size)
    vector = np.where(positions % 2 == 0, 1.0, -1.0) * (1.0 + positions / size)
    for _ in range(2000):
        vector = scaled @ vector
        vector = vector / np.sqrt(np.sum(vector * vector))
    high = float(np.sum(vector * (scaled @ vector)) / np.sum(vector * vector))
    low = 0.1 * high
    theta, delta = 0.5 * (high + low), 0.5 * (high - low)
    sigma = theta / delta
    rho1 = 1.0 / sigma
    rho2 = 1.0 / (2.0 * sigma - rho1)
    return theta, rho2 * rho1, 2.0 * rho2 / delta * theta


def level(degree):
    _, w, k = gll_tables(degree)
    t = w.copy()
    t[0] = t[-1] = w[0] + w[-1]
    s = np.diagonal(k).copy()
    s[0] = s[-1] = k[0, 0] + k[-1, -1]
    c = np.ones(degree + 1)
    c[0] = c[-1] = 0.5
    diag = (
        s[:, None, None] * t[None, :, None] * t[None, None, :]
        + t[:, None, None] * s[None, :, None] * t[None, None, :]
        + t[:, None, None] * t[None, :, None] * s[None, None, :]
    )
    return w, k, t, c, 1.0 / (diag * smoother(degree)[0])


def join_z(count):
    size = EZ * count
    m = np.eye(size)
    for e in range(EZ):
        a, b = e * count + count - 1, ((e + 1) % EZ) * count
        m[a, b] += 1.0
        m[b, a] += 1.0
    return m


def two(m):
    return np.kron(np.eye(2), m)


def lanes(values):
    return np.broadcast_to(values[None, :], (8, LANES))


def rows(values):
    return np.broadcast_to(np.asarray(values)[..., None], np.shape(values) + (LANES,))


def fourier_rows(total):
    k, n = np.meshgrid(np.arange(total), np.arange(total), indexing="ij")
    half = total // 2
    freq = np.where(k <= half, k, k - half)
    angle = 2.0 * np.pi * (freq * n % total) / total
    scale = np.where((k == 0) | (k == half), math.sqrt(1.0 / total), math.sqrt(2.0 / total))
    return scale * np.where(k <= half, np.cos(angle), np.sin(angle))


def sine_rows(mode, point, total):
    product = mode * point % (2 * total)
    inside = (mode > 0) & (mode < total) & (point > 0) & (point < total)
    return np.where(inside, math.sqrt(2.0 / total) * np.sin(np.pi * product / total), 0.0)


def green_table(nx, ny):
    mode = np.arange(MODES)
    wall_gap = 2.0 * np.sin(0.5 * np.pi * mode / ny) ** 2 + np.where(mode % ny == 0, 1.0, 0.0)
    freq = np.arange(EZ)
    freq = np.where(freq <= EZ // 2, freq, freq - EZ // 2)
    span_gap = 2.0 * np.sin(np.pi * freq / EZ) ** 2
    half_gap = wall_gap[:, None] + span_gap[None, :]
    root = np.sqrt(half_gap * (2.0 + half_gap))
    rate = np.log1p(half_gap + root)
    d = np.arange(nx)[:, None, None]
    top = np.exp(-rate * d) + np.exp(-rate * (nx - d))
    return top / (4.0 * root * -np.expm1(-rate * nx))


def modal(values):
    v = values.reshape(values.shape[:-2] + (MODES // 8, 8, EZ))
    v = np.stack([v, v], axis=-2)
    v = np.moveaxis(v, -4, -3)
    return v.reshape(v.shape[:-3] + (LANES,))


def offsets(radius):
    found = [(0, 0), *FACES]
    for ring in range(2, radius + 1):
        found += [
            (dx, dy)
            for dx in range(-ring, ring + 1)
            for dy in range(-ring, ring + 1)
            if abs(dx) + abs(dy) == ring
        ]
    return found


def assembled_1d(local_cols, window):
    count = local_cols.shape[0]
    out = np.zeros((count, window))
    out[:, 1:3] += local_cols
    out[0, 0:2] += local_cols[-1]
    out[-1, 2:4] += local_cols[0]
    return out


@functools.lru_cache(None)
def build_tables(nx, ny):
    f, q = ORDER + 1, MID_ORDER + 1
    w7, k7, t7, c7, e7 = level(ORDER)
    w3, k3, t3, c3, e3 = level(MID_ORDER)
    j73 = lagrange_matrix(ORDER, MID_ORDER)
    j31 = lagrange_matrix(MID_ORDER, 1)
    tile = {}
    tk = np.tile(t7, EZ)
    ones = np.ones((8, LANES))
    tile["kx"] = np.stack(
        [np.stack([k7[i, a] * t7[:, None] * tk[None, :] for i in range(f)]) for a in range(f)]
    ).reshape(f * f, 8, LANES)
    roll = np.stack([[k7[j, (j - s) % f] for j in range(f)] for s in range(f)])
    tile["ky"] = roll[:, :, None] * tk[None, None, :]
    tile["kyl"] = (k7[f - 1][:, None] * tk[None, :])[None]
    tile["kyf"] = (k7[0][:, None] * tk[None, :])[None]
    tile["e7"] = np.tile(e7, (1, 1, EZ))
    tile["ti"] = np.stack([t * ones for t in t7])
    tile["tij"] = np.stack([t * rows(t7) for t in t7])
    tile["cj"] = rows(c7)[None]
    tile["ci"] = np.stack([c * ones for c in c7])
    tile["jx"] = np.stack([j73[i, a] * ones for i in range(f) for a in range(q)])
    green = modal(green_table(nx, ny))
    tile["green"] = green[(np.arange(nx + SPAN - 1) - WIDE) % nx]
    point = np.arange(-WIDE, ny - WIDE + PAD)
    tile["sine"] = modal(
        np.broadcast_to(
            sine_rows(np.arange(MODES)[None, :], point[:, None], ny)[:, :, None],
            (len(point), MODES, EZ),
        )
    )
    row = {}
    mid = [(a, b) for a in range(q) for b in range(q)]
    tc = np.tile(np.tile(t3, EZ), 2)

    def left(matrix, scale=None):
        scale = np.ones(LANES) if scale is None else scale
        return matrix.T[:, :, None] * scale[None, None, :]

    row["jy"] = left(
        np.array([[(a == a2) * j73[j, b] for a2 in range(q) for j in range(f)] for a, b in mid])
    )
    row["lx"] = left(np.kron(k3, np.diag(t3)), tc)
    row["ly"] = left(np.kron(np.diag(t3), k3), tc)
    row["e3"] = np.stack([np.tile(np.tile(e3[a, b], EZ), 2) for a, b in mid])[None]
    row["tab"] = rows([t3[a] * t3[b] for a, b in mid])[None]
    row["ca"] = rows([c3[a] for a, b in mid])[None]
    row["cb"] = rows([c3[b] for a, b in mid])[None]
    groups = [np.array([j31[a, x] * j31[b, y] for a, b in mid]) for x in (0, 1) for y in (0, 1)]
    row["jj"] = np.repeat(np.stack(groups, axis=1), MODES, axis=1)[None]
    own = np.zeros((q, 4))
    own[:, 1:3] = j31
    stiff = assembled_1d(k3 @ j31, 4)
    mass = t3[:, None] * own

    ring1, ring2, ring3 = offsets(1), offsets(2), offsets(3)

    def placed(first, second, elements):
        out = np.zeros((len(elements), q, q, SPAN, PAD))
        for n, (dx, dy) in enumerate(elements):
            x0, y0 = dx - 1 + WIDE, dy - 1 + WIDE
            out[n, :, :, x0 : x0 + 4, y0 : y0 + 4] = np.einsum("at,bq->abtq", first, second)
        return out.reshape(len(elements) * q * q, SPAN * PAD)

    mat = {}
    mat["kt"] = np.concatenate(
        [placed(stiff, mass, ring3) + placed(mass, stiff, ring3), placed(own, own, ring2)])
    mat["tt"] = placed(mass, mass, ring3)
    cross = np.zeros((len(ring2), q, q, len(ring3), q, q))
    ends = {(1, 0): (3, 0), (-1, 0): (0, 3), (0, 1): (3, 0), (0, -1): (0, 3)}
    diag3 = np.diag(t3)
    for n, (dx, dy) in enumerate(ring2):
        cross[n, :, :, n] += np.einsum("ac,bd->abcd", k3, diag3)
        cross[n, :, :, n] += np.einsum("ac,bd->abcd", diag3, k3)
        for (fx, fy), (mine, theirs) in ends.items():
            m = ring3.index((dx + fx, dy + fy))
            line = np.zeros((q, q))
            line[mine] = k3[theirs]
            if fx:
                cross[n, :, :, m] += np.einsum("ac,bd->abcd", line, diag3)
            else:
                cross[n, :, :, m] += np.einsum("ac,bd->abcd", diag3, line)
    mat["lxy"] = cross.reshape(len(ring2) * 16, len(ring3) * 16)
    k7j = k7 @ j73
    lines = np.zeros((len(ring1), 4, 4, len(ring2), q, q))
    fine = np.zeros((f, f, 48))
    t7j = t7[:, None] * j73
    fine[:, :, :16] = (
        np.einsum("ia,jb->ijab", k7j, t7j) + np.einsum("ia,jb->ijab", t7j, k7j)
    ).reshape(f, f, 16)
    fine[:, :, 32:] = np.einsum("ia,jb->ijab", t7j, t7j).reshape(f, f, 16)
    for face, ((fx, fy), (mine, theirs)) in enumerate(ends.items()):
        mine, theirs = (f - 1 if mine else 0), (f - 1 if theirs else 0)
        for n, (dx, dy) in enumerate(ring1):
            m = ring2.index((dx + fx, dy + fy))
            for c in range(q):
                if fx:
                    lines[n, face, c, m, :, c] = k7j[theirs]
                else:
                    lines[n, face, c, m, c, :] = k7j[theirs]
        if fx:
            fine[mine, :, 16 + 4 * face : 20 + 4 * face] = t7j
        else:
            fine[:, mine, 16 + 4 * face : 20 + 4 * face] = t7j
    mat["lines"] = lines.reshape(len(ring1) * 16, len(ring2) * 16)
    mat["fine"] = fine.reshape(f * f, 48)
    mat["pfine"] = np.einsum("ia,jb->ijab", j73, j73).reshape(f * f, 16)
    row["tc"] = np.broadcast_to(tc, (1, 16, LANES))
    az7 = (join_z(f) @ np.kron(np.eye(EZ), k7)).T
    az3 = two((join_z(q) @ np.kron(np.eye(EZ), k3)).T)
    down = (join_z(q) @ np.kron(np.eye(EZ), j73.T) @ np.diag(np.tile(c7, EZ))).T
    zero = np.zeros_like(down)
    mat["az7"] = az7
    mat["down"] = np.concatenate(
        [np.concatenate([down, zero], axis=1), np.concatenate([zero, down], axis=1)], axis=0
    )
    mat["az3"] = az3
    up = np.kron(np.eye(EZ), j73).T
    mat["up"] = two(up)
    up_tk = up * np.tile(t7, EZ)[None]
    mat["upt"] = np.concatenate([two(up_tk), two(up @ az7)], axis=1)
    gather = np.zeros((EZ, EZ * q))
    for e in range(EZ):
        for node in (0, 1):
            gather[(e + node) % EZ, e * q : (e + 1) * q] += j31[:, node] * c3
    b1 = two((fourier_rows(EZ) @ gather).T)
    b1 = np.tile(b1, (1, 4))
    mat["b12"] = np.concatenate([b1, az3 @ b1], axis=0)
    spread = np.zeros((EZ * q, EZ))
    for e in range(EZ):
        for node in (0, 1):
            spread[e * q : (e + 1) * q, (e + node) % EZ] += j31[:, node]
    back = two((spread @ fourier_rows(EZ).T).T)
    back = np.tile(back, (4, 1))
    mat["back"] = np.concatenate([back, back @ az3], axis=1)
    mode, here = np.arange(MODES)[:, None], np.arange(32)[None, :]
    s0 = np.where(here < ny, sine_rows(mode, here, ny), 0.0)
    s1 = np.where(here < ny, sine_rows(mode, here + 1, ny), 0.0)
    mat["sin"] = np.concatenate([s0, s1], axis=0)
    packed, where = [], {}
    at = 0
    for name, value in tile.items():
        where[name] = (at, value.shape[0])
        packed.append(value)
        at += value.shape[0]
    tiles = np.concatenate(packed).astype(np.float32)
    packed, at = [], 0
    for name, value in row.items():
        where[name] = (at, value.shape[0])
        packed.append(value)
        at += value.shape[0]
    row16 = np.concatenate(packed).astype(np.float32)
    mats = {name: value.astype(np.float32) for name, value in mat.items()}
    return tiles, row16, mats, where


MATS = ("az7", "down", "az3", "b12", "sin", "back", "kt", "tt", "lxy", "lines", "up", "upt",
        "fine", "pfine")
N_LINKS = 8 + 4 + 4 + 8 + 4 + 4 + 12 + 24 + 4


def reach(n):
    base = max(n // 8, 1)
    known, hops = base, []
    while known < n // 2:
        hops.append(known)
        known *= 2
    return range(1, base + 1), hops


def kernel(nx, ny, where, *refs):
    names = ("x", "tiles", "rows") + MATS
    count = len(names)
    hbm, out_ref, vmem = refs[:count], refs[count], refs[count + 1 : 2 * count + 1]
    (fine_send, fine_recv, mid_send, mid_recv, line_send, line_recv, mode_send, mode_recv,
     rest3_all, x3_all, rest7_all, load_sem, send_sem, recv_sem, line_ss, line_rs, mode_ss, mode_rs, known) = refs[2 * count + 1 :]
    sx, cx = lax.axis_index("stream"), lax.axis_index("cross")
    tile_ref, row_ref = vmem[1], vmem[2]
    mat = dict(zip(MATS, vmem[3:]))

    def at(dx, dy):
        return {"stream": lax.rem(sx + (nx + dx), nx), "cross": lax.rem(cx + (ny + dy), ny)}

    def tab(name):
        start, size = where[name]
        return tile_ref[start : start + size]

    def rtab(name):
        start, size = where[name]
        return row_ref[start : start + size]

    bar = pltpu.get_barrier_semaphore()
    corners = ((1, 1), (1, -1), (-1, 1), (-1, -1))
    faces = FACES
    near_x, hops_x = reach(nx)
    near_y, hops_y = reach(ny)
    near = [(s * d, 0) for d in near_x for s in (1, -1)]
    near += [(0, s * d) for d in near_y for s in (1, -1)]
    near += corners
    for d in near:
        pl.semaphore_signal(bar, inc=1, device_id=at(*d), device_id_type=MESH_ID)
    loads = {}
    for n, name in enumerate(names):
        loads[name] = pltpu.make_async_copy(hbm[n], vmem[n], load_sem.at[n])
        loads[name].start()

    def need(*wanted):
        for name in wanted:
            if name in loads:
                loads.pop(name).wait()

    def tell(step):
        for n, hops in enumerate((hops_x, hops_y)):
            if step < len(hops):
                for s in (1, -1):
                    d = (s * hops[step], 0) if n == 0 else (0, s * hops[step])
                    pl.semaphore_signal(
                        known.at[step, n], inc=1, device_id=at(*d), device_id_type=MESH_ID)

    def told(step):
        for n, hops in enumerate((hops_x, hops_y)):
            if step < len(hops):
                pl.semaphore_wait(known.at[step, n], 2)

    links = [0]
    sent = []

    def start(src, dst, to):
        n = links[0]
        links[0] += 1
        copy = pltpu.make_async_remote_copy(
            src, dst, send_sem.at[n], recv_sem.at[n], device_id=at(*to), device_id_type=MESH_ID)
        copy.start()
        sent.append(copy)
        return copy

    jrow = lax.broadcasted_iota(jnp.int32, (8, LANES), 0)
    lane = lax.broadcasted_iota(jnp.int32, (8, LANES), 1)
    low_wall = jnp.where(cx == 0, 0, -1)
    high_wall = jnp.where(cx == ny - 1, ORDER, -1)
    keep7 = jnp.where((jrow == low_wall) | (jrow == high_wall), 0.0, 1.0)
    mrow = lax.broadcasted_iota(jnp.int32, (16, LANES), 0)
    brow = lax.rem(mrow, 4)
    high_wall3 = jnp.where(cx == ny - 1, MID_ORDER, -1)
    keep3 = jnp.where((brow == low_wall) | (brow == high_wall3), 0.0, 1.0)
    _, keep_f, gain_f = smoother(ORDER)
    _, keep_m, gain_m = smoother(MID_ORDER)

    def dot(a, b):
        return jnp.dot(a, b, preferred_element_type=jnp.float32, precision=EXACT)

    def fine_xy(u):
        kx = tab("kx").reshape(8, 8, 8, LANES)
        ax = kx[0][None] * u[:, 0:1]
        for a in range(1, 8):
            ax = ax + kx[a][None] * u[:, a : a + 1]
        ky = tab("ky")
        flat = u.reshape(16, 8, LANES)
        ay = ky[0][None] * flat
        for s in range(1, 8):
            ay = ay + ky[s][None] * pltpu.roll(flat, s, 1)
        return ax, ay.reshape(2, 8, 8, LANES) * tab("ti")[None]

    def fine_z(u):
        az = dot(u.reshape(128, LANES), mat["az7"][...])
        return az.reshape(2, 8, 8, LANES) * tab("tij")[None]

    def fine_send_faces(n, ax, ay):
        fine_send[n, 0] = ax[:, 7].reshape(16, LANES)
        fine_send[n, 1] = ax[:, 0].reshape(16, LANES)
        flat = ay.reshape(16, 8, LANES)
        fine_send[n, 2] = flat[:, 7, :]
        fine_send[n, 3] = flat[:, 0, :]
        return [start(fine_send.at[n, d], fine_recv.at[n, d], faces[d]) for d in range(4)]

    def add_x(field, low, high):
        return jnp.concatenate(
            [field[:, 0:1] + low.reshape(2, 1, 8, LANES), field[:, 1:7],
             field[:, 7:8] + high.reshape(2, 1, 8, LANES)], axis=1)

    def add_y(field, low, high):
        flat = field.reshape(16, 8, LANES)
        flat = flat + jnp.where(jrow[None] == 0, low[:, None, :], 0.0)
        flat = flat + jnp.where(jrow[None] == 7, high[:, None, :], 0.0)
        return flat.reshape(2, 8, 8, LANES)

    def fine_join(n, copies, field):
        for copy in copies:
            copy.wait_recv()
        field = add_x(field, fine_recv[n, 0], fine_recv[n, 1])
        return add_y(field, fine_recv[n, 2], fine_recv[n, 3])

    def left(name, v):
        start_row, size = where[name]
        acc = row_ref[start_row] * v[0:1]
        for c in range(1, size):
            acc = acc + row_ref[start_row + c] * v[c : c + 1]
        return acc

    def mid_start(n, ax, ay):
        mid_send[n, 0] = ax
        mid_send[n, 1] = ay
        return [start(mid_send.at[n, d // 2], mid_recv.at[n, d], faces[d]) for d in range(4)]

    def shifted(v, shift, mask):
        return jnp.where(mask, pltpu.roll(v, shift, 0), 0.0)

    def mid_join(n, copies, field):
        for copy in copies:
            copy.wait_recv()
        field = field + shifted(mid_recv[n, 0], 4, mrow < 4)
        field = field + shifted(mid_recv[n, 1], 12, mrow >= 12)
        field = field + shifted(mid_recv[n, 2], 13, brow == 0)
        return field + shifted(mid_recv[n, 3], 3, brow == 3)

    need("x")
    src = vmem[0][...].reshape(16, 8, LANES)
    knode = lax.rem(lane, 8)
    src = (src + jnp.where(knode[None] == 7, pltpu.roll(src, LANES - 1, 2), 0.0)
           + jnp.where(knode[None] == 0, pltpu.roll(src, 1, 2), 0.0))
    fine_send[0, 2] = src[:, 7, :]
    fine_send[0, 3] = src[:, 0, :]
    src = src.reshape(2, 8, 8, LANES)
    fine_send[0, 0] = src[:, 7].reshape(16, LANES)
    fine_send[0, 1] = src[:, 0].reshape(16, LANES)
    pl.semaphore_wait(bar, len(near))
    tell(0)
    copies = [start(fine_send.at[0, 2 if d[1] > 0 else 3], fine_recv.at[5, n], d)
              for n, d in enumerate(corners)]
    copies += [start(fine_send.at[0, d], fine_recv.at[0, d], faces[d]) for d in range(4)]
    need("tiles", "az7")
    e7 = tab("e7") * keep7[None]
    for copy in copies:
        copy.wait_recv()
    told(0)
    tell(1)
    irow = jrow[None]

    def end(n, shift, row):
        line = fine_recv[5, n].reshape(2, 8, LANES)
        return jnp.where(irow == row, pltpu.roll(line, shift, 1), 0.0).reshape(16, LANES)

    low = fine_recv[0, 2] + end(0, 1, 0) + end(2, 7, 7)
    high = fine_recv[0, 3] + end(1, 1, 0) + end(3, 7, 7)
    b7 = add_y(add_x(src, fine_recv[0, 0], fine_recv[0, 1]), low, high)

    u1 = e7[None] * b7
    ax, ay = fine_xy(u1)
    copies = fine_send_faces(1, ax, ay)
    az = fine_z(u1)
    r1 = b7 - fine_join(1, copies, ax + ay + az)
    x7 = (1.0 + keep_f) * u1 + gain_f * (e7[None] * r1)
    ax, ay = fine_xy(x7)
    side7 = fine_send_faces(2, ax, ay)
    az = fine_z(x7)
    local7 = ax + ay + az
    ci = tab("ci")[None]
    rest7 = (src - tab("cj")[None] * (ax + ci * az) - ci * ay) * keep7[None, None]
    need("rows", "down")
    jx = tab("jx").reshape(8, 4, 8, LANES)
    g = jx[0][None] * rest7[:, 0:1]
    for i in range(1, 8):
        g = g + jx[i][None] * rest7[:, i : i + 1]
    g = jnp.concatenate([g[0].reshape(32, LANES), g[1].reshape(32, LANES)], axis=1)
    g3 = left("jy", dot(g, mat["down"][...]))
    mid_send[3, 0] = g3
    around = faces + corners
    copies = [start(mid_send.at[3, 0], mid_recv.at[3 + n // 4, n % 4], d)
              for n, d in enumerate(around)]
    rest7_all[0] = (b7 - fine_join(2, side7, local7)).reshape(128, LANES)
    for copy in copies:
        copy.wait_recv()
    shifts = ((4, mrow < 4), (12, mrow >= 12), (13, brow == 0), (3, brow == 3),
              (1, mrow == 0), (7, mrow == 3), (9, mrow == 12), (15, mrow == 15))
    b3 = g3
    for n, (shift, mask) in enumerate(shifts):
        b3 = b3 + shifted(mid_recv[3 + n // 4, n % 4], shift, mask)

    need("az3", "b12")
    told(1)
    e3 = rtab("e3")[0] * keep3
    tab3 = rtab("tab")[0]

    def mid_z(v):
        return tab3 * dot(v, mat["az3"][...])

    v1 = e3 * b3
    ax, ay = left("lx", v1), left("ly", v1)
    copies = mid_start(0, ax, ay)
    az = mid_z(v1)
    r1 = b3 - mid_join(0, copies, ax + ay + az)
    x3 = (1.0 + keep_m) * v1 + gain_m * (e3 * r1)
    ax, ay = left("lx", x3), left("ly", x3)
    ca, cb = rtab("ca")[0], rtab("cb")[0]
    part = keep3 * (g3 - cb * ax - ca * ay)
    other = keep3 * (ca * cb * tab3) * x3
    line = dot(jnp.concatenate([part, -other], axis=1), mat["b12"][...])
    line = jnp.sum(rtab("jj")[0] * line, axis=0, keepdims=True)
    line_send[0] = line

    def line_copy(d, slot, to):
        return pltpu.make_async_remote_copy(
            line_send.at[0], line_recv.at[slot], line_ss.at[d], line_rs.at[d],
            device_id={"cross": to}, device_id_type=MESH_ID)

    def line_out(d, carry):
        line_copy(d, cx, lax.rem(cx + d, ny)).start()
        return carry

    lax.fori_loop(1, ny, line_out, 0)
    line_recv[cx] = line
    ring1, ring2, ring3 = offsets(1), offsets(2), offsets(3)
    side3 = mid_start(1, ax, ay)
    x3_all[0] = x3
    side = [start(x3_all.at[0], x3_all.at[n], (-dx, -dy))
            for n, (dx, dy) in enumerate(ring2) if n]
    side += [start(rest7_all.at[0], rest7_all.at[n], (-dx, -dy))
             for n, (dx, dy) in enumerate(ring1) if n]
    if ny < 32:
        line_recv[ny:] = jnp.zeros((32 - ny, 1, LANES), jnp.float32)
    rest3_all[0] = b3 - mid_join(1, side3, ax + ay + mid_z(x3))
    side += [start(rest3_all.at[0], rest3_all.at[n], (-dx, -dy))
             for n, (dx, dy) in enumerate(ring3) if n]
    need("sin")

    def line_in(d, carry):
        line_copy(d, lax.rem(cx + ny - d, ny), cx).wait()
        return carry

    lax.fori_loop(1, ny, line_in, 0)
    spectrum = dot(mat["sin"][...], line_recv[:, 0, :])
    group = lax.div(lane, 32)
    for alpha in range(2):
        total = jnp.zeros((8, LANES), jnp.float32)
        for hi in range(4):
            for beta in range(2):
                piece = spectrum[(beta * 4 + hi) * 8 : (beta * 4 + hi + 1) * 8]
                shift = 32 * (hi - 2 * alpha - beta) % LANES
                if shift:
                    piece = pltpu.roll(piece, shift, 1)
                total = total + jnp.where(group == hi, piece, 0.0)
        mode_send[alpha] = total

    def mode_copy(d, to):
        return pltpu.make_async_remote_copy(
            mode_send, mode_recv.at[d], mode_ss.at[d], mode_rs.at[d],
            device_id={"stream": to}, device_id_type=MESH_ID)

    def mode_out(d, carry):
        mode_copy(d, lax.rem(sx + d, nx)).start()
        return carry

    def mode_in(d, carry):
        mode_copy(d, sx).wait()
        return carry

    lax.fori_loop(1, nx, mode_out, 0)
    mode_recv[0] = mode_send[...]
    lax.fori_loop(1, nx, mode_in, 0)
    first = mode_recv[:, 0]
    second = mode_recv[:, 1]
    nodes = first + jnp.concatenate([second[1:], second[:1]], axis=0)
    start_g = where["green"][0]
    solved = [jnp.sum(tile_ref[start_g + n : start_g + n + nx] * nodes, axis=0)
              for n in range(SPAN)]
    sine = tile_ref[pl.ds(where["sine"][0] + cx, PAD)]
    window = [jnp.sum(sine * s[None], axis=1) for s in solved]
    window = jnp.concatenate(window, axis=0)
    need(*MATS)
    window = dot(window, mat["back"][...])
    zval, zstiff = window[:, :LANES], window[:, LANES:]

    def masked(dy, table, top, index):
        low = jnp.where(cx + dy == 0, 0, -1)
        high = jnp.where(cx + dy == ny - 1, top, -1)
        return table * jnp.where((index == low) | (index == high), 0.0, 1.0)

    e3 = {dy: masked(dy, rtab("e3")[0], MID_ORDER, brow) for dy in range(-3, 4)}
    tc = rtab("tc")[0]
    n2, n3 = 16 * len(ring2), 16 * len(ring3)
    for copy in side:
        copy.wait_recv()

    def per(table, count):
        return jnp.concatenate([table] * count, axis=0)

    from_low = dot(mat["kt"][...], zval)
    r0 = rest3_all[...].reshape(n3, LANES) - per(tc, len(ring3)) * from_low[:n3]
    r0 = r0 - dot(mat["tt"][...], zstiff)
    e3_all = jnp.concatenate([e3[dy] for _, dy in ring3], axis=0)
    w1 = e3_all * r0
    aw = per(tc, len(ring2)) * dot(mat["lxy"][...], w1)
    aw = aw + per(tab3, len(ring2)) * dot(w1[:n2], mat["az3"][...])
    x3 = x3_all[...].reshape(n2, LANES) + from_low[n3:]
    x3 = x3 + (1.0 + keep_m) * w1[:n2] + gain_m * (e3_all[:n2] * (r0[:n2] - aw))

    n1 = 16 * len(ring1)
    lines = dot(dot(mat["lines"][...], x3), mat["upt"][:, : 2 * LANES])
    mine = dot(x3[:n1], mat["upt"][...])
    px = dot(x3[:16], mat["up"][...])
    px = jnp.stack([dot(mat["pfine"][...], px[:, r * LANES : (r + 1) * LANES]) for r in range(2)])
    px = px.reshape(2, 8, 8, LANES)
    columns = []
    for n in range(len(ring1)):
        for r in range(2):
            at_n, at_r = slice(16 * n, 16 * n + 16), slice(r * LANES, (r + 1) * LANES)
            also = slice((2 + r) * LANES, (3 + r) * LANES)
            columns.append(jnp.concatenate(
                [mine[at_n, at_r], lines[at_n, at_r], mine[at_n, also]], axis=0))
    apx = dot(mat["fine"][...], jnp.concatenate(columns, axis=1))
    kx = tab("kx").reshape(8, 8, 8, LANES)
    ky_last, ky_first = tab("kyl"), tab("kyf")
    r0, u1 = [], []
    for n, (dx, dy) in enumerate(ring1):
        moved = jnp.stack([apx[:, (2 * n + r) * LANES : (2 * n + r + 1) * LANES] for r in range(2)])
        r0.append(rest7_all[n].reshape(2, 8, 8, LANES) - moved.reshape(2, 8, 8, LANES))
        scale = masked(dy, tab("e7"), ORDER, jrow[None]) if dy else e7
        u1.append(scale[None] * r0[n])

    def along_x(u, row):
        acc = kx[0][row][None] * u[:, 0]
        for a in range(1, 8):
            acc = acc + kx[a][row][None] * u[:, a]
        return acc.reshape(16, LANES)

    def along_y(u, table):
        weighted = jnp.sum(table[None] * u, axis=2)
        return (tab("ti")[:, 0][None] * weighted).reshape(16, LANES)

    ax, ay = fine_xy(u1[0])
    au = ax + ay + fine_z(u1[0])
    au = add_x(au, along_x(u1[2], 7), along_x(u1[1], 0))
    au = add_y(au, along_y(u1[4], ky_last), along_y(u1[3], ky_first))
    x7 = x7 + px
    out = x7 + (1.0 + keep_f) * u1[0] + gain_f * (e7[None] * (r0[0] - au))
    out_ref[...] = out.reshape(128, LANES)
    for copy in sent:
        copy.wait_send()


def solution(mesh):
    nx, ny = mesh.shape["stream"], mesh.shape["cross"]
    tiles, row16, mats, where = build_tables(nx, ny)

    def body(sources):
        flat = sources.reshape(128, LANES)
        operands = [flat, jnp.asarray(tiles), jnp.asarray(row16)]
        operands += [jnp.asarray(mats[name]) for name in MATS]
        links, f32 = pltpu.SemaphoreType.DMA, jnp.float32
        out = pl.pallas_call(
            functools.partial(kernel, nx, ny, where),
            out_shape=jax.ShapeDtypeStruct((128, LANES), jnp.float32),
            in_specs=[pl.BlockSpec(memory_space=pl.ANY)] * len(operands),
            out_specs=pl.BlockSpec(memory_space=pltpu.VMEM),
            scratch_shapes=[pltpu.VMEM(o.shape, f32) for o in operands]
            + [
                pltpu.VMEM((5, 4, 16, LANES), f32),
                pltpu.VMEM((6, 4, 16, LANES), f32),
                pltpu.VMEM((4, 2, 16, LANES), f32),
                pltpu.VMEM((5, 4, 16, LANES), f32),
                pltpu.VMEM((1, 1, LANES), f32),
                pltpu.VMEM((32, 1, LANES), f32),
                pltpu.VMEM((2, 8, LANES), f32),
                pltpu.VMEM((nx, 2, 8, LANES), f32),
                pltpu.VMEM((len(offsets(3)), 16, LANES), f32),
                pltpu.VMEM((len(offsets(2)), 16, LANES), f32),
                pltpu.VMEM((len(offsets(1)), 128, LANES), f32),
                links((len(operands),)),
                links((N_LINKS,)),
                links((N_LINKS,)),
                links((ny,)),
                links((ny,)),
                links((nx,)),
                links((nx,)),
                pltpu.SemaphoreType.REGULAR((2, 2)),
            ],
            compiler_params=pltpu.CompilerParams(collective_id=0, has_side_effects=True),
            name="vcycle",
        )(*operands)
        return out.reshape(sources.shape)

    spec = P(None, "stream", "cross", None, None, None)
    return jax.shard_map(body, mesh=mesh, in_specs=(spec,), out_specs=spec, check_vma=False)
```

```python
import functools
import math

import jax
import jax.numpy as jnp
import numpy as np
from jax import lax
from jax.experimental import pallas as pl
from jax.experimental.pallas import tpu as pltpu
from jax.sharding import PartitionSpec as P

ORDER = 7
MID_ORDER = 3
EZ = 16
LANES = 128
MODES = 32
MESH_ID = pl.DeviceIdType.MESH
FACES = ((1, 0), (-1, 0), (0, 1), (0, -1))
CORNERS = ((1, 1), (1, -1), (-1, 1), (-1, -1))
TWICE = ((2, 0), (-2, 0), (0, 2), (0, -2))
KNIGHTS = tuple((s * a, t * b) for a, b in ((2, 1), (1, 2)) for s in (1, -1) for t in (1, -1))
AROUND = ((0, 0),) + FACES + CORNERS + TWICE + KNIGHTS
WIDE, SPAN, PAD = 4, 10, 16


def legendre_pair(degree, points):
    below_poly = np.ones(points.shape)
    top_poly = points.copy()
    for step in range(2, degree + 1):
        below_poly, top_poly = (
            top_poly,
            ((2 * step - 1) * points * top_poly - (step - 1) * below_poly) / step,
        )
    return (below_poly, top_poly)


@functools.lru_cache(None)
def gll_tables(degree):
    nodes = -np.cos(np.pi * np.arange(degree + 1) / degree)
    for _ in range(100):
        below_poly, top_poly = legendre_pair(degree, nodes)
        nodes = nodes - (nodes * top_poly - below_poly) / ((degree + 1) * top_poly)
    at_nodes = legendre_pair(degree, nodes)[1]
    weights = 2.0 / (degree * (degree + 1) * at_nodes**2)
    count = degree + 1
    derivative = np.zeros((count, count))
    for target in range(count):
        for source in range(count):
            if target != source:
                derivative[target, source] = at_nodes[target] / (
                    at_nodes[source] * (nodes[target] - nodes[source])
                )
    derivative[0, 0] = -degree * (degree + 1) / 4.0
    derivative[degree, degree] = degree * (degree + 1) / 4.0
    stiffness = derivative.T @ (weights[:, None] * derivative)
    return (nodes, weights, stiffness)


def lagrange_matrix(fine_degree, coarse_degree):
    fine_nodes = gll_tables(fine_degree)[0]
    coarse_nodes = gll_tables(coarse_degree)[0]
    table = np.ones((fine_degree + 1, coarse_degree + 1))
    for column in range(coarse_degree + 1):
        for other in range(coarse_degree + 1):
            if other != column:
                table[:, column] *= (fine_nodes - coarse_nodes[other]) / (
                    coarse_nodes[column] - coarse_nodes[other]
                )
    return table


@functools.lru_cache(None)
def smoother(degree):
    stiffness = gll_tables(degree)[2]
    elements = 6
    size = elements * degree
    assembled = np.zeros((size, size))
    for element in range(elements):
        for row in range(degree + 1):
            for col in range(degree + 1):
                assembled[(element * degree + row) % size, (element * degree + col) % size] += (
                    stiffness[row, col]
                )
    diagonal = np.sqrt(np.diagonal(assembled))
    scaled = assembled / diagonal[:, None] / diagonal[None, :]
    positions = np.arange(size)
    vector = np.where(positions % 2 == 0, 1.0, -1.0) * (1.0 + positions / size)
    for _ in range(2000):
        vector = scaled @ vector
        vector = vector / np.sqrt(np.sum(vector * vector))
    high = float(np.sum(vector * (scaled @ vector)) / np.sum(vector * vector))
    low = 0.1 * high
    theta, delta = 0.5 * (high + low), 0.5 * (high - low)
    sigma = theta / delta
    rho1 = 1.0 / sigma
    rho2 = 1.0 / (2.0 * sigma - rho1)
    return theta, rho2 * rho1, 2.0 * rho2 / delta * theta


def level(degree):
    _, w, k = gll_tables(degree)
    t = w.copy()
    t[0] = t[-1] = w[0] + w[-1]
    s = np.diagonal(k).copy()
    s[0] = s[-1] = k[0, 0] + k[-1, -1]
    c = np.ones(degree + 1)
    c[0] = c[-1] = 0.5
    diag = (
        s[:, None, None] * t[None, :, None] * t[None, None, :]
        + t[:, None, None] * s[None, :, None] * t[None, None, :]
        + t[:, None, None] * t[None, :, None] * s[None, None, :]
    )
    return w, k, t, c, 1.0 / (diag * smoother(degree)[0])


def join_z(count):
    size = EZ * count
    m = np.eye(size)
    for e in range(EZ):
        a, b = e * count + count - 1, ((e + 1) % EZ) * count
        m[a, b] += 1.0
        m[b, a] += 1.0
    return m


def two(m):
    return np.kron(np.eye(2), m)


def lanes(values):
    return np.broadcast_to(values[None, :], (8, LANES))


def rows(values):
    return np.broadcast_to(np.asarray(values)[..., None], np.shape(values) + (LANES,))


def fourier_rows(total):
    k, n = np.meshgrid(np.arange(total), np.arange(total), indexing="ij")
    half = total // 2
    freq = np.where(k <= half, k, k - half)
    angle = 2.0 * np.pi * (freq * n % total) / total
    scale = np.where((k == 0) | (k == half), math.sqrt(1.0 / total), math.sqrt(2.0 / total))
    return scale * np.where(k <= half, np.cos(angle), np.sin(angle))


def sine_rows(mode, point, total):
    product = mode * point % (2 * total)
    inside = (mode > 0) & (mode < total) & (point > 0) & (point < total)
    return np.where(inside, math.sqrt(2.0 / total) * np.sin(np.pi * product / total), 0.0)


def green_table(nx, ny):
    mode = np.arange(MODES)
    wall_gap = 2.0 * np.sin(0.5 * np.pi * mode / ny) ** 2 + np.where(mode % ny == 0, 1.0, 0.0)
    freq = np.arange(EZ)
    freq = np.where(freq <= EZ // 2, freq, freq - EZ // 2)
    span_gap = 2.0 * np.sin(np.pi * freq / EZ) ** 2
    half_gap = wall_gap[:, None] + span_gap[None, :]
    root = np.sqrt(half_gap * (2.0 + half_gap))
    rate = np.log1p(half_gap + root)
    d = np.arange(nx)[:, None, None]
    top = np.exp(-rate * d) + np.exp(-rate * (nx - d))
    return top / (4.0 * root * -np.expm1(-rate * nx))


def modal(values):
    v = values.reshape(values.shape[:-2] + (MODES // 8, 8, EZ))
    v = np.stack([v, v], axis=-2)
    v = np.moveaxis(v, -4, -3)
    return v.reshape(v.shape[:-3] + (LANES,))


def offsets(radius):
    found = [(0, 0), *FACES]
    for ring in range(2, radius + 1):
        found += [
            (dx, dy)
            for dx in range(-ring, ring + 1)
            for dy in range(-ring, ring + 1)
            if abs(dx) + abs(dy) == ring
        ]
    return found


def assembled_1d(local_cols, window):
    count = local_cols.shape[0]
    out = np.zeros((count, window))
    out[:, 1:3] += local_cols
    out[0, 0:2] += local_cols[-1]
    out[-1, 2:4] += local_cols[0]
    return out


@functools.lru_cache(None)
def build_tables(nx, ny):
    f, q = ORDER + 1, MID_ORDER + 1
    w7, k7, t7, c7, e7 = level(ORDER)
    w3, k3, t3, c3, e3 = level(MID_ORDER)
    j73 = lagrange_matrix(ORDER, MID_ORDER)
    j31 = lagrange_matrix(MID_ORDER, 1)
    tile = {}
    tk = np.tile(t7, EZ)
    ones = np.ones((8, LANES))
    tile["kx"] = np.stack(
        [np.stack([k7[i, a] * t7[:, None] * tk[None, :] for i in range(f)]) for a in range(f)]
    ).reshape(f * f, 8, LANES)
    roll = np.stack([[k7[j, (j - s) % f] for j in range(f)] for s in range(f)])
    tile["ky"] = roll[:, :, None] * tk[None, None, :]
    tile["kyl"] = (k7[f - 1][:, None] * tk[None, :])[None]
    tile["kyf"] = (k7[0][:, None] * tk[None, :])[None]
    tile["e7"] = np.tile(e7, (1, 1, EZ))
    tile["ti"] = np.stack([t * ones for t in t7])
    tile["tij"] = np.stack([t * rows(t7) for t in t7])
    tile["cj"] = rows(c7)[None]
    tile["ci"] = np.stack([c * ones for c in c7])
    tile["jx"] = np.stack([j73[i, a] * ones for i in range(f) for a in range(q)])
    green = modal(green_table(nx, ny))
    tile["green"] = green[(np.arange(nx + SPAN - 1) - WIDE) % nx]
    point = np.arange(-WIDE, ny - WIDE + PAD)
    tile["sine"] = modal(
        np.broadcast_to(
            sine_rows(np.arange(MODES)[None, :], point[:, None], ny)[:, :, None],
            (len(point), MODES, EZ),
        )
    )
    row = {}
    mid = [(a, b) for a in range(q) for b in range(q)]
    tc = np.tile(np.tile(t3, EZ), 2)

    def left(matrix, scale=None):
        scale = np.ones(LANES) if scale is None else scale
        return matrix.T[:, :, None] * scale[None, None, :]

    row["jy"] = left(
        np.array([[(a == a2) * j73[j, b] for a2 in range(q) for j in range(f)] for a, b in mid])
    )
    row["lx"] = left(np.kron(k3, np.diag(t3)), tc)
    row["ly"] = left(np.kron(np.diag(t3), k3), tc)
    row["e3"] = np.stack([np.tile(np.tile(e3[a, b], EZ), 2) for a, b in mid])[None]
    row["tab"] = rows([t3[a] * t3[b] for a, b in mid])[None]
    row["ca"] = rows([c3[a] for a, b in mid])[None]
    row["cb"] = rows([c3[b] for a, b in mid])[None]
    groups = [np.array([j31[a, x] * j31[b, y] for a, b in mid]) for x in (0, 1) for y in (0, 1)]
    row["jj"] = np.repeat(np.stack(groups, axis=1), MODES, axis=1)[None]
    own = np.zeros((q, 4))
    own[:, 1:3] = j31
    stiff = assembled_1d(k3 @ j31, 4)
    mass = t3[:, None] * own

    ring1, ring2, ring3 = offsets(1), offsets(2), offsets(3)

    def placed(first, second, elements):
        out = np.zeros((len(elements), q, q, SPAN, PAD))
        for n, (dx, dy) in enumerate(elements):
            x0, y0 = dx - 1 + WIDE, dy - 1 + WIDE
            out[n, :, :, x0 : x0 + 4, y0 : y0 + 4] = np.einsum("at,bq->abtq", first, second)
        return out.reshape(len(elements) * q * q, SPAN * PAD)

    mat = {}
    mat["kt"] = np.concatenate(
        [placed(stiff, mass, ring3) + placed(mass, stiff, ring3), placed(own, own, ring2)])
    mat["tt"] = placed(mass, mass, ring3)
    cross = np.zeros((len(ring2), q, q, len(ring3), q, q))
    ends = {(1, 0): (3, 0), (-1, 0): (0, 3), (0, 1): (3, 0), (0, -1): (0, 3)}
    diag3 = np.diag(t3)
    for n, (dx, dy) in enumerate(ring2):
        cross[n, :, :, n] += np.einsum("ac,bd->abcd", k3, diag3)
        cross[n, :, :, n] += np.einsum("ac,bd->abcd", diag3, k3)
        for (fx, fy), (mine, theirs) in ends.items():
            m = ring3.index((dx + fx, dy + fy))
            line = np.zeros((q, q))
            line[mine] = k3[theirs]
            if fx:
                cross[n, :, :, m] += np.einsum("ac,bd->abcd", line, diag3)
            else:
                cross[n, :, :, m] += np.einsum("ac,bd->abcd", diag3, line)
    pick = np.zeros((len(ring1), q, q, len(AROUND), q, q))
    for n, (dx, dy) in enumerate(ring1):
        for m, (gx, gy) in enumerate(AROUND):
            sx, sy = gx - dx, gy - dy
            if max(abs(sx), abs(sy)) > 1:
                continue
            span_x = [(a, a) for a in range(q)] if sx == 0 else [(q - 1, 0) if sx > 0 else (0, q - 1)]
            span_y = [(b, b) for b in range(q)] if sy == 0 else [(q - 1, 0) if sy > 0 else (0, q - 1)]
            for a, a2 in span_x:
                for b, b2 in span_y:
                    pick[n, a, b, m, a2, b2] = 1.0
    mat["pick"] = pick.reshape(len(ring1) * 16, len(AROUND) * 16)
    mat["lxy"] = cross.reshape(len(ring2) * 16, len(ring3) * 16)
    k7j = k7 @ j73
    lines = np.zeros((len(ring1), 4, 4, len(ring2), q, q))
    fine = np.zeros((f, f, 48))
    t7j = t7[:, None] * j73
    fine[:, :, :16] = (
        np.einsum("ia,jb->ijab", k7j, t7j) + np.einsum("ia,jb->ijab", t7j, k7j)
    ).reshape(f, f, 16)
    fine[:, :, 32:] = np.einsum("ia,jb->ijab", t7j, t7j).reshape(f, f, 16)
    for face, ((fx, fy), (mine, theirs)) in enumerate(ends.items()):
        mine, theirs = (f - 1 if mine else 0), (f - 1 if theirs else 0)
        for n, (dx, dy) in enumerate(ring1):
            m = ring2.index((dx + fx, dy + fy))
            for c in range(q):
                if fx:
                    lines[n, face, c, m, :, c] = k7j[theirs]
                else:
                    lines[n, face, c, m, c, :] = k7j[theirs]
        if fx:
            fine[mine, :, 16 + 4 * face : 20 + 4 * face] = t7j
        else:
            fine[:, mine, 16 + 4 * face : 20 + 4 * face] = t7j
    mat["lown"] = mat["lxy"][:16, : 16 * len(ring1)]
    mat["lines"] = lines.reshape(len(ring1) * 16, len(ring2) * 16)
    mat["fine"] = fine.reshape(f * f, 48)
    mat["pfine"] = np.einsum("ia,jb->ijab", j73, j73).reshape(f * f, 16)
    row["tc"] = np.broadcast_to(tc, (1, 16, LANES))
    az7 = (join_z(f) @ np.kron(np.eye(EZ), k7)).T
    az3 = two((join_z(q) @ np.kron(np.eye(EZ), k3)).T)
    down = (join_z(q) @ np.kron(np.eye(EZ), j73.T) @ np.diag(np.tile(c7, EZ))).T
    zero = np.zeros_like(down)
    mat["az7"] = az7
    mat["down"] = np.concatenate(
        [np.concatenate([down, zero], axis=1), np.concatenate([zero, down], axis=1)], axis=0
    )
    mat["az3"] = az3
    up = np.kron(np.eye(EZ), j73).T
    mat["up"] = two(up)
    up_tk = up * np.tile(t7, EZ)[None]
    mat["upt"] = np.concatenate([two(up_tk), two(up @ az7)], axis=1)
    gather = np.zeros((EZ, EZ * q))
    for e in range(EZ):
        for node in (0, 1):
            gather[(e + node) % EZ, e * q : (e + 1) * q] += j31[:, node] * c3
    b1 = two((fourier_rows(EZ) @ gather).T)
    b1 = np.tile(b1, (1, 4))
    mat["b12"] = np.concatenate([b1, az3 @ b1], axis=0)
    spread = np.zeros((EZ * q, EZ))
    for e in range(EZ):
        for node in (0, 1):
            spread[e * q : (e + 1) * q, (e + node) % EZ] += j31[:, node]
    back = two((spread @ fourier_rows(EZ).T).T)
    back = np.tile(back, (4, 1))
    mat["back"] = np.concatenate([back, back @ az3], axis=1)
    mode, here = np.arange(MODES)[:, None], np.arange(32)[None, :]
    s0 = np.where(here < ny, sine_rows(mode, here, ny), 0.0)
    s1 = np.where(here < ny, sine_rows(mode, here + 1, ny), 0.0)
    mat["sin"] = np.concatenate([s0, s1], axis=0)
    packed, where = [], {}
    at = 0
    for name, value in tile.items():
        where[name] = (at, value.shape[0])
        packed.append(value)
        at += value.shape[0]
    tiles = np.concatenate(packed).astype(np.float32)
    packed, at = [], 0
    for name, value in row.items():
        where[name] = (at, value.shape[0])
        packed.append(value)
        at += value.shape[0]
    row16 = np.concatenate(packed).astype(np.float32)
    mats = {name: value.astype(np.float32) for name, value in mat.items()}
    return tiles, row16, mats, where


MATS = ("az7", "down", "pick", "lown", "az3", "b12", "sin", "back", "kt", "tt", "lxy", "lines", "up", "upt",
        "fine", "pfine")
N_LINKS = 20 + 4 + 20 + 4 + 12 + 24 + 4


def reach(n):
    base = max(n // 8, 1)
    known, hops = base, []
    while known < n // 2:
        hops.append(known)
        known *= 2
    return range(1, base + 1), hops


def kernel(nx, ny, where, *refs):
    names = ("x", "tiles", "rows") + MATS
    count = len(names)
    hbm, out_ref, vmem = refs[:count], refs[count], refs[count + 1 : 2 * count + 1]
    (pair_send, pair_recv, edge_send, corner_recv, twice_recv, knight_send, knight_recv, g3_all,
     fine_send, fine_recv, mid_send, mid_recv, line_send, line_recv, mode_send, mode_recv,
     rest3_all, x3_all, rest7_all, load_sem, send_sem, recv_sem, line_ss, line_rs, mode_ss, mode_rs, known) = refs[2 * count + 1 :]
    sx, cx = lax.axis_index("stream"), lax.axis_index("cross")
    tile_ref, row_ref = vmem[1], vmem[2]
    mat = dict(zip(MATS, vmem[3:]))

    def at(dx, dy):
        return {"stream": lax.rem(sx + (nx + dx), nx), "cross": lax.rem(cx + (ny + dy), ny)}

    def tab(name):
        start, size = where[name]
        return tile_ref[start : start + size]

    def rtab(name):
        start, size = where[name]
        return row_ref[start : start + size]

    bar = pltpu.get_barrier_semaphore()
    faces = FACES
    near_x, hops_x = reach(nx)
    near_y, hops_y = reach(ny)
    near = [(s * d, 0) for d in near_x for s in (1, -1)]
    near += [(0, s * d) for d in near_y for s in (1, -1)]
    near += CORNERS + KNIGHTS
    for d in near:
        pl.semaphore_signal(bar, inc=1, device_id=at(*d), device_id_type=MESH_ID)
    loads = {}
    for n, name in enumerate(names):
        loads[name] = pltpu.make_async_copy(hbm[n], vmem[n], load_sem.at[n])
        loads[name].start()

    def need(*wanted):
        for name in wanted:
            if name in loads:
                loads.pop(name).wait()

    def tell(step):
        for n, hops in enumerate((hops_x, hops_y)):
            if step < len(hops):
                for s in (1, -1):
                    d = (s * hops[step], 0) if n == 0 else (0, s * hops[step])
                    pl.semaphore_signal(
                        known.at[step, n], inc=1, device_id=at(*d), device_id_type=MESH_ID)

    def told(step):
        for n, hops in enumerate((hops_x, hops_y)):
            if step < len(hops):
                pl.semaphore_wait(known.at[step, n], 2)

    links = [0]
    sent = []

    def start(src, dst, to):
        n = links[0]
        links[0] += 1
        copy = pltpu.make_async_remote_copy(
            src, dst, send_sem.at[n], recv_sem.at[n], device_id=at(*to), device_id_type=MESH_ID)
        copy.start()
        sent.append(copy)
        return copy

    jrow = lax.broadcasted_iota(jnp.int32, (8, LANES), 0)
    lane = lax.broadcasted_iota(jnp.int32, (8, LANES), 1)
    low_wall = jnp.where(cx == 0, 0, -1)
    high_wall = jnp.where(cx == ny - 1, ORDER, -1)
    keep7 = jnp.where((jrow == low_wall) | (jrow == high_wall), 0.0, 1.0)
    mrow = lax.broadcasted_iota(jnp.int32, (16, LANES), 0)
    brow = lax.rem(mrow, 4)
    high_wall3 = jnp.where(cx == ny - 1, MID_ORDER, -1)
    keep3 = jnp.where((brow == low_wall) | (brow == high_wall3), 0.0, 1.0)
    _, keep_f, gain_f = smoother(ORDER)
    _, keep_m, gain_m = smoother(MID_ORDER)

    def halves(a):
        top = a.astype(jnp.bfloat16)
        return top, (a - top.astype(jnp.float32)).astype(jnp.bfloat16)

    def dot(a, b):
        (a1, a2), (b1, b2) = halves(a), halves(b)
        parts = [jnp.dot(x, y, preferred_element_type=jnp.float32)
                 for x, y in ((a1, b2), (a2, b1), (a1, b1))]
        return parts[0] + parts[1] + parts[2]

    def fine_xy(u):
        kx = tab("kx").reshape(8, 8, 8, LANES)
        ax = kx[0][None] * u[:, 0:1]
        for a in range(1, 8):
            ax = ax + kx[a][None] * u[:, a : a + 1]
        ky = tab("ky")
        flat = u.reshape(16, 8, LANES)
        ay = ky[0][None] * flat
        for s in range(1, 8):
            ay = ay + ky[s][None] * pltpu.roll(flat, s, 1)
        return ax, ay.reshape(2, 8, 8, LANES) * tab("ti")[None]

    def fine_z(u):
        az = dot(u.reshape(128, LANES), mat["az7"][...])
        return az.reshape(2, 8, 8, LANES) * tab("tij")[None]

    def fine_send_faces(ax, ay):
        fine_send[0] = ax[:, 7].reshape(16, LANES)
        fine_send[1] = ax[:, 0].reshape(16, LANES)
        flat = ay.reshape(16, 8, LANES)
        fine_send[2] = flat[:, 7, :]
        fine_send[3] = flat[:, 0, :]
        return [start(fine_send.at[d], fine_recv.at[d], faces[d]) for d in range(4)]

    def add_x(field, low, high):
        return jnp.concatenate(
            [field[:, 0:1] + low.reshape(2, 1, 8, LANES), field[:, 1:7],
             field[:, 7:8] + high.reshape(2, 1, 8, LANES)], axis=1)

    def add_y(field, low, high):
        flat = field.reshape(16, 8, LANES)
        flat = flat + jnp.where(jrow[None] == 0, low[:, None, :], 0.0)
        flat = flat + jnp.where(jrow[None] == 7, high[:, None, :], 0.0)
        return flat.reshape(2, 8, 8, LANES)

    def fine_join(copies, field):
        for copy in copies:
            copy.wait_recv()
        field = add_x(field, fine_recv[0], fine_recv[1])
        return add_y(field, fine_recv[2], fine_recv[3])

    def left(name, v):
        start_row, size = where[name]
        acc = row_ref[start_row] * v[0:1]
        for c in range(1, size):
            acc = acc + row_ref[start_row + c] * v[c : c + 1]
        return acc

    def mid_start(ax, ay):
        mid_send[0] = ax
        mid_send[1] = ay
        return [start(mid_send.at[d // 2], mid_recv.at[d], faces[d]) for d in range(4)]

    def shifted(v, shift, mask):
        return jnp.where(mask, pltpu.roll(v, shift, 0), 0.0)

    def mid_join(copies, field):
        for copy in copies:
            copy.wait_recv()
        field = field + shifted(mid_recv[0], 4, mrow < 4)
        field = field + shifted(mid_recv[1], 12, mrow >= 12)
        field = field + shifted(mid_recv[2], 13, brow == 0)
        return field + shifted(mid_recv[3], 3, brow == 3)

    def masked(dy, table, top, index):
        low = jnp.where(cx + dy == 0, 0, -1)
        high = jnp.where(cx + dy == ny - 1, top, -1)
        return table * jnp.where((index == low) | (index == high), 0.0, 1.0)

    def along_x(u, row):
        acc = kx[0][row][None] * u[:, 0]
        for a in range(1, 8):
            acc = acc + kx[a][row][None] * u[:, a]
        return acc.reshape(16, LANES)

    def along_y(u, table):
        weighted = jnp.sum(table[None] * u, axis=2)
        return (tab("ti")[:, 0][None] * weighted).reshape(16, LANES)

    need("x")
    src = vmem[0][...].reshape(16, 8, LANES)
    knode = lax.rem(lane, 8)
    src = (src + jnp.where(knode[None] == 7, pltpu.roll(src, LANES - 1, 2), 0.0)
           + jnp.where(knode[None] == 0, pltpu.roll(src, 1, 2), 0.0))
    y7, y0 = src[:, 7, :], src[:, 0, :]
    src = src.reshape(2, 8, 8, LANES)
    x7, x0 = src[:, 7].reshape(16, LANES), src[:, 0].reshape(16, LANES)
    for n, edge in enumerate((x7, y7, x0, y0, x7)):
        edge_send[n] = edge
    for i, row in ((1, 7), (0, 0)):
        for j, line in ((1, y7), (0, y0)):
            knight_send[2 * i + j] = line.reshape(2, 8, LANES)[:, row : row + 1]
    need("tiles")
    e7 = masked(0, tab("e7"), ORDER, jrow[None])
    kx = tab("kx").reshape(8, 8, 8, LANES)
    ky_last, ky_first = tab("kyl"), tab("kyf")
    scaled = e7[None] * src
    pairs = ((x0, along_x(scaled, 0)), (x7, along_x(scaled, 7)),
             (y0, along_y(scaled, ky_first)), (y7, along_y(scaled, ky_last)))
    for n, (raw, contracted) in enumerate(pairs):
        pair_send[n, 0] = raw
        pair_send[n, 1] = contracted
    pl.semaphore_wait(bar, len(near))
    tell(0)
    copies = [start(knight_send.at[2 * (dx < 0) + (dy < 0)], knight_recv.at[n], (-dx, -dy))
              for n, (dx, dy) in enumerate(KNIGHTS)]
    pick_edge = {(1, 1): 2, (1, -1): 1, (-1, 1): 3, (-1, -1): 0}
    copies += [start(edge_send.at[pick_edge[d] : pick_edge[d] + 2], corner_recv.at[n],
                     (-d[0], -d[1])) for n, d in enumerate(CORNERS)]
    copies += [start(edge_send.at[(2, 0, 3, 1)[n]], twice_recv.at[n], (-dx, -dy))
               for n, (dx, dy) in enumerate(TWICE)]
    copies += [start(pair_send.at[n], pair_recv.at[n], (-dx, -dy))
               for n, (dx, dy) in enumerate(FACES)]
    need("az7")
    for copy in copies:
        copy.wait_recv()
    told(0)
    tell(1)
    irow = jrow[None]

    def lines_of(value):
        return value.reshape(2, 8, LANES)

    def row_of(value, row):
        return lines_of(value)[:, row : row + 1]

    def with_ends(line, first, last):
        line = lines_of(line) + jnp.where(irow == 0, first, 0.0) + jnp.where(irow == 7, last, 0.0)
        return line.reshape(16, LANES)

    knight = {d: knight_recv[n] for n, d in enumerate(KNIGHTS)}
    twice = {d: twice_recv[n] for n, d in enumerate(TWICE)}
    raw = {d: pair_recv[n, 0] for n, d in enumerate(FACES)}
    corner_x = {d: corner_recv[n, 0 if d[0] == d[1] else 1] for n, d in enumerate(CORNERS)}
    corner_y = {d: corner_recv[n, 1 if d[0] == d[1] else 0] for n, d in enumerate(CORNERS)}

    def joined(center, low_x, high_x, low_y, high_y):
        return add_y(add_x(center, low_x, high_x), low_y, high_y)

    b7 = joined(
        src, raw[-1, 0], raw[1, 0],
        with_ends(raw[0, -1], row_of(corner_y[-1, -1], 7), row_of(corner_y[1, -1], 0)),
        with_ends(raw[0, 1], row_of(corner_y[-1, 1], 7), row_of(corner_y[1, 1], 0)))
    zero = jnp.zeros_like(src)
    extra = {
        (1, 0): joined(
            zero, x7, twice[2, 0],
            with_ends(corner_y[1, -1], row_of(raw[0, -1], 7), knight[2, -1]),
            with_ends(corner_y[1, 1], row_of(raw[0, 1], 7), knight[2, 1])),
        (-1, 0): joined(
            zero, twice[-2, 0], x0,
            with_ends(corner_y[-1, -1], knight[-2, -1], row_of(raw[0, -1], 0)),
            with_ends(corner_y[-1, 1], knight[-2, 1], row_of(raw[0, 1], 0))),
        (0, 1): joined(
            zero, corner_x[-1, 1], corner_x[1, 1],
            with_ends(y7, row_of(raw[-1, 0], 7), row_of(raw[1, 0], 7)),
            with_ends(twice[0, 2], knight[-1, 2], knight[1, 2])),
        (0, -1): joined(
            zero, corner_x[-1, -1], corner_x[1, -1],
            with_ends(twice[0, -2], knight[-1, -2], knight[1, -2]),
            with_ends(y0, row_of(raw[-1, 0], 0), row_of(raw[1, 0], 0))),
    }
    extra = {d: masked(d[1], tab("e7"), ORDER, jrow[None])[None] * v for d, v in extra.items()}

    u1 = e7[None] * b7
    ax, ay = fine_xy(u1)
    au = add_x(ax + ay + fine_z(u1), pair_recv[1, 1] + along_x(extra[-1, 0], 7),
               pair_recv[0, 1] + along_x(extra[1, 0], 0))
    au = add_y(au, pair_recv[3, 1] + along_y(extra[0, -1], ky_last),
               pair_recv[2, 1] + along_y(extra[0, 1], ky_first))
    r1 = b7 - au
    x7 = (1.0 + keep_f) * u1 + gain_f * (e7[None] * r1)
    ax, ay = fine_xy(x7)
    side7 = fine_send_faces(ax, ay)
    az = fine_z(x7)
    local7 = ax + ay + az
    ci = tab("ci")[None]
    rest7 = (src - tab("cj")[None] * (ax + ci * az) - ci * ay) * keep7[None, None]
    need("rows", "down")
    jx = tab("jx").reshape(8, 4, 8, LANES)
    g = jx[0][None] * rest7[:, 0:1]
    for i in range(1, 8):
        g = g + jx[i][None] * rest7[:, i : i + 1]
    g = jnp.concatenate([g[0].reshape(32, LANES), g[1].reshape(32, LANES)], axis=1)
    g3 = left("jy", dot(g, mat["down"][...]))
    g3_all[0] = g3
    copies = [start(g3_all.at[0], g3_all.at[n], (-dx, -dy))
              for n, (dx, dy) in enumerate(AROUND) if n]
    rest7_all[0] = (b7 - fine_join(side7, local7)).reshape(128, LANES)
    need("az3", "b12", "pick", "lown")
    told(1)
    ring1, ring2, ring3 = offsets(1), offsets(2), offsets(3)
    e3 = {dy: masked(dy, rtab("e3")[0], MID_ORDER, brow) for dy in range(-3, 4)}
    e3_all = jnp.concatenate([e3[dy] for _, dy in ring3], axis=0)
    tc, tab3 = rtab("tc")[0], rtab("tab")[0]
    n1, n2, n3 = 16 * len(ring1), 16 * len(ring2), 16 * len(ring3)

    def mid_z(v):
        return tab3 * dot(v, mat["az3"][...])

    for copy in copies:
        copy.wait_recv()

    b3 = dot(mat["pick"][...], g3_all[...].reshape(16 * len(AROUND), LANES))
    v1 = e3_all[:n1] * b3
    b3, e3 = b3[:16], e3[0]
    r1 = b3 - tc * dot(mat["lown"][...], v1) - mid_z(v1[:16])
    x3 = (1.0 + keep_m) * v1[:16] + gain_m * (e3 * r1)
    ax, ay = left("lx", x3), left("ly", x3)
    ca, cb = rtab("ca")[0], rtab("cb")[0]
    part = keep3 * (g3 - cb * ax - ca * ay)
    other = keep3 * (ca * cb * tab3) * x3
    line = dot(jnp.concatenate([part, -other], axis=1), mat["b12"][...])
    line = jnp.sum(rtab("jj")[0] * line, axis=0, keepdims=True)
    line_send[0] = line

    def line_copy(d, slot, to):
        return pltpu.make_async_remote_copy(
            line_send.at[0], line_recv.at[slot], line_ss.at[d], line_rs.at[d],
            device_id={"cross": to}, device_id_type=MESH_ID)

    def far_first(n, size):
        step = lax.div(n + 1, 2)
        return size // 2 + step * (1 - 2 * lax.rem(n, 2))

    def line_out(n, carry):
        d = far_first(n, ny)
        line_copy(d, cx, lax.rem(cx + d, ny)).start()
        return carry

    lax.fori_loop(0, ny - 1, line_out, 0)
    line_recv[cx] = line
    side3 = mid_start(ax, ay)
    x3_all[0] = x3
    side = [start(x3_all.at[0], x3_all.at[n], (-dx, -dy))
            for n, (dx, dy) in enumerate(ring2) if n]
    side += [start(rest7_all.at[0], rest7_all.at[n], (-dx, -dy))
             for n, (dx, dy) in enumerate(ring1) if n]
    if ny < 32:
        line_recv[ny:] = jnp.zeros((32 - ny, 1, LANES), jnp.float32)
    rest3_all[0] = b3 - mid_join(side3, ax + ay + mid_z(x3))
    side += [start(rest3_all.at[0], rest3_all.at[n], (-dx, -dy))
             for n, (dx, dy) in enumerate(ring3) if n]
    need("sin")

    def line_in(d, carry):
        line_copy(d, lax.rem(cx + ny - d, ny), cx).wait()
        return carry

    lax.fori_loop(1, ny, line_in, 0)
    spectrum = dot(mat["sin"][...], line_recv[:, 0, :])
    group = lax.div(lane, 32)
    for alpha in range(2):
        total = jnp.zeros((8, LANES), jnp.float32)
        for hi in range(4):
            for beta in range(2):
                piece = spectrum[(beta * 4 + hi) * 8 : (beta * 4 + hi + 1) * 8]
                shift = 32 * (hi - 2 * alpha - beta) % LANES
                if shift:
                    piece = pltpu.roll(piece, shift, 1)
                total = total + jnp.where(group == hi, piece, 0.0)
        mode_send[alpha] = total

    def mode_copy(d, to):
        return pltpu.make_async_remote_copy(
            mode_send, mode_recv.at[d], mode_ss.at[d], mode_rs.at[d],
            device_id={"stream": to}, device_id_type=MESH_ID)

    def mode_out(n, carry):
        d = far_first(n, nx)
        mode_copy(d, lax.rem(sx + d, nx)).start()
        return carry

    def mode_in(d, carry):
        mode_copy(d, sx).wait()
        return carry

    lax.fori_loop(0, nx - 1, mode_out, 0)
    mode_recv[0] = mode_send[...]
    lax.fori_loop(1, nx, mode_in, 0)
    first = mode_recv[:, 0]
    second = mode_recv[:, 1]
    nodes = first + jnp.concatenate([second[1:], second[:1]], axis=0)
    start_g = where["green"][0]
    solved = [jnp.sum(tile_ref[start_g + n : start_g + n + nx] * nodes, axis=0)
              for n in range(SPAN)]
    sine = tile_ref[pl.ds(where["sine"][0] + cx, PAD)]
    window = [jnp.sum(sine * s[None], axis=1) for s in solved]
    window = jnp.concatenate(window, axis=0)
    need(*MATS)
    window = dot(window, mat["back"][...])
    zval, zstiff = window[:, :LANES], window[:, LANES:]

    for copy in side:
        copy.wait_recv()

    def per(table, count):
        return jnp.concatenate([table] * count, axis=0)

    from_low = dot(mat["kt"][...], zval)
    r0 = rest3_all[...].reshape(n3, LANES) - per(tc, len(ring3)) * from_low[:n3]
    r0 = r0 - dot(mat["tt"][...], zstiff)
    w1 = e3_all * r0
    aw = per(tc, len(ring2)) * dot(mat["lxy"][...], w1)
    aw = aw + per(tab3, len(ring2)) * dot(w1[:n2], mat["az3"][...])
    x3 = x3_all[...].reshape(n2, LANES) + from_low[n3:]
    x3 = x3 + (1.0 + keep_m) * w1[:n2] + gain_m * (e3_all[:n2] * (r0[:n2] - aw))

    lines = dot(dot(mat["lines"][...], x3), mat["upt"][:, : 2 * LANES])
    mine = dot(x3[:n1], mat["upt"][...])
    px = dot(x3[:16], mat["up"][...])
    px = jnp.stack([dot(mat["pfine"][...], px[:, r * LANES : (r + 1) * LANES]) for r in range(2)])
    px = px.reshape(2, 8, 8, LANES)
    columns = []
    for n in range(len(ring1)):
        for r in range(2):
            at_n, at_r = slice(16 * n, 16 * n + 16), slice(r * LANES, (r + 1) * LANES)
            also = slice((2 + r) * LANES, (3 + r) * LANES)
            columns.append(jnp.concatenate(
                [mine[at_n, at_r], lines[at_n, at_r], mine[at_n, also]], axis=0))
    apx = dot(mat["fine"][...], jnp.concatenate(columns, axis=1))
    r0, u1 = [], []
    for n, (dx, dy) in enumerate(ring1):
        moved = jnp.stack([apx[:, (2 * n + r) * LANES : (2 * n + r + 1) * LANES] for r in range(2)])
        r0.append(rest7_all[n].reshape(2, 8, 8, LANES) - moved.reshape(2, 8, 8, LANES))
        scale = masked(dy, tab("e7"), ORDER, jrow[None]) if dy else e7
        u1.append(scale[None] * r0[n])

    ax, ay = fine_xy(u1[0])
    au = ax + ay + fine_z(u1[0])
    au = add_x(au, along_x(u1[2], 7), along_x(u1[1], 0))
    au = add_y(au, along_y(u1[4], ky_last), along_y(u1[3], ky_first))
    x7 = x7 + px
    out = x7 + (1.0 + keep_f) * u1[0] + gain_f * (e7[None] * (r0[0] - au))
    out_ref[...] = out.reshape(128, LANES)
    for copy in sent:
        copy.wait_send()


def solution(mesh):
    nx, ny = mesh.shape["stream"], mesh.shape["cross"]
    tiles, row16, mats, where = build_tables(nx, ny)

    def body(sources):
        flat = sources.reshape(128, LANES)
        operands = [flat, jnp.asarray(tiles), jnp.asarray(row16)]
        operands += [jnp.asarray(mats[name]) for name in MATS]
        links, f32 = pltpu.SemaphoreType.DMA, jnp.float32
        out = pl.pallas_call(
            functools.partial(kernel, nx, ny, where),
            out_shape=jax.ShapeDtypeStruct((128, LANES), jnp.float32),
            in_specs=[pl.BlockSpec(memory_space=pl.ANY)] * len(operands),
            out_specs=pl.BlockSpec(memory_space=pltpu.VMEM),
            scratch_shapes=[pltpu.VMEM(o.shape, f32) for o in operands]
            + [
                pltpu.VMEM((4, 2, 16, LANES), f32),
                pltpu.VMEM((4, 2, 16, LANES), f32),
                pltpu.VMEM((5, 16, LANES), f32),
                pltpu.VMEM((4, 2, 16, LANES), f32),
                pltpu.VMEM((4, 16, LANES), f32),
                pltpu.VMEM((4, 2, 1, LANES), f32),
                pltpu.VMEM((8, 2, 1, LANES), f32),
                pltpu.VMEM((len(AROUND), 16, LANES), f32),
                pltpu.VMEM((4, 16, LANES), f32),
                pltpu.VMEM((4, 16, LANES), f32),
                pltpu.VMEM((2, 16, LANES), f32),
                pltpu.VMEM((4, 16, LANES), f32),
                pltpu.VMEM((1, 1, LANES), f32),
                pltpu.VMEM((32, 1, LANES), f32),
                pltpu.VMEM((2, 8, LANES), f32),
                pltpu.VMEM((nx, 2, 8, LANES), f32),
                pltpu.VMEM((len(offsets(3)), 16, LANES), f32),
                pltpu.VMEM((len(offsets(2)), 16, LANES), f32),
                pltpu.VMEM((len(offsets(1)), 128, LANES), f32),
                links((len(operands),)),
                links((N_LINKS,)),
                links((N_LINKS,)),
                links((ny,)),
                links((ny,)),
                links((nx,)),
                links((nx,)),
                pltpu.SemaphoreType.REGULAR((2, 2)),
            ],
            compiler_params=pltpu.CompilerParams(collective_id=0, has_side_effects=True),
            name="vcycle",
        )(*operands)
        return out.reshape(sources.shape)

    spec = P(None, "stream", "cross", None, None, None)
    return jax.shard_map(body, mesh=mesh, in_specs=(spec,), out_specs=spec, check_vma=False)
```

```python
import functools
import math

import jax
import jax.numpy as jnp
import ml_dtypes
import numpy as np
from jax import lax
from jax.experimental import pallas as pl
from jax.experimental.pallas import tpu as pltpu
from jax.sharding import PartitionSpec as P

ORDER = 7
MID_ORDER = 3
EZ = 16
LANES = 128
MODES = 32
MESH_ID = pl.DeviceIdType.MESH
FACES = ((1, 0), (-1, 0), (0, 1), (0, -1))
CORNERS = ((1, 1), (1, -1), (-1, 1), (-1, -1))
TWICE = ((2, 0), (-2, 0), (0, 2), (0, -2))
KNIGHTS = tuple((s * a, t * b) for a, b in ((2, 1), (1, 2)) for s in (1, -1) for t in (1, -1))
AROUND = ((0, 0),) + FACES + CORNERS + TWICE + KNIGHTS
WIDE, SPAN, PAD = 4, 10, 16


def legendre_pair(degree, points):
    below_poly = np.ones(points.shape)
    top_poly = points.copy()
    for step in range(2, degree + 1):
        below_poly, top_poly = (
            top_poly,
            ((2 * step - 1) * points * top_poly - (step - 1) * below_poly) / step,
        )
    return (below_poly, top_poly)


@functools.lru_cache(None)
def gll_tables(degree):
    nodes = -np.cos(np.pi * np.arange(degree + 1) / degree)
    for _ in range(100):
        below_poly, top_poly = legendre_pair(degree, nodes)
        nodes = nodes - (nodes * top_poly - below_poly) / ((degree + 1) * top_poly)
    at_nodes = legendre_pair(degree, nodes)[1]
    weights = 2.0 / (degree * (degree + 1) * at_nodes**2)
    count = degree + 1
    derivative = np.zeros((count, count))
    for target in range(count):
        for source in range(count):
            if target != source:
                derivative[target, source] = at_nodes[target] / (
                    at_nodes[source] * (nodes[target] - nodes[source])
                )
    derivative[0, 0] = -degree * (degree + 1) / 4.0
    derivative[degree, degree] = degree * (degree + 1) / 4.0
    stiffness = derivative.T @ (weights[:, None] * derivative)
    return (nodes, weights, stiffness)


def lagrange_matrix(fine_degree, coarse_degree):
    fine_nodes = gll_tables(fine_degree)[0]
    coarse_nodes = gll_tables(coarse_degree)[0]
    table = np.ones((fine_degree + 1, coarse_degree + 1))
    for column in range(coarse_degree + 1):
        for other in range(coarse_degree + 1):
            if other != column:
                table[:, column] *= (fine_nodes - coarse_nodes[other]) / (
                    coarse_nodes[column] - coarse_nodes[other]
                )
    return table


@functools.lru_cache(None)
def smoother(degree):
    stiffness = gll_tables(degree)[2]
    elements = 6
    size = elements * degree
    assembled = np.zeros((size, size))
    for element in range(elements):
        for row in range(degree + 1):
            for col in range(degree + 1):
                assembled[(element * degree + row) % size, (element * degree + col) % size] += (
                    stiffness[row, col]
                )
    diagonal = np.sqrt(np.diagonal(assembled))
    scaled = assembled / diagonal[:, None] / diagonal[None, :]
    positions = np.arange(size)
    vector = np.where(positions % 2 == 0, 1.0, -1.0) * (1.0 + positions / size)
    for _ in range(2000):
        vector = scaled @ vector
        vector = vector / np.sqrt(np.sum(vector * vector))
    high = float(np.sum(vector * (scaled @ vector)) / np.sum(vector * vector))
    low = 0.1 * high
    theta, delta = 0.5 * (high + low), 0.5 * (high - low)
    sigma = theta / delta
    rho1 = 1.0 / sigma
    rho2 = 1.0 / (2.0 * sigma - rho1)
    return theta, rho2 * rho1, 2.0 * rho2 / delta * theta


def level(degree):
    _, w, k = gll_tables(degree)
    t = w.copy()
    t[0] = t[-1] = w[0] + w[-1]
    s = np.diagonal(k).copy()
    s[0] = s[-1] = k[0, 0] + k[-1, -1]
    c = np.ones(degree + 1)
    c[0] = c[-1] = 0.5
    diag = (
        s[:, None, None] * t[None, :, None] * t[None, None, :]
        + t[:, None, None] * s[None, :, None] * t[None, None, :]
        + t[:, None, None] * t[None, :, None] * s[None, None, :]
    )
    return w, k, t, c, 1.0 / (diag * smoother(degree)[0])


def join_z(count):
    size = EZ * count
    m = np.eye(size)
    for e in range(EZ):
        a, b = e * count + count - 1, ((e + 1) % EZ) * count
        m[a, b] += 1.0
        m[b, a] += 1.0
    return m


def two(m):
    return np.kron(np.eye(2), m)


def lanes(values):
    return np.broadcast_to(values[None, :], (8, LANES))


def rows(values):
    return np.broadcast_to(np.asarray(values)[..., None], np.shape(values) + (LANES,))


def fourier_rows(total):
    k, n = np.meshgrid(np.arange(total), np.arange(total), indexing="ij")
    half = total // 2
    freq = np.where(k <= half, k, k - half)
    angle = 2.0 * np.pi * (freq * n % total) / total
    scale = np.where((k == 0) | (k == half), math.sqrt(1.0 / total), math.sqrt(2.0 / total))
    return scale * np.where(k <= half, np.cos(angle), np.sin(angle))


def sine_rows(mode, point, total):
    product = mode * point % (2 * total)
    inside = (mode > 0) & (mode < total) & (point > 0) & (point < total)
    return np.where(inside, math.sqrt(2.0 / total) * np.sin(np.pi * product / total), 0.0)


def green_table(nx, ny):
    mode = np.arange(MODES)
    wall_gap = 2.0 * np.sin(0.5 * np.pi * mode / ny) ** 2 + np.where(mode % ny == 0, 1.0, 0.0)
    freq = np.arange(EZ)
    freq = np.where(freq <= EZ // 2, freq, freq - EZ // 2)
    span_gap = 2.0 * np.sin(np.pi * freq / EZ) ** 2
    half_gap = wall_gap[:, None] + span_gap[None, :]
    root = np.sqrt(half_gap * (2.0 + half_gap))
    rate = np.log1p(half_gap + root)
    d = np.arange(nx)[:, None, None]
    top = np.exp(-rate * d) + np.exp(-rate * (nx - d))
    return top / (4.0 * root * -np.expm1(-rate * nx))


def modal(values):
    v = values.reshape(values.shape[:-2] + (MODES // 8, 8, EZ))
    v = np.stack([v, v], axis=-2)
    v = np.moveaxis(v, -4, -3)
    return v.reshape(v.shape[:-3] + (LANES,))


def offsets(radius):
    found = [(0, 0), *FACES]
    for ring in range(2, radius + 1):
        found += [
            (dx, dy)
            for dx in range(-ring, ring + 1)
            for dy in range(-ring, ring + 1)
            if abs(dx) + abs(dy) == ring
        ]
    return found


def assembled_1d(local_cols, window):
    count = local_cols.shape[0]
    out = np.zeros((count, window))
    out[:, 1:3] += local_cols
    out[0, 0:2] += local_cols[-1]
    out[-1, 2:4] += local_cols[0]
    return out


@functools.lru_cache(None)
def build_tables(nx, ny):
    f, q = ORDER + 1, MID_ORDER + 1
    w7, k7, t7, c7, e7 = level(ORDER)
    w3, k3, t3, c3, e3 = level(MID_ORDER)
    j73 = lagrange_matrix(ORDER, MID_ORDER)
    j31 = lagrange_matrix(MID_ORDER, 1)
    tile = {}
    tk = np.tile(t7, EZ)
    ones = np.ones((8, LANES))
    tile["kx"] = np.stack(
        [np.stack([k7[i, a] * t7[:, None] * tk[None, :] for i in range(f)]) for a in range(f)]
    ).reshape(f * f, 8, LANES)
    roll = np.stack([[k7[j, (j - s) % f] for j in range(f)] for s in range(f)])
    tile["ky"] = roll[:, :, None] * tk[None, None, :]
    tile["kyl"] = (k7[f - 1][:, None] * tk[None, :])[None]
    tile["kyf"] = (k7[0][:, None] * tk[None, :])[None]
    tile["e7"] = np.tile(e7, (1, 1, EZ))
    tile["ti"] = np.stack([t * ones for t in t7])
    tile["tij"] = np.stack([t * rows(t7) for t in t7])
    tile["cj"] = rows(c7)[None]
    tile["ci"] = np.stack([c * ones for c in c7])
    tile["jx"] = np.stack([j73[i, a] * ones for i in range(f) for a in range(q)])
    green = modal(green_table(nx, ny))
    tile["green"] = green[(np.arange(nx + SPAN - 1) - WIDE) % nx]
    point = np.arange(-WIDE, ny - WIDE + PAD)
    tile["sine"] = modal(
        np.broadcast_to(
            sine_rows(np.arange(MODES)[None, :], point[:, None], ny)[:, :, None],
            (len(point), MODES, EZ),
        )
    )
    row = {}
    mid = [(a, b) for a in range(q) for b in range(q)]
    tc = np.tile(np.tile(t3, EZ), 2)

    def left(matrix, scale=None):
        scale = np.ones(LANES) if scale is None else scale
        return matrix.T[:, :, None] * scale[None, None, :]

    row["jy"] = left(
        np.array([[(a == a2) * j73[j, b] for a2 in range(q) for j in range(f)] for a, b in mid])
    )
    row["lx"] = left(np.kron(k3, np.diag(t3)), tc)
    row["ly"] = left(np.kron(np.diag(t3), k3), tc)
    row["e3"] = np.stack([np.tile(np.tile(e3[a, b], EZ), 2) for a, b in mid])[None]
    row["tab"] = rows([t3[a] * t3[b] for a, b in mid])[None]
    row["ca"] = rows([c3[a] for a, b in mid])[None]
    row["cb"] = rows([c3[b] for a, b in mid])[None]
    groups = [np.array([j31[a, x] * j31[b, y] for a, b in mid]) for x in (0, 1) for y in (0, 1)]
    row["jj"] = np.repeat(np.stack(groups, axis=1), MODES, axis=1)[None]
    own = np.zeros((q, 4))
    own[:, 1:3] = j31
    stiff = assembled_1d(k3 @ j31, 4)
    mass = t3[:, None] * own

    ring1, ring2, ring3 = offsets(1), offsets(2), offsets(3)

    def placed(first, second, elements):
        out = np.zeros((len(elements), q, q, SPAN, PAD))
        for n, (dx, dy) in enumerate(elements):
            x0, y0 = dx - 1 + WIDE, dy - 1 + WIDE
            out[n, :, :, x0 : x0 + 4, y0 : y0 + 4] = np.einsum("at,bq->abtq", first, second)
        return out.reshape(len(elements) * q * q, SPAN * PAD)

    mat = {}
    mat["kt"] = np.concatenate(
        [placed(stiff, mass, ring3) + placed(mass, stiff, ring3), placed(own, own, ring2)])
    mat["tt"] = placed(mass, mass, ring3)
    cross = np.zeros((len(ring2), q, q, len(ring3), q, q))
    ends = {(1, 0): (3, 0), (-1, 0): (0, 3), (0, 1): (3, 0), (0, -1): (0, 3)}
    diag3 = np.diag(t3)
    for n, (dx, dy) in enumerate(ring2):
        cross[n, :, :, n] += np.einsum("ac,bd->abcd", k3, diag3)
        cross[n, :, :, n] += np.einsum("ac,bd->abcd", diag3, k3)
        for (fx, fy), (mine, theirs) in ends.items():
            m = ring3.index((dx + fx, dy + fy))
            line = np.zeros((q, q))
            line[mine] = k3[theirs]
            if fx:
                cross[n, :, :, m] += np.einsum("ac,bd->abcd", line, diag3)
            else:
                cross[n, :, :, m] += np.einsum("ac,bd->abcd", diag3, line)
    pick = np.zeros((len(ring1), q, q, len(AROUND), q, q))
    for n, (dx, dy) in enumerate(ring1):
        for m, (gx, gy) in enumerate(AROUND):
            sx, sy = gx - dx, gy - dy
            if max(abs(sx), abs(sy)) > 1:
                continue
            span_x = [(a, a) for a in range(q)] if sx == 0 else [(q - 1, 0) if sx > 0 else (0, q - 1)]
            span_y = [(b, b) for b in range(q)] if sy == 0 else [(q - 1, 0) if sy > 0 else (0, q - 1)]
            for a, a2 in span_x:
                for b, b2 in span_y:
                    pick[n, a, b, m, a2, b2] = 1.0
    mat["pick"] = pick.reshape(len(ring1) * 16, len(AROUND) * 16)
    mat["lxy"] = cross.reshape(len(ring2) * 16, len(ring3) * 16)
    k7j = k7 @ j73
    t7j = t7[:, None] * j73
    fine = np.zeros((len(ring1), f, f, len(ring2), q, q))
    own_z = np.zeros((len(ring1), f, f, len(ring1), q, q))
    for n, (dx, dy) in enumerate(ring1):
        fine[n, :, :, n] += np.einsum("ia,jb->ijab", k7j, t7j) + np.einsum("ia,jb->ijab", t7j, k7j)
        own_z[n, :, :, n] = np.einsum("ia,jb->ijab", t7j, t7j)
        for (fx, fy), (mine, theirs) in ends.items():
            mine, theirs = (f - 1 if mine else 0), (f - 1 if theirs else 0)
            m = ring2.index((dx + fx, dy + fy))
            if fx:
                fine[n, mine, :, m] += np.einsum("a,jb->jab", k7j[theirs], t7j)
            else:
                fine[n, :, mine, m] += np.einsum("ia,b->iab", t7j, k7j[theirs])
    count = len(ring1) * f * f
    mat["fine"] = np.concatenate([fine.reshape(count, -1), own_z.reshape(count, -1)], axis=1)
    mat["lown"] = mat["lxy"][:16, : 16 * len(ring1)]
    mat["pfine"] = np.einsum("ia,jb->ijab", j73, j73).reshape(f * f, 16)
    row["tc"] = np.broadcast_to(tc, (1, 16, LANES))
    az7 = (join_z(f) @ np.kron(np.eye(EZ), k7)).T
    az3 = two((join_z(q) @ np.kron(np.eye(EZ), k3)).T)
    down = (join_z(q) @ np.kron(np.eye(EZ), j73.T) @ np.diag(np.tile(c7, EZ))).T
    zero = np.zeros_like(down)
    mat["az7"] = az7
    mat["down"] = np.concatenate(
        [np.concatenate([down, zero], axis=1), np.concatenate([zero, down], axis=1)], axis=0
    )
    mat["az3"] = az3
    up = np.kron(np.eye(EZ), j73).T
    mat["up"] = two(up)
    up_tk = up * np.tile(t7, EZ)[None]
    mat["upt"] = np.concatenate([two(up_tk), two(up @ az7)], axis=1)
    gather = np.zeros((EZ, EZ * q))
    for e in range(EZ):
        for node in (0, 1):
            gather[(e + node) % EZ, e * q : (e + 1) * q] += j31[:, node] * c3
    b1 = two((fourier_rows(EZ) @ gather).T)
    b1 = np.tile(b1, (1, 4))
    mat["b12"] = np.concatenate([b1, az3 @ b1], axis=0)
    spread = np.zeros((EZ * q, EZ))
    for e in range(EZ):
        for node in (0, 1):
            spread[e * q : (e + 1) * q, (e + node) % EZ] += j31[:, node]
    back = two((spread @ fourier_rows(EZ).T).T)
    back = np.tile(back, (4, 1))
    mat["back"] = np.concatenate([back, back @ az3], axis=1)
    mode, here = np.arange(MODES)[:, None], np.arange(32)[None, :]
    s0 = np.where(here < ny, sine_rows(mode, here, ny), 0.0)
    s1 = np.where(here < ny, sine_rows(mode, here + 1, ny), 0.0)
    mat["sin"] = np.concatenate([s0, s1], axis=0)
    where, tiles = {}, []
    for names in EARLY, LATE:
        packed, start = [], 0
        for name in names:
            where[name] = (start, tile[name].shape[0])
            packed.append(tile[name])
            start += tile[name].shape[0]
        tiles.append(np.concatenate(packed).astype(np.float32))
    packed, start = [], 0
    for name, value in row.items():
        where[name] = (start, value.shape[0])
        packed.append(value)
        start += value.shape[0]
    row16 = np.concatenate(packed).astype(np.float32)
    mats = []
    for name in MATS:
        value = mat[name].astype(np.float32)
        top = value.astype(ml_dtypes.bfloat16)
        rest = (value - top.astype(np.float32)).astype(ml_dtypes.bfloat16)
        parts = [top, top] if name == "pick" else [top, rest, top]
        mats.append(np.concatenate(parts, axis=0 if name in RIGHT else 1))
    return (*tiles, row16, *mats), where


EARLY = ("e7", "kx", "kyl", "kyf", "ti", "ky", "tij")
LATE = ("cj", "ci", "jx", "green", "sine")
RIGHT = ("az7", "down", "az3", "b12", "back", "up", "upt")
MATS = ("az7", "down", "pick", "lown", "az3", "b12", "sin", "back", "kt", "tt", "lxy", "up", "upt",
        "fine", "pfine")
LINKS = 20 + 4 + 20 + 4 + 12 + 4 + 24


def reach(n):
    base = max(n // 8, 1)
    known, hops = base, []
    while known < n // 2:
        hops.append(known)
        known *= 2
    return range(1, base + 1), hops


def kernel(nx, ny, where, *refs):
    names = ("x", "early", "late", "rows") + MATS
    count = len(names)
    hbm, out_ref, vmem = refs[:count], refs[count], refs[count + 1 : 2 * count + 1]
    (pair_send, pair_recv, edge_send, corner_recv, twice_recv, knight_send, knight_recv, g3_all,
     fine_send, fine_recv, mid_send, mid_recv, line_send, line_recv, mode_send, mode_recv,
     rest3_all, x3_all, rest7_all, load_sem, send_sem, recv_sem, known) = refs[2 * count + 1 :]
    sx, cx = lax.axis_index("stream"), lax.axis_index("cross")
    early_ref, late_ref, row_ref = vmem[1:4]
    mat = dict(zip(MATS, vmem[4:]))

    def at(dx, dy):
        return {"stream": lax.rem(sx + (nx + dx), nx), "cross": lax.rem(cx + (ny + dy), ny)}

    def tab(name):
        start, size = where[name]
        return (early_ref if name in EARLY else late_ref)[start : start + size]

    def rtab(name):
        start, size = where[name]
        return row_ref[start : start + size]

    bar = pltpu.get_barrier_semaphore()
    faces = FACES
    near_x, hops_x = reach(nx)
    near_y, hops_y = reach(ny)
    near = [(s * d, 0) for d in near_x for s in (1, -1)]
    near += [(0, s * d) for d in near_y for s in (1, -1)]
    near += CORNERS + KNIGHTS
    for d in near:
        pl.semaphore_signal(bar, inc=1, device_id=at(*d), device_id_type=MESH_ID)
    loads = {}

    def load(first, last):
        for n in range(first, last):
            copy = pltpu.make_async_copy(hbm[n], vmem[n], load_sem.at[n])
            copy.start()
            loads[names[n]] = copy

    load(0, 2)

    def need(*wanted):
        for name in wanted:
            if name in loads:
                loads.pop(name).wait()

    def tell(step):
        for n, hops in enumerate((hops_x, hops_y)):
            if step < len(hops):
                for s in (1, -1):
                    d = (s * hops[step], 0) if n == 0 else (0, s * hops[step])
                    pl.semaphore_signal(
                        known.at[step, n], inc=1, device_id=at(*d), device_id_type=MESH_ID)

    def told(step):
        for n, hops in enumerate((hops_x, hops_y)):
            if step < len(hops):
                pl.semaphore_wait(known.at[step, n], 2)

    used = [0]

    class Group:
        def __init__(self, size):
            self.base, self.copies = used[0], []
            used[0] += size

        def make(self, n, src, dst, device):
            return pltpu.make_async_remote_copy(
                src, dst, send_sem.at[self.base + n], recv_sem.at[self.base + n],
                device_id=device, device_id_type=MESH_ID)

        def start(self, src, dst, to):
            copy = self.make(len(self.copies), src, dst, at(*to))
            copy.start()
            self.copies.append(copy)

        def arrived(self):
            for copy in self.copies:
                copy.wait_recv()

        def left(self):
            for copy in self.copies:
                copy.wait_send()

    jrow = lax.broadcasted_iota(jnp.int32, (8, LANES), 0)
    lane = lax.broadcasted_iota(jnp.int32, (8, LANES), 1)
    low_wall = jnp.where(cx == 0, 0, -1)
    high_wall = jnp.where(cx == ny - 1, ORDER, -1)
    keep7 = jnp.where((jrow == low_wall) | (jrow == high_wall), 0.0, 1.0)
    mrow = lax.broadcasted_iota(jnp.int32, (16, LANES), 0)
    brow = lax.rem(mrow, 4)
    high_wall3 = jnp.where(cx == ny - 1, MID_ORDER, -1)
    keep3 = jnp.where((brow == low_wall) | (brow == high_wall3), 0.0, 1.0)
    _, keep_f, gain_f = smoother(ORDER)
    _, keep_m, gain_m = smoother(MID_ORDER)

    def halves(a):
        top = a.astype(jnp.bfloat16)
        return top, (a - top.astype(jnp.float32)).astype(jnp.bfloat16)

    def rdot(a, name):
        top, rest = halves(a)
        return jnp.dot(jnp.concatenate([top, top, rest], axis=1), mat[name][...],
                       preferred_element_type=jnp.float32)

    def ldot(name, b):
        top, rest = halves(b)
        parts = [top, rest] if name == "pick" else [top, top, rest]
        return jnp.dot(mat[name][...], jnp.concatenate(parts, axis=0),
                       preferred_element_type=jnp.float32)

    def fine_xy(u):
        kx = tab("kx").reshape(8, 8, 8, LANES)
        ax = kx[0][None] * u[:, 0:1]
        for a in range(1, 8):
            ax = ax + kx[a][None] * u[:, a : a + 1]
        ky = tab("ky")
        flat = u.reshape(16, 8, LANES)
        ay = ky[0][None] * flat
        for s in range(1, 8):
            ay = ay + ky[s][None] * pltpu.roll(flat, s, 1)
        return ax, ay.reshape(2, 8, 8, LANES) * tab("ti")[None]

    def fine_z(u):
        az = rdot(u.reshape(128, LANES), "az7")
        return az.reshape(2, 8, 8, LANES) * tab("tij")[None]

    def fine_send_faces(ax, ay):
        fine_send[0] = ax[:, 7].reshape(16, LANES)
        fine_send[1] = ax[:, 0].reshape(16, LANES)
        flat = ay.reshape(16, 8, LANES)
        fine_send[2] = flat[:, 7, :]
        fine_send[3] = flat[:, 0, :]
        group = Group(4)
        for d in range(4):
            group.start(fine_send.at[d], fine_recv.at[d], faces[d])
        return group

    def add_x(field, low, high):
        return jnp.concatenate(
            [field[:, 0:1] + low.reshape(2, 1, 8, LANES), field[:, 1:7],
             field[:, 7:8] + high.reshape(2, 1, 8, LANES)], axis=1)

    def add_y(field, low, high):
        flat = field.reshape(16, 8, LANES)
        flat = flat + jnp.where(jrow[None] == 0, low[:, None, :], 0.0)
        flat = flat + jnp.where(jrow[None] == 7, high[:, None, :], 0.0)
        return flat.reshape(2, 8, 8, LANES)

    def fine_join(group, field):
        group.arrived()
        field = add_x(field, fine_recv[0], fine_recv[1])
        return add_y(field, fine_recv[2], fine_recv[3])

    def left(name, v):
        start_row, size = where[name]
        acc = row_ref[start_row] * v[0:1]
        for c in range(1, size):
            acc = acc + row_ref[start_row + c] * v[c : c + 1]
        return acc

    def mid_start(ax, ay):
        mid_send[0] = ax
        mid_send[1] = ay
        group = Group(4)
        for d in range(4):
            group.start(mid_send.at[d // 2], mid_recv.at[d], faces[d])
        return group

    def shifted(v, shift, mask):
        return jnp.where(mask, pltpu.roll(v, shift, 0), 0.0)

    def mid_join(group, field):
        group.arrived()
        field = field + shifted(mid_recv[0], 4, mrow < 4)
        field = field + shifted(mid_recv[1], 12, mrow >= 12)
        field = field + shifted(mid_recv[2], 13, brow == 0)
        return field + shifted(mid_recv[3], 3, brow == 3)

    def masked(dy, table, top, index):
        low = jnp.where(cx + dy == 0, 0, -1)
        high = jnp.where(cx + dy == ny - 1, top, -1)
        return table * jnp.where((index == low) | (index == high), 0.0, 1.0)

    def along_x(u, row):
        acc = kx[0][row][None] * u[:, 0]
        for a in range(1, 8):
            acc = acc + kx[a][row][None] * u[:, a]
        return acc.reshape(16, LANES)

    def along_y(u, table):
        weighted = jnp.sum(table[None] * u, axis=2)
        return (tab("ti")[:, 0][None] * weighted).reshape(16, LANES)

    need("x")
    src = vmem[0][...].reshape(16, 8, LANES)
    knode = lax.rem(lane, 8)
    src = (src + jnp.where(knode[None] == 7, pltpu.roll(src, LANES - 1, 2), 0.0)
           + jnp.where(knode[None] == 0, pltpu.roll(src, 1, 2), 0.0))
    y7, y0 = src[:, 7, :], src[:, 0, :]
    src = src.reshape(2, 8, 8, LANES)
    x7, x0 = src[:, 7].reshape(16, LANES), src[:, 0].reshape(16, LANES)
    for n, edge in enumerate((x7, y7, x0, y0, x7)):
        edge_send[n] = edge
    for i, row in ((1, 7), (0, 0)):
        for j, line in ((1, y7), (0, y0)):
            knight_send[2 * i + j] = line.reshape(2, 8, LANES)[:, row : row + 1]
    need("early")
    e7 = masked(0, tab("e7"), ORDER, jrow[None])
    kx = tab("kx").reshape(8, 8, 8, LANES)
    ky_last, ky_first = tab("kyl"), tab("kyf")
    scaled = e7[None] * src
    pairs = ((x0, along_x(scaled, 0)), (x7, along_x(scaled, 7)),
             (y0, along_y(scaled, ky_first)), (y7, along_y(scaled, ky_last)))
    for n, (raw, contracted) in enumerate(pairs):
        pair_send[n, 0] = raw
        pair_send[n, 1] = contracted
    pl.semaphore_wait(bar, len(near))
    tell(0)
    first = [Group(size) for size in (8, 4, 4, 4)]
    for n, (dx, dy) in enumerate(KNIGHTS):
        first[0].start(knight_send.at[2 * (dx < 0) + (dy < 0)], knight_recv.at[n], (-dx, -dy))
    pick_edge = {(1, 1): 2, (1, -1): 1, (-1, 1): 3, (-1, -1): 0}
    for n, d in enumerate(CORNERS):
        first[1].start(edge_send.at[pick_edge[d] : pick_edge[d] + 2], corner_recv.at[n],
                       (-d[0], -d[1]))
    for n, (dx, dy) in enumerate(TWICE):
        first[2].start(edge_send.at[(2, 0, 3, 1)[n]], twice_recv.at[n], (-dx, -dy))
    for n, (dx, dy) in enumerate(FACES):
        first[3].start(pair_send.at[n], pair_recv.at[n], (-dx, -dy))
    load(2, count)
    need("az7")
    for group in first:
        group.arrived()
    told(0)
    tell(1)
    irow = jrow[None]

    def lines_of(value):
        return value.reshape(2, 8, LANES)

    def row_of(value, row):
        return lines_of(value)[:, row : row + 1]

    def with_ends(line, first, last):
        line = lines_of(line) + jnp.where(irow == 0, first, 0.0) + jnp.where(irow == 7, last, 0.0)
        return line.reshape(16, LANES)

    knight = {d: knight_recv[n] for n, d in enumerate(KNIGHTS)}
    twice = {d: twice_recv[n] for n, d in enumerate(TWICE)}
    raw = {d: pair_recv[n, 0] for n, d in enumerate(FACES)}
    corner_x = {d: corner_recv[n, 0 if d[0] == d[1] else 1] for n, d in enumerate(CORNERS)}
    corner_y = {d: corner_recv[n, 1 if d[0] == d[1] else 0] for n, d in enumerate(CORNERS)}

    def joined(center, low_x, high_x, low_y, high_y):
        return add_y(add_x(center, low_x, high_x), low_y, high_y)

    b7 = joined(
        src, raw[-1, 0], raw[1, 0],
        with_ends(raw[0, -1], row_of(corner_y[-1, -1], 7), row_of(corner_y[1, -1], 0)),
        with_ends(raw[0, 1], row_of(corner_y[-1, 1], 7), row_of(corner_y[1, 1], 0)))
    zero = jnp.zeros_like(src)
    extra = {
        (1, 0): joined(
            zero, x7, twice[2, 0],
            with_ends(corner_y[1, -1], row_of(raw[0, -1], 7), knight[2, -1]),
            with_ends(corner_y[1, 1], row_of(raw[0, 1], 7), knight[2, 1])),
        (-1, 0): joined(
            zero, twice[-2, 0], x0,
            with_ends(corner_y[-1, -1], knight[-2, -1], row_of(raw[0, -1], 0)),
            with_ends(corner_y[-1, 1], knight[-2, 1], row_of(raw[0, 1], 0))),
        (0, 1): joined(
            zero, corner_x[-1, 1], corner_x[1, 1],
            with_ends(y7, row_of(raw[-1, 0], 7), row_of(raw[1, 0], 7)),
            with_ends(twice[0, 2], knight[-1, 2], knight[1, 2])),
        (0, -1): joined(
            zero, corner_x[-1, -1], corner_x[1, -1],
            with_ends(twice[0, -2], knight[-1, -2], knight[1, -2]),
            with_ends(y0, row_of(raw[-1, 0], 0), row_of(raw[1, 0], 0))),
    }
    extra = {d: masked(d[1], tab("e7"), ORDER, jrow[None])[None] * v for d, v in extra.items()}

    u1 = e7[None] * b7
    ax, ay = fine_xy(u1)
    au = add_x(ax + ay + fine_z(u1), pair_recv[1, 1] + along_x(extra[-1, 0], 7),
               pair_recv[0, 1] + along_x(extra[1, 0], 0))
    au = add_y(au, pair_recv[3, 1] + along_y(extra[0, -1], ky_last),
               pair_recv[2, 1] + along_y(extra[0, 1], ky_first))
    r1 = b7 - au
    x7 = (1.0 + keep_f) * u1 + gain_f * (e7[None] * r1)
    ax, ay = fine_xy(x7)
    side7 = fine_send_faces(ax, ay)
    az = fine_z(x7)
    local7 = ax + ay + az
    need("late", "rows", "down")
    ci = tab("ci")[None]
    rest7 = (src - tab("cj")[None] * (ax + ci * az) - ci * ay) * keep7[None, None]
    jx = tab("jx").reshape(8, 4, 8, LANES)
    g = jx[0][None] * rest7[:, 0:1]
    for i in range(1, 8):
        g = g + jx[i][None] * rest7[:, i : i + 1]
    g = jnp.concatenate([g[0].reshape(32, LANES), g[1].reshape(32, LANES)], axis=1)
    g3 = left("jy", rdot(g, "down"))
    g3_all[0] = g3
    wide = Group(len(AROUND) - 1)
    for n, (dx, dy) in enumerate(AROUND):
        if n:
            wide.start(g3_all.at[0], g3_all.at[n], (-dx, -dy))
    rest7_all[0] = (b7 - fine_join(side7, local7)).reshape(128, LANES)
    need("az3", "b12", "pick", "lown")
    told(1)
    ring1, ring2, ring3 = offsets(1), offsets(2), offsets(3)
    e3 = {dy: masked(dy, rtab("e3")[0], MID_ORDER, brow) for dy in range(-3, 4)}
    e3_all = jnp.concatenate([e3[dy] for _, dy in ring3], axis=0)
    tc, tab3 = rtab("tc")[0], rtab("tab")[0]
    n1, n2, n3 = 16 * len(ring1), 16 * len(ring2), 16 * len(ring3)

    def mid_z(v):
        return tab3 * rdot(v, "az3")

    wide.arrived()

    b3 = ldot("pick", g3_all[...].reshape(16 * len(AROUND), LANES))
    v1 = e3_all[:n1] * b3
    b3, e3 = b3[:16], e3[0]
    r1 = b3 - tc * ldot("lown", v1) - mid_z(v1[:16])
    x3 = (1.0 + keep_m) * v1[:16] + gain_m * (e3 * r1)
    ax, ay = left("lx", x3), left("ly", x3)
    ca, cb = rtab("ca")[0], rtab("cb")[0]
    part = keep3 * (g3 - cb * ax - ca * ay)
    other = keep3 * (ca * cb * tab3) * x3
    line = rdot(jnp.concatenate([part, -other], axis=1), "b12")
    line = jnp.sum(rtab("jj")[0] * line, axis=0, keepdims=True)
    line_send[0] = line

    lines = Group(ny)

    def line_copy(d, slot, to):
        return lines.make(d, line_send.at[0], line_recv.at[slot], {"cross": to})

    def far_first(n, size):
        step = lax.div(n + 1, 2)
        return size // 2 + step * (1 - 2 * lax.rem(n, 2))

    def line_out(n, carry):
        d = far_first(n, ny)
        line_copy(d, cx, lax.rem(cx + d, ny)).start()
        return carry

    def line_left(d, carry):
        line_copy(d, cx, cx).wait_send()
        return carry

    def line_arrived(n, carry):
        d = far_first(ny - 2 - n, ny)
        line_copy(d, lax.rem(cx + ny - d, ny), cx).wait_recv()
        return carry

    lax.fori_loop(0, ny - 1, line_out, 0)
    line_recv[cx] = line
    side3 = mid_start(ax, ay)
    x3_all[0] = x3
    side = [Group(len(ring) - 1) for ring in (ring2, ring1, ring3)]
    for n, (dx, dy) in enumerate(ring2):
        if n:
            side[0].start(x3_all.at[0], x3_all.at[n], (-dx, -dy))
    for n, (dx, dy) in enumerate(ring1):
        if n:
            side[1].start(rest7_all.at[0], rest7_all.at[n], (-dx, -dy))
    if ny < 32:
        line_recv[ny:] = jnp.zeros((32 - ny, 1, LANES), jnp.float32)
    rest3_all[0] = b3 - mid_join(side3, ax + ay + mid_z(x3))
    for n, (dx, dy) in enumerate(ring3):
        if n:
            side[2].start(rest3_all.at[0], rest3_all.at[n], (-dx, -dy))
    need("sin")
    for group in first + [wide, side7]:
        group.left()
    lax.fori_loop(1, ny, line_left, 0)
    lax.fori_loop(0, ny - 1, line_arrived, 0)
    spectrum = ldot("sin", line_recv[:, 0, :])
    group = lax.div(lane, 32)
    for alpha in range(2):
        total = jnp.zeros((8, LANES), jnp.float32)
        for hi in range(4):
            for beta in range(2):
                piece = spectrum[(beta * 4 + hi) * 8 : (beta * 4 + hi + 1) * 8]
                shift = 32 * (hi - 2 * alpha - beta) % LANES
                if shift:
                    piece = pltpu.roll(piece, shift, 1)
                total = total + jnp.where(group == hi, piece, 0.0)
        mode_send[alpha] = total

    modes = Group(nx)

    def mode_copy(d, to):
        return modes.make(d, mode_send, mode_recv.at[d], {"stream": to})

    def mode_out(n, carry):
        d = far_first(n, nx)
        mode_copy(d, lax.rem(sx + d, nx)).start()
        return carry

    def mode_left(d, carry):
        mode_copy(d, sx).wait_send()
        return carry

    def mode_arrived(n, carry):
        mode_copy(far_first(nx - 2 - n, nx), sx).wait_recv()
        return carry

    lax.fori_loop(0, nx - 1, mode_out, 0)
    mode_recv[0] = mode_send[...]
    need(*MATS)
    for group in side:
        group.arrived()
    for group in [side3] + side:
        group.left()
    lax.fori_loop(1, nx, mode_left, 0)
    lax.fori_loop(0, nx - 1, mode_arrived, 0)
    first = mode_recv[:, 0]
    second = mode_recv[:, 1]
    nodes = first + jnp.concatenate([second[1:], second[:1]], axis=0)
    start_g = where["green"][0]
    solved = [jnp.sum(late_ref[start_g + n : start_g + n + nx] * nodes, axis=0)
              for n in range(SPAN)]
    sine = late_ref[pl.ds(where["sine"][0] + cx, PAD)]
    window = [jnp.sum(sine * s[None], axis=1) for s in solved]
    window = jnp.concatenate(window, axis=0)
    window = rdot(window, "back")
    zval, zstiff = window[:, :LANES], window[:, LANES:]

    def per(table, count):
        return jnp.concatenate([table] * count, axis=0)

    from_low = ldot("kt", zval)
    r0 = rest3_all[...].reshape(n3, LANES) - per(tc, len(ring3)) * from_low[:n3]
    r0 = r0 - ldot("tt", zstiff)
    w1 = e3_all * r0
    aw = per(tc, len(ring2)) * ldot("lxy", w1)
    aw = aw + per(tab3, len(ring2)) * rdot(w1[:n2], "az3")
    x3 = x3_all[...].reshape(n2, LANES) + from_low[n3:]
    x3 = x3 + (1.0 + keep_m) * w1[:n2] + gain_m * (e3_all[:n2] * (r0[:n2] - aw))

    raised = rdot(x3, "upt")
    apx = ldot("fine", jnp.concatenate(
        [raised[:, : 2 * LANES], raised[:n1, 2 * LANES :]], axis=0))
    px = rdot(x3[:16], "up")
    px = jnp.stack([ldot("pfine", px[:, r * LANES : (r + 1) * LANES]) for r in range(2)])
    px = px.reshape(2, 8, 8, LANES)
    r0, u1 = [], []
    for n, (dx, dy) in enumerate(ring1):
        mine = apx[64 * n : 64 * n + 64]
        moved = jnp.stack([mine[:, r * LANES : (r + 1) * LANES] for r in range(2)])
        r0.append(rest7_all[n].reshape(2, 8, 8, LANES) - moved.reshape(2, 8, 8, LANES))
        scale = masked(dy, tab("e7"), ORDER, jrow[None]) if dy else e7
        u1.append(scale[None] * r0[n])

    ax, ay = fine_xy(u1[0])
    au = ax + ay + fine_z(u1[0])
    au = add_x(au, along_x(u1[2], 7), along_x(u1[1], 0))
    au = add_y(au, along_y(u1[4], ky_last), along_y(u1[3], ky_first))
    x7 = x7 + px
    out = x7 + (1.0 + keep_f) * u1[0] + gain_f * (e7[None] * (r0[0] - au))
    out_ref[...] = out.reshape(128, LANES)


def solution(mesh):
    nx, ny = mesh.shape["stream"], mesh.shape["cross"]
    tables, where = build_tables(nx, ny)

    def body(sources):
        flat = sources.reshape(128, LANES)
        operands = [flat] + [jnp.asarray(table) for table in tables]
        links, f32 = pltpu.SemaphoreType.DMA, jnp.float32
        out = pl.pallas_call(
            functools.partial(kernel, nx, ny, where),
            out_shape=jax.ShapeDtypeStruct((128, LANES), jnp.float32),
            in_specs=[pl.BlockSpec(memory_space=pl.ANY)] * len(operands),
            out_specs=pl.BlockSpec(memory_space=pltpu.VMEM),
            scratch_shapes=[pltpu.VMEM(o.shape, o.dtype) for o in operands]
            + [
                pltpu.VMEM((4, 2, 16, LANES), f32),
                pltpu.VMEM((4, 2, 16, LANES), f32),
                pltpu.VMEM((5, 16, LANES), f32),
                pltpu.VMEM((4, 2, 16, LANES), f32),
                pltpu.VMEM((4, 16, LANES), f32),
                pltpu.VMEM((4, 2, 1, LANES), f32),
                pltpu.VMEM((8, 2, 1, LANES), f32),
                pltpu.VMEM((len(AROUND), 16, LANES), f32),
                pltpu.VMEM((4, 16, LANES), f32),
                pltpu.VMEM((4, 16, LANES), f32),
                pltpu.VMEM((2, 16, LANES), f32),
                pltpu.VMEM((4, 16, LANES), f32),
                pltpu.VMEM((1, 1, LANES), f32),
                pltpu.VMEM((32, 1, LANES), f32),
                pltpu.VMEM((2, 8, LANES), f32),
                pltpu.VMEM((nx, 2, 8, LANES), f32),
                pltpu.VMEM((len(offsets(3)), 16, LANES), f32),
                pltpu.VMEM((len(offsets(2)), 16, LANES), f32),
                pltpu.VMEM((len(offsets(1)), 128, LANES), f32),
                links((len(operands),)),
                links((LINKS + nx + ny,)),
                links((LINKS + nx + ny,)),
                pltpu.SemaphoreType.REGULAR((2, 2)),
            ],
            compiler_params=pltpu.CompilerParams(collective_id=0, has_side_effects=True),
            name="vcycle",
        )(*operands)
        return out.reshape(sources.shape)

    spec = P(None, "stream", "cross", None, None, None)
    return jax.shard_map(body, mesh=mesh, in_specs=(spec,), out_specs=spec, check_vma=False)
```

```python
import functools
import math

import jax
import jax.numpy as jnp
import ml_dtypes
import numpy as np
from jax import lax
from jax.experimental import pallas as pl
from jax.experimental.pallas import tpu as pltpu
from jax.sharding import PartitionSpec as P

ORDER = 7
MID_ORDER = 3
EZ = 16
LANES = 128
MODES = 32
MESH_ID = pl.DeviceIdType.MESH
FACES = ((1, 0), (-1, 0), (0, 1), (0, -1))
CORNERS = ((1, 1), (1, -1), (-1, 1), (-1, -1))
TWICE = ((2, 0), (-2, 0), (0, 2), (0, -2))
KNIGHTS = tuple((s * a, t * b) for a, b in ((2, 1), (1, 2)) for s in (1, -1) for t in (1, -1))
AROUND = ((0, 0),) + FACES + CORNERS + TWICE + KNIGHTS
VMEM_LIMIT = 55168 * 1024
WIDE, SPAN, PAD = 4, 10, 16


def legendre_pair(degree, points):
    below_poly = np.ones(points.shape)
    top_poly = points.copy()
    for step in range(2, degree + 1):
        below_poly, top_poly = (
            top_poly,
            ((2 * step - 1) * points * top_poly - (step - 1) * below_poly) / step,
        )
    return (below_poly, top_poly)


@functools.lru_cache(None)
def gll_tables(degree):
    nodes = -np.cos(np.pi * np.arange(degree + 1) / degree)
    for _ in range(100):
        below_poly, top_poly = legendre_pair(degree, nodes)
        nodes = nodes - (nodes * top_poly - below_poly) / ((degree + 1) * top_poly)
    at_nodes = legendre_pair(degree, nodes)[1]
    weights = 2.0 / (degree * (degree + 1) * at_nodes**2)
    count = degree + 1
    derivative = np.zeros((count, count))
    for target in range(count):
        for source in range(count):
            if target != source:
                derivative[target, source] = at_nodes[target] / (
                    at_nodes[source] * (nodes[target] - nodes[source])
                )
    derivative[0, 0] = -degree * (degree + 1) / 4.0
    derivative[degree, degree] = degree * (degree + 1) / 4.0
    stiffness = derivative.T @ (weights[:, None] * derivative)
    return (nodes, weights, stiffness)


def lagrange_matrix(fine_degree, coarse_degree):
    fine_nodes = gll_tables(fine_degree)[0]
    coarse_nodes = gll_tables(coarse_degree)[0]
    table = np.ones((fine_degree + 1, coarse_degree + 1))
    for column in range(coarse_degree + 1):
        for other in range(coarse_degree + 1):
            if other != column:
                table[:, column] *= (fine_nodes - coarse_nodes[other]) / (
                    coarse_nodes[column] - coarse_nodes[other]
                )
    return table


@functools.lru_cache(None)
def smoother(degree):
    stiffness = gll_tables(degree)[2]
    elements = 6
    size = elements * degree
    assembled = np.zeros((size, size))
    for element in range(elements):
        for row in range(degree + 1):
            for col in range(degree + 1):
                assembled[(element * degree + row) % size, (element * degree + col) % size] += (
                    stiffness[row, col]
                )
    diagonal = np.sqrt(np.diagonal(assembled))
    scaled = assembled / diagonal[:, None] / diagonal[None, :]
    positions = np.arange(size)
    vector = np.where(positions % 2 == 0, 1.0, -1.0) * (1.0 + positions / size)
    for _ in range(2000):
        vector = scaled @ vector
        vector = vector / np.sqrt(np.sum(vector * vector))
    high = float(np.sum(vector * (scaled @ vector)) / np.sum(vector * vector))
    low = 0.1 * high
    theta, delta = 0.5 * (high + low), 0.5 * (high - low)
    sigma = theta / delta
    rho1 = 1.0 / sigma
    rho2 = 1.0 / (2.0 * sigma - rho1)
    return theta, rho2 * rho1, 2.0 * rho2 / delta * theta


def level(degree):
    _, w, k = gll_tables(degree)
    t = w.copy()
    t[0] = t[-1] = w[0] + w[-1]
    s = np.diagonal(k).copy()
    s[0] = s[-1] = k[0, 0] + k[-1, -1]
    c = np.ones(degree + 1)
    c[0] = c[-1] = 0.5
    diag = (
        s[:, None, None] * t[None, :, None] * t[None, None, :]
        + t[:, None, None] * s[None, :, None] * t[None, None, :]
        + t[:, None, None] * t[None, :, None] * s[None, None, :]
    )
    return w, k, t, c, 1.0 / (diag * smoother(degree)[0])


def join_z(count):
    size = EZ * count
    m = np.eye(size)
    for e in range(EZ):
        a, b = e * count + count - 1, ((e + 1) % EZ) * count
        m[a, b] += 1.0
        m[b, a] += 1.0
    return m


def two(m):
    return np.kron(np.eye(2), m)


def lanes(values):
    return np.broadcast_to(values[None, :], (8, LANES))


def rows(values):
    return np.broadcast_to(np.asarray(values)[..., None], np.shape(values) + (LANES,))


def fourier_rows(total):
    k, n = np.meshgrid(np.arange(total), np.arange(total), indexing="ij")
    half = total // 2
    freq = np.where(k <= half, k, k - half)
    angle = 2.0 * np.pi * (freq * n % total) / total
    scale = np.where((k == 0) | (k == half), math.sqrt(1.0 / total), math.sqrt(2.0 / total))
    return scale * np.where(k <= half, np.cos(angle), np.sin(angle))


def sine_rows(mode, point, total):
    product = mode * point % (2 * total)
    inside = (mode > 0) & (mode < total) & (point > 0) & (point < total)
    return np.where(inside, math.sqrt(2.0 / total) * np.sin(np.pi * product / total), 0.0)


def green_table(nx, ny):
    mode = np.arange(MODES)
    wall_gap = 2.0 * np.sin(0.5 * np.pi * mode / ny) ** 2 + np.where(mode % ny == 0, 1.0, 0.0)
    freq = np.arange(EZ)
    freq = np.where(freq <= EZ // 2, freq, freq - EZ // 2)
    span_gap = 2.0 * np.sin(np.pi * freq / EZ) ** 2
    half_gap = wall_gap[:, None] + span_gap[None, :]
    root = np.sqrt(half_gap * (2.0 + half_gap))
    rate = np.log1p(half_gap + root)
    d = np.arange(nx)[:, None, None]
    top = np.exp(-rate * d) + np.exp(-rate * (nx - d))
    return top / (4.0 * root * -np.expm1(-rate * nx))


def modal(values):
    v = values.reshape(values.shape[:-2] + (MODES // 8, 8, EZ))
    v = np.stack([v, v], axis=-2)
    v = np.moveaxis(v, -4, -3)
    return v.reshape(v.shape[:-3] + (LANES,))


def offsets(radius):
    found = [(0, 0), *FACES]
    for ring in range(2, radius + 1):
        found += [
            (dx, dy)
            for dx in range(-ring, ring + 1)
            for dy in range(-ring, ring + 1)
            if abs(dx) + abs(dy) == ring
        ]
    return found


def assembled_1d(local_cols, window):
    count = local_cols.shape[0]
    out = np.zeros((count, window))
    out[:, 1:3] += local_cols
    out[0, 0:2] += local_cols[-1]
    out[-1, 2:4] += local_cols[0]
    return out


@functools.lru_cache(None)
def build_tables(nx, ny):
    f, q = ORDER + 1, MID_ORDER + 1
    w7, k7, t7, c7, e7 = level(ORDER)
    w3, k3, t3, c3, e3 = level(MID_ORDER)
    j73 = lagrange_matrix(ORDER, MID_ORDER)
    j31 = lagrange_matrix(MID_ORDER, 1)
    tile = {}
    tk = np.tile(t7, EZ)
    ones = np.ones((8, LANES))
    tile["kx"] = np.stack(
        [np.stack([k7[i, a] * t7[:, None] * tk[None, :] for i in range(f)]) for a in range(f)]
    ).reshape(f * f, 8, LANES)
    roll = np.stack([[k7[j, (j - s) % f] for j in range(f)] for s in range(f)])
    tile["ky"] = roll[:, :, None] * tk[None, None, :]
    tile["kyl"] = (k7[f - 1][:, None] * tk[None, :])[None]
    tile["kyf"] = (k7[0][:, None] * tk[None, :])[None]
    tile["e7"] = np.tile(e7, (1, 1, EZ))
    tile["ti"] = np.stack([t * ones for t in t7])
    tile["tij"] = np.stack([t * rows(t7) for t in t7])
    tile["cj"] = rows(c7)[None]
    tile["ci"] = np.stack([c * ones for c in c7])
    tile["jx"] = np.stack([j73[i, a] * ones for i in range(f) for a in range(q)])
    green = modal(green_table(nx, ny))
    tile["green"] = green[(np.arange(nx + SPAN - 1) - WIDE) % nx]
    point = np.arange(-WIDE, ny - WIDE + PAD)
    tile["sine"] = modal(
        np.broadcast_to(
            sine_rows(np.arange(MODES)[None, :], point[:, None], ny)[:, :, None],
            (len(point), MODES, EZ),
        )
    )
    row = {}
    mid = [(a, b) for a in range(q) for b in range(q)]
    tc = np.tile(np.tile(t3, EZ), 2)

    def left(matrix, scale=None):
        scale = np.ones(LANES) if scale is None else scale
        return matrix.T[:, :, None] * scale[None, None, :]

    row["jy"] = left(
        np.array([[(a == a2) * j73[j, b] for a2 in range(q) for j in range(f)] for a, b in mid])
    )
    row["lx"] = left(np.kron(k3, np.diag(t3)), tc)
    row["ly"] = left(np.kron(np.diag(t3), k3), tc)
    row["e3"] = np.stack([np.tile(np.tile(e3[a, b], EZ), 2) for a, b in mid])[None]
    row["tab"] = rows([t3[a] * t3[b] for a, b in mid])[None]
    row["ca"] = rows([c3[a] for a, b in mid])[None]
    row["cb"] = rows([c3[b] for a, b in mid])[None]
    groups = [np.array([j31[a, x] * j31[b, y] for a, b in mid]) for x in (0, 1) for y in (0, 1)]
    row["jj"] = np.repeat(np.stack(groups, axis=1), MODES, axis=1)[None]
    own = np.zeros((q, 4))
    own[:, 1:3] = j31
    stiff = assembled_1d(k3 @ j31, 4)
    mass = t3[:, None] * own

    ring1, ring2, ring3 = offsets(1), offsets(2), offsets(3)

    def placed(first, second, elements):
        out = np.zeros((len(elements), q, q, SPAN, PAD))
        for n, (dx, dy) in enumerate(elements):
            x0, y0 = dx - 1 + WIDE, dy - 1 + WIDE
            out[n, :, :, x0 : x0 + 4, y0 : y0 + 4] = np.einsum("at,bq->abtq", first, second)
        return out.reshape(len(elements) * q * q, SPAN * PAD)

    mat = {}
    mat["kt"] = np.concatenate(
        [placed(stiff, mass, ring3) + placed(mass, stiff, ring3), placed(own, own, ring2)])
    mat["tt"] = placed(mass, mass, ring3)
    cross = np.zeros((len(ring2), q, q, len(ring3), q, q))
    ends = {(1, 0): (3, 0), (-1, 0): (0, 3), (0, 1): (3, 0), (0, -1): (0, 3)}
    diag3 = np.diag(t3)
    for n, (dx, dy) in enumerate(ring2):
        cross[n, :, :, n] += np.einsum("ac,bd->abcd", k3, diag3)
        cross[n, :, :, n] += np.einsum("ac,bd->abcd", diag3, k3)
        for (fx, fy), (mine, theirs) in ends.items():
            m = ring3.index((dx + fx, dy + fy))
            line = np.zeros((q, q))
            line[mine] = k3[theirs]
            if fx:
                cross[n, :, :, m] += np.einsum("ac,bd->abcd", line, diag3)
            else:
                cross[n, :, :, m] += np.einsum("ac,bd->abcd", diag3, line)
    pick = np.zeros((len(ring1), q, q, len(AROUND), q, q))
    for n, (dx, dy) in enumerate(ring1):
        for m, (gx, gy) in enumerate(AROUND):
            sx, sy = gx - dx, gy - dy
            if max(abs(sx), abs(sy)) > 1:
                continue
            span_x = [(a, a) for a in range(q)] if sx == 0 else [(q - 1, 0) if sx > 0 else (0, q - 1)]
            span_y = [(b, b) for b in range(q)] if sy == 0 else [(q - 1, 0) if sy > 0 else (0, q - 1)]
            for a, a2 in span_x:
                for b, b2 in span_y:
                    pick[n, a, b, m, a2, b2] = 1.0
    mat["pick"] = pick.reshape(len(ring1) * 16, len(AROUND) * 16)
    mat["lxy"] = cross.reshape(len(ring2) * 16, len(ring3) * 16)
    k7j = k7 @ j73
    t7j = t7[:, None] * j73
    fine = np.zeros((len(ring1), f, f, len(ring2), q, q))
    own_z = np.zeros((len(ring1), f, f, len(ring1), q, q))
    for n, (dx, dy) in enumerate(ring1):
        fine[n, :, :, n] += np.einsum("ia,jb->ijab", k7j, t7j) + np.einsum("ia,jb->ijab", t7j, k7j)
        own_z[n, :, :, n] = np.einsum("ia,jb->ijab", t7j, t7j)
        for (fx, fy), (mine, theirs) in ends.items():
            mine, theirs = (f - 1 if mine else 0), (f - 1 if theirs else 0)
            m = ring2.index((dx + fx, dy + fy))
            if fx:
                fine[n, mine, :, m] += np.einsum("a,jb->jab", k7j[theirs], t7j)
            else:
                fine[n, :, mine, m] += np.einsum("ia,b->iab", t7j, k7j[theirs])
    count = len(ring1) * f * f
    mat["fine"] = np.concatenate([fine.reshape(count, -1), own_z.reshape(count, -1)], axis=1)
    mat["lown"] = mat["lxy"][:16, : 16 * len(ring1)]
    mat["pfine"] = np.einsum("ia,jb->ijab", j73, j73).reshape(f * f, 16)
    row["tc"] = np.broadcast_to(tc, (1, 16, LANES))
    az7 = (join_z(f) @ np.kron(np.eye(EZ), k7)).T
    az3 = two((join_z(q) @ np.kron(np.eye(EZ), k3)).T)
    down = (join_z(q) @ np.kron(np.eye(EZ), j73.T) @ np.diag(np.tile(c7, EZ))).T
    zero = np.zeros_like(down)
    mat["az7"] = az7
    mat["down"] = np.concatenate(
        [np.concatenate([down, zero], axis=1), np.concatenate([zero, down], axis=1)], axis=0
    )
    mat["az3"] = az3
    up = np.kron(np.eye(EZ), j73).T
    mat["up"] = two(up)
    up_tk = up * np.tile(t7, EZ)[None]
    mat["upt"] = np.concatenate([two(up_tk), two(up @ az7)], axis=1)
    gather = np.zeros((EZ, EZ * q))
    for e in range(EZ):
        for node in (0, 1):
            gather[(e + node) % EZ, e * q : (e + 1) * q] += j31[:, node] * c3
    b1 = two((fourier_rows(EZ) @ gather).T)
    b1 = np.tile(b1, (1, 4))
    mat["b12"] = np.concatenate([b1, az3 @ b1], axis=0)
    spread = np.zeros((EZ * q, EZ))
    for e in range(EZ):
        for node in (0, 1):
            spread[e * q : (e + 1) * q, (e + node) % EZ] += j31[:, node]
    back = two((spread @ fourier_rows(EZ).T).T)
    back = np.tile(back, (4, 1))
    mat["back"] = np.concatenate([back, back @ az3], axis=1)
    mode, here = np.arange(MODES)[:, None], np.arange(32)[None, :]
    s0 = np.where(here < ny, sine_rows(mode, here, ny), 0.0)
    s1 = np.where(here < ny, sine_rows(mode, here + 1, ny), 0.0)
    mat["sin"] = np.concatenate([s0, s1], axis=0)
    where, tiles, at = {}, [], 0
    for name in EARLY + LATE + tuple(row):
        value = tile[name] if name in tile else row[name].reshape(-1, 8, LANES)
        where[name] = (at, value.shape[0])
        tiles.append(value.astype(np.float32))
        at += value.shape[0]
    blocks, at = [], 0
    for name in MATS:
        value = mat[name].astype(np.float32)
        top = value.astype(ml_dtypes.bfloat16)
        rest = (value - top.astype(np.float32)).astype(ml_dtypes.bfloat16)
        parts = [top, top] if name == "pick" else [top, rest, top]
        value = np.concatenate(parts, axis=0 if name in RIGHT else 1)
        height, width = value.shape
        count = -(-width // LANES)
        value = np.pad(value, ((0, 0), (0, count * LANES - width)))
        where[name] = (at, height, width)
        blocks += [value[:, LANES * n : LANES * n + LANES] for n in range(count)]
        at += height * count
    return np.concatenate(tiles), np.concatenate(blocks), where


EARLY = ("e7", "kx", "kyl", "kyf", "ti", "ky", "tij")
LATE = ("cj", "ci", "jx", "green", "sine")
RIGHT = ("az7", "down", "az3", "b12", "back", "up", "upt")
MATS = ("az7", "down", "pick", "lown", "az3", "b12", "sin", "back", "kt", "tt", "lxy", "up", "upt",
        "fine", "pfine")
LINKS = 20 + 4 + 20 + 4 + 12 + 4 + 24


def reach(n):
    base = max(n // 8, 1)
    known, hops = base, []
    while known < n // 2:
        hops.append(known)
        known *= 2
    return range(1, base + 1), hops


def kernel(nx, ny, where, *refs):
    hbm, out_ref, vmem = refs[:3], refs[3], refs[4:7]
    (pair_send, pair_recv, edge_send, corner_recv, twice_recv, knight_send, knight_recv, g3_all,
     fine_send, fine_recv, mid_send, mid_recv, line_send, line_recv, mode_send, mode_recv,
     rest3_all, x3_all, rest7_all, load_sem, send_sem, recv_sem, known) = refs[7:]
    sx, cx = lax.axis_index("stream"), lax.axis_index("cross")
    tile_ref, block_ref = vmem[1:]

    def at(dx, dy):
        return {"stream": lax.rem(sx + (nx + dx), nx), "cross": lax.rem(cx + (ny + dy), ny)}

    def tab(name):
        start, size = where[name]
        return tile_ref[start : start + size]

    def rtab(name):
        return tab(name).reshape(-1, 16, LANES)

    def mat(name):
        start, height, width = where[name]
        parts = [block_ref[start + n * height : start + (n + 1) * height]
                 for n in range(-(-width // LANES))]
        return (parts[0] if len(parts) == 1 else jnp.concatenate(parts, axis=1))[:, :width]

    bar = pltpu.get_barrier_semaphore()
    faces = FACES
    near_x, hops_x = reach(nx)
    near_y, hops_y = reach(ny)
    near = list(KNIGHTS + CORNERS)
    near += [(s * d, 0) for d in reversed(near_x) for s in (1, -1)]
    near += [(0, s * d) for d in reversed(near_y) for s in (1, -1)]
    for d in near:
        pl.semaphore_signal(bar, inc=1, device_id=at(*d), device_id_type=MESH_ID)
    late, last = where[LATE[0]][0], where["sin"][0]
    spans = {"x": (0, 0, 128), "early": (1, 0, late), "late": (1, late, hbm[1].shape[0]),
             "first": (2, 0, last), "last": (2, last, hbm[2].shape[0])}
    loads = {}

    def load(*wanted):
        for name in wanted:
            operand, start, end = spans[name]
            part = pl.ds(start, end - start)
            loads[name] = pltpu.make_async_copy(
                hbm[operand].at[part], vmem[operand].at[part], load_sem.at[list(spans).index(name)])
            loads[name].start()

    load("x", "early")

    def need(*wanted):
        for name in wanted:
            if name in loads:
                loads.pop(name).wait()

    def tell(step):
        for n, hops in enumerate((hops_x, hops_y)):
            if step < len(hops):
                for s in (1, -1):
                    d = (s * hops[step], 0) if n == 0 else (0, s * hops[step])
                    pl.semaphore_signal(
                        known.at[step, n], inc=1, device_id=at(*d), device_id_type=MESH_ID)

    def told(step):
        for n, hops in enumerate((hops_x, hops_y)):
            if step < len(hops):
                pl.semaphore_wait(known.at[step, n], 2)

    used = [0]

    class Group:
        def __init__(self, size):
            self.base, self.copies = used[0], []
            used[0] += size

        def make(self, n, src, dst, device):
            return pltpu.make_async_remote_copy(
                src, dst, send_sem.at[self.base + n], recv_sem.at[self.base + n],
                device_id=device, device_id_type=MESH_ID)

        def start(self, src, dst, to):
            copy = self.make(len(self.copies), src, dst, at(*to))
            copy.start()
            self.copies.append(copy)

        def arrived(self):
            for copy in self.copies:
                copy.wait_recv()

        def left(self):
            for copy in self.copies:
                copy.wait_send()

    jrow = lax.broadcasted_iota(jnp.int32, (8, LANES), 0)
    lane = lax.broadcasted_iota(jnp.int32, (8, LANES), 1)
    low_wall = jnp.where(cx == 0, 0, -1)
    high_wall = jnp.where(cx == ny - 1, ORDER, -1)
    keep7 = jnp.where((jrow == low_wall) | (jrow == high_wall), 0.0, 1.0)
    mrow = lax.broadcasted_iota(jnp.int32, (16, LANES), 0)
    brow = lax.rem(mrow, 4)
    high_wall3 = jnp.where(cx == ny - 1, MID_ORDER, -1)
    keep3 = jnp.where((brow == low_wall) | (brow == high_wall3), 0.0, 1.0)
    _, keep_f, gain_f = smoother(ORDER)
    _, keep_m, gain_m = smoother(MID_ORDER)

    def halves(a):
        top = a.astype(jnp.bfloat16)
        return top, (a - top.astype(jnp.float32)).astype(jnp.bfloat16)

    def rdot(a, name):
        top, rest = halves(a)
        return jnp.dot(jnp.concatenate([top, top, rest], axis=1), mat(name),
                       preferred_element_type=jnp.float32)

    def ldot(name, b):
        top, rest = halves(b)
        parts = [top, rest] if name == "pick" else [top, top, rest]
        return jnp.dot(mat(name), jnp.concatenate(parts, axis=0),
                       preferred_element_type=jnp.float32)

    def fine_xy(u):
        kx = tab("kx").reshape(8, 8, 8, LANES)
        ax = kx[0][None] * u[:, 0:1]
        for a in range(1, 8):
            ax = ax + kx[a][None] * u[:, a : a + 1]
        ky = tab("ky")
        flat = u.reshape(16, 8, LANES)
        ay = ky[0][None] * flat
        for s in range(1, 8):
            ay = ay + ky[s][None] * pltpu.roll(flat, s, 1)
        return ax, ay.reshape(2, 8, 8, LANES) * tab("ti")[None]

    def fine_z(u):
        az = rdot(u.reshape(128, LANES), "az7")
        return az.reshape(2, 8, 8, LANES) * tab("tij")[None]

    def fine_send_faces(ax, ay):
        fine_send[0] = ax[:, 7].reshape(16, LANES)
        fine_send[1] = ax[:, 0].reshape(16, LANES)
        flat = ay.reshape(16, 8, LANES)
        fine_send[2] = flat[:, 7, :]
        fine_send[3] = flat[:, 0, :]
        group = Group(4)
        for d in range(4):
            group.start(fine_send.at[d], fine_recv.at[d], faces[d])
        return group

    def add_x(field, low, high):
        return jnp.concatenate(
            [field[:, 0:1] + low.reshape(2, 1, 8, LANES), field[:, 1:7],
             field[:, 7:8] + high.reshape(2, 1, 8, LANES)], axis=1)

    def add_y(field, low, high):
        flat = field.reshape(16, 8, LANES)
        flat = flat + jnp.where(jrow[None] == 0, low[:, None, :], 0.0)
        flat = flat + jnp.where(jrow[None] == 7, high[:, None, :], 0.0)
        return flat.reshape(2, 8, 8, LANES)

    def fine_join(group, field):
        group.arrived()
        field = add_x(field, fine_recv[0], fine_recv[1])
        return add_y(field, fine_recv[2], fine_recv[3])

    def left(name, v):
        start_row, size = where[name]
        acc = 0.0
        for c in range(size // 2):
            both = tile_ref[start_row + 2 * c : start_row + 2 * c + 2].reshape(16, LANES)
            acc = acc + both * v[c : c + 1]
        return acc

    def mid_start(ax, ay):
        mid_send[0] = ax
        mid_send[1] = ay
        group = Group(4)
        for d in range(4):
            group.start(mid_send.at[d // 2], mid_recv.at[d], faces[d])
        return group

    def shifted(v, shift, mask):
        return jnp.where(mask, pltpu.roll(v, shift, 0), 0.0)

    def mid_join(group, field):
        group.arrived()
        field = field + shifted(mid_recv[0], 4, mrow < 4)
        field = field + shifted(mid_recv[1], 12, mrow >= 12)
        field = field + shifted(mid_recv[2], 13, brow == 0)
        return field + shifted(mid_recv[3], 3, brow == 3)

    def masked(dy, table, top, index):
        low = jnp.where(cx + dy == 0, 0, -1)
        high = jnp.where(cx + dy == ny - 1, top, -1)
        return table * jnp.where((index == low) | (index == high), 0.0, 1.0)

    def along_x(u, row):
        acc = kx[0][row][None] * u[:, 0]
        for a in range(1, 8):
            acc = acc + kx[a][row][None] * u[:, a]
        return acc.reshape(16, LANES)

    def along_y(u, table):
        weighted = jnp.sum(table[None] * u, axis=2)
        return (tab("ti")[:, 0][None] * weighted).reshape(16, LANES)

    need("x")
    src = vmem[0][...].reshape(16, 8, LANES)
    knode = lax.rem(lane, 8)
    src = (src + jnp.where(knode[None] == 7, pltpu.roll(src, LANES - 1, 2), 0.0)
           + jnp.where(knode[None] == 0, pltpu.roll(src, 1, 2), 0.0))
    y7, y0 = src[:, 7, :], src[:, 0, :]
    src = src.reshape(2, 8, 8, LANES)
    x7, x0 = src[:, 7].reshape(16, LANES), src[:, 0].reshape(16, LANES)
    for n, edge in enumerate((x7, y7, x0, y0, x7)):
        edge_send[n] = edge
    for i, row in ((1, 7), (0, 0)):
        for j, line in ((1, y7), (0, y0)):
            knight_send[2 * i + j] = line.reshape(2, 8, LANES)[:, row : row + 1]
    need("early")
    e7 = masked(0, tab("e7"), ORDER, jrow[None])
    kx = tab("kx").reshape(8, 8, 8, LANES)
    ky_last, ky_first = tab("kyl"), tab("kyf")
    scaled = e7[None] * src
    pairs = ((x0, along_x(scaled, 0)), (x7, along_x(scaled, 7)),
             (y0, along_y(scaled, ky_first)), (y7, along_y(scaled, ky_last)))
    for n, (raw, contracted) in enumerate(pairs):
        pair_send[n, 0] = raw
        pair_send[n, 1] = contracted
    pl.semaphore_wait(bar, len(near))
    tell(0)
    first = [Group(size) for size in (8, 4, 4, 4)]
    for n, (dx, dy) in enumerate(KNIGHTS):
        first[0].start(knight_send.at[2 * (dx < 0) + (dy < 0)], knight_recv.at[n], (-dx, -dy))
    pick_edge = {(1, 1): 2, (1, -1): 1, (-1, 1): 3, (-1, -1): 0}
    for n, d in enumerate(CORNERS):
        first[1].start(edge_send.at[pick_edge[d] : pick_edge[d] + 2], corner_recv.at[n],
                       (-d[0], -d[1]))
    for n, (dx, dy) in enumerate(TWICE):
        first[2].start(edge_send.at[(2, 0, 3, 1)[n]], twice_recv.at[n], (-dx, -dy))
    for n, (dx, dy) in enumerate(FACES):
        first[3].start(pair_send.at[n], pair_recv.at[n], (-dx, -dy))
    load("first", "late", "last")
    need("first")
    for group in first:
        group.arrived()
    told(0)
    tell(1)
    irow = jrow[None]

    def lines_of(value):
        return value.reshape(2, 8, LANES)

    def row_of(value, row):
        return lines_of(value)[:, row : row + 1]

    def with_ends(line, first, last):
        line = lines_of(line) + jnp.where(irow == 0, first, 0.0) + jnp.where(irow == 7, last, 0.0)
        return line.reshape(16, LANES)

    knight = {d: knight_recv[n] for n, d in enumerate(KNIGHTS)}
    twice = {d: twice_recv[n] for n, d in enumerate(TWICE)}
    raw = {d: pair_recv[n, 0] for n, d in enumerate(FACES)}
    corner_x = {d: corner_recv[n, 0 if d[0] == d[1] else 1] for n, d in enumerate(CORNERS)}
    corner_y = {d: corner_recv[n, 1 if d[0] == d[1] else 0] for n, d in enumerate(CORNERS)}

    def joined(center, low_x, high_x, low_y, high_y):
        return add_y(add_x(center, low_x, high_x), low_y, high_y)

    b7 = joined(
        src, raw[-1, 0], raw[1, 0],
        with_ends(raw[0, -1], row_of(corner_y[-1, -1], 7), row_of(corner_y[1, -1], 0)),
        with_ends(raw[0, 1], row_of(corner_y[-1, 1], 7), row_of(corner_y[1, 1], 0)))
    zero = jnp.zeros_like(src)
    extra = {
        (1, 0): joined(
            zero, x7, twice[2, 0],
            with_ends(corner_y[1, -1], row_of(raw[0, -1], 7), knight[2, -1]),
            with_ends(corner_y[1, 1], row_of(raw[0, 1], 7), knight[2, 1])),
        (-1, 0): joined(
            zero, twice[-2, 0], x0,
            with_ends(corner_y[-1, -1], knight[-2, -1], row_of(raw[0, -1], 0)),
            with_ends(corner_y[-1, 1], knight[-2, 1], row_of(raw[0, 1], 0))),
        (0, 1): joined(
            zero, corner_x[-1, 1], corner_x[1, 1],
            with_ends(y7, row_of(raw[-1, 0], 7), row_of(raw[1, 0], 7)),
            with_ends(twice[0, 2], knight[-1, 2], knight[1, 2])),
        (0, -1): joined(
            zero, corner_x[-1, -1], corner_x[1, -1],
            with_ends(twice[0, -2], knight[-1, -2], knight[1, -2]),
            with_ends(y0, row_of(raw[-1, 0], 0), row_of(raw[1, 0], 0))),
    }
    extra = {d: masked(d[1], tab("e7"), ORDER, jrow[None])[None] * v for d, v in extra.items()}

    u1 = e7[None] * b7
    ax, ay = fine_xy(u1)
    au = add_x(ax + ay + fine_z(u1), pair_recv[1, 1] + along_x(extra[-1, 0], 7),
               pair_recv[0, 1] + along_x(extra[1, 0], 0))
    au = add_y(au, pair_recv[3, 1] + along_y(extra[0, -1], ky_last),
               pair_recv[2, 1] + along_y(extra[0, 1], ky_first))
    r1 = b7 - au
    x7 = (1.0 + keep_f) * u1 + gain_f * (e7[None] * r1)
    ax, ay = fine_xy(x7)
    side7 = fine_send_faces(ax, ay)
    az = fine_z(x7)
    local7 = ax + ay + az
    need("late")
    ci = tab("ci")[None]
    rest7 = (src - tab("cj")[None] * (ax + ci * az) - ci * ay) * keep7[None, None]
    jx = tab("jx").reshape(8, 4, 8, LANES)
    g = jx[0][None] * rest7[:, 0:1]
    for i in range(1, 8):
        g = g + jx[i][None] * rest7[:, i : i + 1]
    g = jnp.concatenate([g[0].reshape(32, LANES), g[1].reshape(32, LANES)], axis=1)
    g3 = left("jy", rdot(g, "down"))
    g3_all[0] = g3
    wide = Group(len(AROUND) - 1)
    for n, (dx, dy) in enumerate(AROUND):
        if n:
            wide.start(g3_all.at[0], g3_all.at[n], (-dx, -dy))
    rest7_all[0] = (b7 - fine_join(side7, local7)).reshape(128, LANES)
    told(1)
    ring1, ring2, ring3 = offsets(1), offsets(2), offsets(3)
    e3 = {dy: masked(dy, rtab("e3")[0], MID_ORDER, brow) for dy in range(-3, 4)}
    e3_all = jnp.concatenate([e3[dy] for _, dy in ring3], axis=0)
    tc, tab3 = rtab("tc")[0], rtab("tab")[0]
    n1, n2, n3 = 16 * len(ring1), 16 * len(ring2), 16 * len(ring3)

    def mid_z(v):
        return tab3 * rdot(v, "az3")

    wide.arrived()

    b3 = ldot("pick", g3_all[...].reshape(16 * len(AROUND), LANES))
    v1 = e3_all[:n1] * b3
    b3, e3 = b3[:16], e3[0]
    r1 = b3 - tc * ldot("lown", v1) - mid_z(v1[:16])
    x3 = (1.0 + keep_m) * v1[:16] + gain_m * (e3 * r1)
    ax, ay = left("lx", x3), left("ly", x3)
    ca, cb = rtab("ca")[0], rtab("cb")[0]
    part = keep3 * (g3 - cb * ax - ca * ay)
    other = keep3 * (ca * cb * tab3) * x3
    line = rdot(jnp.concatenate([part, -other], axis=1), "b12")
    line = jnp.sum(rtab("jj")[0] * line, axis=0, keepdims=True)
    line_send[0] = line

    lines = Group(ny)

    def line_copy(d, slot, to):
        return lines.make(d, line_send.at[0], line_recv.at[slot], {"cross": to})

    def far_first(n, size):
        step = lax.div(n + 1, 2)
        return size // 2 + step * (1 - 2 * lax.rem(n, 2))

    def line_out(n, carry):
        d = far_first(n, ny)
        line_copy(d, cx, lax.rem(cx + d, ny)).start()
        return carry

    def line_left(d, carry):
        line_copy(d, cx, cx).wait_send()
        return carry

    def line_arrived(n, carry):
        d = far_first(ny - 2 - n, ny)
        line_copy(d, lax.rem(cx + ny - d, ny), cx).wait_recv()
        return carry

    lax.fori_loop(0, ny - 1, line_out, 0)
    line_recv[cx] = line
    side3 = mid_start(ax, ay)
    x3_all[0] = x3
    side = [Group(len(ring) - 1) for ring in (ring2, ring1, ring3)]
    for n, (dx, dy) in enumerate(ring2):
        if n:
            side[0].start(x3_all.at[0], x3_all.at[n], (-dx, -dy))
    for n, (dx, dy) in enumerate(ring1):
        if n:
            side[1].start(rest7_all.at[0], rest7_all.at[n], (-dx, -dy))
    if ny < 32:
        line_recv[ny:] = jnp.zeros((32 - ny, 1, LANES), jnp.float32)
    rest3_all[0] = b3 - mid_join(side3, ax + ay + mid_z(x3))
    for n, (dx, dy) in enumerate(ring3):
        if n:
            side[2].start(rest3_all.at[0], rest3_all.at[n], (-dx, -dy))
    need("last")
    for group in first + [wide, side7]:
        group.left()
    lax.fori_loop(1, ny, line_left, 0)
    lax.fori_loop(0, ny - 1, line_arrived, 0)
    spectrum = ldot("sin", line_recv[:, 0, :])
    group = lax.div(lane, 32)
    for alpha in range(2):
        total = jnp.zeros((8, LANES), jnp.float32)
        for hi in range(4):
            for beta in range(2):
                piece = spectrum[(beta * 4 + hi) * 8 : (beta * 4 + hi + 1) * 8]
                shift = 32 * (hi - 2 * alpha - beta) % LANES
                if shift:
                    piece = pltpu.roll(piece, shift, 1)
                total = total + jnp.where(group == hi, piece, 0.0)
        mode_send[alpha] = total

    modes = Group(nx)

    def mode_copy(d, to):
        return modes.make(d, mode_send, mode_recv.at[d], {"stream": to})

    def mode_out(n, carry):
        d = far_first(n, nx)
        mode_copy(d, lax.rem(sx + d, nx)).start()
        return carry

    def mode_left(d, carry):
        mode_copy(d, sx).wait_send()
        return carry

    def mode_arrived(n, carry):
        mode_copy(far_first(nx - 2 - n, nx), sx).wait_recv()
        return carry

    lax.fori_loop(0, nx - 1, mode_out, 0)
    mode_recv[0] = mode_send[...]
    for group in side:
        group.arrived()
    for group in [side3] + side:
        group.left()
    lax.fori_loop(1, nx, mode_left, 0)
    lax.fori_loop(0, nx - 1, mode_arrived, 0)
    first = mode_recv[:, 0]
    second = mode_recv[:, 1]
    nodes = first + jnp.concatenate([second[1:], second[:1]], axis=0)
    start_g = where["green"][0]
    solved = [jnp.sum(tile_ref[start_g + n : start_g + n + nx] * nodes, axis=0)
              for n in range(SPAN)]
    sine = tile_ref[pl.ds(where["sine"][0] + cx, PAD)]
    window = [jnp.sum(sine * s[None], axis=1) for s in solved]
    window = jnp.concatenate(window, axis=0)
    window = rdot(window, "back")
    zval, zstiff = window[:, :LANES], window[:, LANES:]

    def per(table, count):
        return jnp.concatenate([table] * count, axis=0)

    from_low = ldot("kt", zval)
    r0 = rest3_all[...].reshape(n3, LANES) - per(tc, len(ring3)) * from_low[:n3]
    r0 = r0 - ldot("tt", zstiff)
    w1 = e3_all * r0
    aw = per(tc, len(ring2)) * ldot("lxy", w1)
    aw = aw + per(tab3, len(ring2)) * rdot(w1[:n2], "az3")
    x3 = x3_all[...].reshape(n2, LANES) + from_low[n3:]
    x3 = x3 + (1.0 + keep_m) * w1[:n2] + gain_m * (e3_all[:n2] * (r0[:n2] - aw))

    raised = rdot(x3, "upt")
    apx = ldot("fine", jnp.concatenate(
        [raised[:, : 2 * LANES], raised[:n1, 2 * LANES :]], axis=0))
    px = rdot(x3[:16], "up")
    px = jnp.stack([ldot("pfine", px[:, r * LANES : (r + 1) * LANES]) for r in range(2)])
    px = px.reshape(2, 8, 8, LANES)
    r0, u1 = [], []
    for n, (dx, dy) in enumerate(ring1):
        mine = apx[64 * n : 64 * n + 64]
        moved = jnp.stack([mine[:, r * LANES : (r + 1) * LANES] for r in range(2)])
        r0.append(rest7_all[n].reshape(2, 8, 8, LANES) - moved.reshape(2, 8, 8, LANES))
        scale = masked(dy, tab("e7"), ORDER, jrow[None]) if dy else e7
        u1.append(scale[None] * r0[n])

    ax, ay = fine_xy(u1[0])
    au = ax + ay + fine_z(u1[0])
    au = add_x(au, along_x(u1[2], 7), along_x(u1[1], 0))
    au = add_y(au, along_y(u1[4], ky_last), along_y(u1[3], ky_first))
    x7 = x7 + px
    out = x7 + (1.0 + keep_f) * u1[0] + gain_f * (e7[None] * (r0[0] - au))
    out_ref[...] = out.reshape(128, LANES)


def solution(mesh):
    nx, ny = mesh.shape["stream"], mesh.shape["cross"]
    tiles, blocks, where = build_tables(nx, ny)

    def body(sources):
        flat = sources.reshape(128, LANES)
        operands = [flat, jnp.asarray(tiles), jnp.asarray(blocks)]
        links, f32 = pltpu.SemaphoreType.DMA, jnp.float32
        out = pl.pallas_call(
            functools.partial(kernel, nx, ny, where),
            out_shape=jax.ShapeDtypeStruct((128, LANES), jnp.float32),
            in_specs=[pl.BlockSpec(memory_space=pl.ANY)] * len(operands),
            out_specs=pl.BlockSpec(memory_space=pltpu.VMEM),
            scratch_shapes=[pltpu.VMEM(o.shape, o.dtype) for o in operands]
            + [
                pltpu.VMEM((4, 2, 16, LANES), f32),
                pltpu.VMEM((4, 2, 16, LANES), f32),
                pltpu.VMEM((5, 16, LANES), f32),
                pltpu.VMEM((4, 2, 16, LANES), f32),
                pltpu.VMEM((4, 16, LANES), f32),
                pltpu.VMEM((4, 2, 1, LANES), f32),
                pltpu.VMEM((8, 2, 1, LANES), f32),
                pltpu.VMEM((len(AROUND), 16, LANES), f32),
                pltpu.VMEM((4, 16, LANES), f32),
                pltpu.VMEM((4, 16, LANES), f32),
                pltpu.VMEM((2, 16, LANES), f32),
                pltpu.VMEM((4, 16, LANES), f32),
                pltpu.VMEM((1, 1, LANES), f32),
                pltpu.VMEM((32, 1, LANES), f32),
                pltpu.VMEM((2, 8, LANES), f32),
                pltpu.VMEM((nx, 2, 8, LANES), f32),
                pltpu.VMEM((len(offsets(3)), 16, LANES), f32),
                pltpu.VMEM((len(offsets(2)), 16, LANES), f32),
                pltpu.VMEM((len(offsets(1)), 128, LANES), f32),
                links((5,)),
                links((LINKS + nx + ny,)),
                links((LINKS + nx + ny,)),
                pltpu.SemaphoreType.REGULAR((2, 2)),
            ],
            compiler_params=pltpu.CompilerParams(
                collective_id=0, has_side_effects=True, vmem_limit_bytes=VMEM_LIMIT),
            name="vcycle",
        )(*operands)
        return out.reshape(sources.shape)

    spec = P(None, "stream", "cross", None, None, None)
    return jax.shard_map(body, mesh=mesh, in_specs=(spec,), out_specs=spec, check_vma=False)
```

```python
import functools
import math

import jax
import jax.numpy as jnp
import ml_dtypes
import numpy as np
from jax import lax
from jax.experimental import pallas as pl
from jax.experimental.pallas import tpu as pltpu
from jax.sharding import PartitionSpec as P

ORDER = 7
MID_ORDER = 3
EZ = 16
LANES = 128
MODES = 32
MESH_ID = pl.DeviceIdType.MESH
FACES = ((1, 0), (-1, 0), (0, 1), (0, -1))
CORNERS = ((1, 1), (1, -1), (-1, 1), (-1, -1))
TWICE = ((2, 0), (-2, 0), (0, 2), (0, -2))
KNIGHTS = tuple((s * a, t * b) for a, b in ((2, 1), (1, 2)) for s in (1, -1) for t in (1, -1))
AROUND = ((0, 0),) + FACES + CORNERS + TWICE + KNIGHTS
VMEM_LIMIT = 55168 * 1024
WIDE, SPAN, PAD = 4, 10, 16


def legendre_pair(degree, points):
    below_poly = np.ones(points.shape)
    top_poly = points.copy()
    for step in range(2, degree + 1):
        below_poly, top_poly = (
            top_poly,
            ((2 * step - 1) * points * top_poly - (step - 1) * below_poly) / step,
        )
    return (below_poly, top_poly)


@functools.lru_cache(None)
def gll_tables(degree):
    nodes = -np.cos(np.pi * np.arange(degree + 1) / degree)
    for _ in range(100):
        below_poly, top_poly = legendre_pair(degree, nodes)
        nodes = nodes - (nodes * top_poly - below_poly) / ((degree + 1) * top_poly)
    at_nodes = legendre_pair(degree, nodes)[1]
    weights = 2.0 / (degree * (degree + 1) * at_nodes**2)
    count = degree + 1
    derivative = np.zeros((count, count))
    for target in range(count):
        for source in range(count):
            if target != source:
                derivative[target, source] = at_nodes[target] / (
                    at_nodes[source] * (nodes[target] - nodes[source])
                )
    derivative[0, 0] = -degree * (degree + 1) / 4.0
    derivative[degree, degree] = degree * (degree + 1) / 4.0
    stiffness = derivative.T @ (weights[:, None] * derivative)
    return (nodes, weights, stiffness)


def lagrange_matrix(fine_degree, coarse_degree):
    fine_nodes = gll_tables(fine_degree)[0]
    coarse_nodes = gll_tables(coarse_degree)[0]
    table = np.ones((fine_degree + 1, coarse_degree + 1))
    for column in range(coarse_degree + 1):
        for other in range(coarse_degree + 1):
            if other != column:
                table[:, column] *= (fine_nodes - coarse_nodes[other]) / (
                    coarse_nodes[column] - coarse_nodes[other]
                )
    return table


@functools.lru_cache(None)
def smoother(degree):
    stiffness = gll_tables(degree)[2]
    elements = 6
    size = elements * degree
    assembled = np.zeros((size, size))
    for element in range(elements):
        for row in range(degree + 1):
            for col in range(degree + 1):
                assembled[(element * degree + row) % size, (element * degree + col) % size] += (
                    stiffness[row, col]
                )
    diagonal = np.sqrt(np.diagonal(assembled))
    scaled = assembled / diagonal[:, None] / diagonal[None, :]
    positions = np.arange(size)
    vector = np.where(positions % 2 == 0, 1.0, -1.0) * (1.0 + positions / size)
    for _ in range(2000):
        vector = scaled @ vector
        vector = vector / np.sqrt(np.sum(vector * vector))
    high = float(np.sum(vector * (scaled @ vector)) / np.sum(vector * vector))
    low = 0.1 * high
    theta, delta = 0.5 * (high + low), 0.5 * (high - low)
    sigma = theta / delta
    rho1 = 1.0 / sigma
    rho2 = 1.0 / (2.0 * sigma - rho1)
    return theta, rho2 * rho1, 2.0 * rho2 / delta * theta


def level(degree):
    _, w, k = gll_tables(degree)
    t = w.copy()
    t[0] = t[-1] = w[0] + w[-1]
    s = np.diagonal(k).copy()
    s[0] = s[-1] = k[0, 0] + k[-1, -1]
    c = np.ones(degree + 1)
    c[0] = c[-1] = 0.5
    diag = (
        s[:, None, None] * t[None, :, None] * t[None, None, :]
        + t[:, None, None] * s[None, :, None] * t[None, None, :]
        + t[:, None, None] * t[None, :, None] * s[None, None, :]
    )
    return w, k, t, c, 1.0 / (diag * smoother(degree)[0])


def join_z(count):
    size = EZ * count
    m = np.eye(size)
    for e in range(EZ):
        a, b = e * count + count - 1, ((e + 1) % EZ) * count
        m[a, b] += 1.0
        m[b, a] += 1.0
    return m


def two(m):
    return np.kron(np.eye(2), m)


def lanes(values):
    return np.broadcast_to(values[None, :], (8, LANES))


def rows(values):
    return np.broadcast_to(np.asarray(values)[..., None], np.shape(values) + (LANES,))


def fourier_rows(total):
    k, n = np.meshgrid(np.arange(total), np.arange(total), indexing="ij")
    half = total // 2
    freq = np.where(k <= half, k, k - half)
    angle = 2.0 * np.pi * (freq * n % total) / total
    scale = np.where((k == 0) | (k == half), math.sqrt(1.0 / total), math.sqrt(2.0 / total))
    return scale * np.where(k <= half, np.cos(angle), np.sin(angle))


def sine_rows(mode, point, total):
    product = mode * point % (2 * total)
    inside = (mode > 0) & (mode < total) & (point > 0) & (point < total)
    return np.where(inside, math.sqrt(2.0 / total) * np.sin(np.pi * product / total), 0.0)


def green_table(nx, ny):
    mode = np.arange(MODES)
    wall_gap = 2.0 * np.sin(0.5 * np.pi * mode / ny) ** 2 + np.where(mode % ny == 0, 1.0, 0.0)
    freq = np.arange(EZ)
    freq = np.where(freq <= EZ // 2, freq, freq - EZ // 2)
    span_gap = 2.0 * np.sin(np.pi * freq / EZ) ** 2
    half_gap = wall_gap[:, None] + span_gap[None, :]
    root = np.sqrt(half_gap * (2.0 + half_gap))
    rate = np.log1p(half_gap + root)
    d = np.arange(nx)[:, None, None]
    top = np.exp(-rate * d) + np.exp(-rate * (nx - d))
    return top / (4.0 * root * -np.expm1(-rate * nx))


def modal(values):
    v = values.reshape(values.shape[:-2] + (MODES // 8, 8, EZ))
    v = np.stack([v, v], axis=-2)
    v = np.moveaxis(v, -4, -3)
    return v.reshape(v.shape[:-3] + (LANES,))


def offsets(radius):
    found = [(0, 0), *FACES]
    for ring in range(2, radius + 1):
        found += [
            (dx, dy)
            for dx in range(-ring, ring + 1)
            for dy in range(-ring, ring + 1)
            if abs(dx) + abs(dy) == ring
        ]
    return found


def assembled_1d(local_cols, window):
    count = local_cols.shape[0]
    out = np.zeros((count, window))
    out[:, 1:3] += local_cols
    out[0, 0:2] += local_cols[-1]
    out[-1, 2:4] += local_cols[0]
    return out


@functools.lru_cache(None)
def build_tables(nx, ny):
    f, q = ORDER + 1, MID_ORDER + 1
    w7, k7, t7, c7, e7 = level(ORDER)
    w3, k3, t3, c3, e3 = level(MID_ORDER)
    j73 = lagrange_matrix(ORDER, MID_ORDER)
    j31 = lagrange_matrix(MID_ORDER, 1)
    tile = {}
    tk = np.tile(t7, EZ)
    ones = np.ones((8, LANES))
    tile["kx"] = np.stack(
        [np.stack([k7[i, a] * t7[:, None] * tk[None, :] for i in range(f)]) for a in range(f)]
    ).reshape(f * f, 8, LANES)
    roll = np.stack([[k7[j, (j - s) % f] for j in range(f)] for s in range(f)])
    tile["ky"] = roll[:, :, None] * tk[None, None, :]
    tile["kyl"] = (k7[f - 1][:, None] * tk[None, :])[None]
    tile["kyf"] = (k7[0][:, None] * tk[None, :])[None]
    tile["e7"] = np.tile(e7, (1, 1, EZ))
    tile["ti"] = np.stack([t * ones for t in t7])
    tile["tij"] = np.stack([t * rows(t7) for t in t7])
    tile["cj"] = rows(c7)[None]
    tile["ci"] = np.stack([c * ones for c in c7])
    tile["jx"] = np.stack([j73[i, a] * ones for i in range(f) for a in range(q)])
    green = modal(green_table(nx, ny))
    tile["green"] = green[(np.arange(nx + SPAN - 1) - WIDE) % nx]
    point = np.arange(-WIDE, ny - WIDE + PAD)
    tile["sine"] = modal(
        np.broadcast_to(
            sine_rows(np.arange(MODES)[None, :], point[:, None], ny)[:, :, None],
            (len(point), MODES, EZ),
        )
    )
    row = {}
    mid = [(a, b) for a in range(q) for b in range(q)]
    tc = np.tile(np.tile(t3, EZ), 2)

    def left(matrix, scale=None):
        scale = np.ones(LANES) if scale is None else scale
        return matrix.T[:, :, None] * scale[None, None, :]

    row["jy"] = left(
        np.array([[(a == a2) * j73[j, b] for a2 in range(q) for j in range(f)] for a, b in mid])
    )
    row["lx"] = left(np.kron(k3, np.diag(t3)), tc)
    row["ly"] = left(np.kron(np.diag(t3), k3), tc)
    row["e3"] = np.stack([np.tile(np.tile(e3[a, b], EZ), 2) for a, b in mid])[None]
    row["tab"] = rows([t3[a] * t3[b] for a, b in mid])[None]
    row["ca"] = rows([c3[a] for a, b in mid])[None]
    row["cb"] = rows([c3[b] for a, b in mid])[None]
    groups = [np.array([j31[a, x] * j31[b, y] for a, b in mid]) for x in (0, 1) for y in (0, 1)]
    row["jj"] = np.repeat(np.stack(groups, axis=1), MODES, axis=1)[None]
    own = np.zeros((q, 4))
    own[:, 1:3] = j31
    stiff = assembled_1d(k3 @ j31, 4)
    mass = t3[:, None] * own

    ring1, ring2, ring3 = offsets(1), offsets(2), offsets(3)

    def placed(first, second, elements):
        out = np.zeros((len(elements), q, q, SPAN, PAD))
        for n, (dx, dy) in enumerate(elements):
            x0, y0 = dx - 1 + WIDE, dy - 1 + WIDE
            out[n, :, :, x0 : x0 + 4, y0 : y0 + 4] = np.einsum("at,bq->abtq", first, second)
        return out.reshape(len(elements) * q * q, SPAN * PAD)

    mat = {}
    mat["kt"] = np.concatenate(
        [placed(stiff, mass, ring3) + placed(mass, stiff, ring3), placed(own, own, ring2)])
    mat["tt"] = placed(mass, mass, ring3)
    cross = np.zeros((len(ring2), q, q, len(ring3), q, q))
    ends = {(1, 0): (3, 0), (-1, 0): (0, 3), (0, 1): (3, 0), (0, -1): (0, 3)}
    diag3 = np.diag(t3)
    for n, (dx, dy) in enumerate(ring2):
        cross[n, :, :, n] += np.einsum("ac,bd->abcd", k3, diag3)
        cross[n, :, :, n] += np.einsum("ac,bd->abcd", diag3, k3)
        for (fx, fy), (mine, theirs) in ends.items():
            m = ring3.index((dx + fx, dy + fy))
            line = np.zeros((q, q))
            line[mine] = k3[theirs]
            if fx:
                cross[n, :, :, m] += np.einsum("ac,bd->abcd", line, diag3)
            else:
                cross[n, :, :, m] += np.einsum("ac,bd->abcd", diag3, line)
    pick = np.zeros((len(ring1), q, q, 144))
    for n, (dx, dy) in enumerate(ring1):
        for gx, gy in AROUND:
            sx, sy = gx - dx, gy - dy
            if max(abs(sx), abs(sy)) > 1:
                continue
            span_x = [(a, a) for a in range(q)] if sx == 0 else [(q - 1, 0) if sx > 0 else (0, q - 1)]
            span_y = [(b, b) for b in range(q)] if sy == 0 else [(q - 1, 0) if sy > 0 else (0, q - 1)]
            for a, a2 in span_x:
                for b, b2 in span_y:
                    d = (gx, gy)
                    if d in ring1:
                        column = 16 * ring1.index(d) + 4 * a2 + b2
                    elif d in CORNERS:
                        part = (d[0] != d[1]) if sx else (d[0] == d[1])
                        column = 80 + 8 * CORNERS.index(d) + 4 * part + (b2 if sx else a2)
                    elif d in TWICE:
                        column = 112 + 4 * TWICE.index(d) + (b2 if sx else a2)
                    else:
                        column = 128 + KNIGHTS.index(d)
                    pick[n, a, b, column] = 1.0
    mat["pick"] = pick.reshape(len(ring1) * 16, 144)
    mat["lxy"] = cross.reshape(len(ring2) * 16, len(ring3) * 16)
    k7j = k7 @ j73
    t7j = t7[:, None] * j73
    fine = np.zeros((len(ring1), f, f, len(ring2), q, q))
    own_z = np.zeros((len(ring1), f, f, len(ring1), q, q))
    for n, (dx, dy) in enumerate(ring1):
        fine[n, :, :, n] += np.einsum("ia,jb->ijab", k7j, t7j) + np.einsum("ia,jb->ijab", t7j, k7j)
        own_z[n, :, :, n] = np.einsum("ia,jb->ijab", t7j, t7j)
        for (fx, fy), (mine, theirs) in ends.items():
            mine, theirs = (f - 1 if mine else 0), (f - 1 if theirs else 0)
            m = ring2.index((dx + fx, dy + fy))
            if fx:
                fine[n, mine, :, m] += np.einsum("a,jb->jab", k7j[theirs], t7j)
            else:
                fine[n, :, mine, m] += np.einsum("ia,b->iab", t7j, k7j[theirs])
    count = len(ring1) * f * f
    mat["fine"] = np.concatenate([fine.reshape(count, -1), own_z.reshape(count, -1)], axis=1)
    mat["lown"] = mat["lxy"][:16, : 16 * len(ring1)]
    mat["pfine"] = np.einsum("ia,jb->ijab", j73, j73).reshape(f * f, 16)
    row["tc"] = np.broadcast_to(tc, (1, 16, LANES))
    az7 = (join_z(f) @ np.kron(np.eye(EZ), k7)).T
    az3 = two((join_z(q) @ np.kron(np.eye(EZ), k3)).T)
    down = (join_z(q) @ np.kron(np.eye(EZ), j73.T) @ np.diag(np.tile(c7, EZ))).T
    zero = np.zeros_like(down)
    mat["az7"] = az7
    mat["down"] = np.concatenate(
        [np.concatenate([down, zero], axis=1), np.concatenate([zero, down], axis=1)], axis=0
    )
    mat["az3"] = az3
    up = np.kron(np.eye(EZ), j73).T
    mat["up"] = two(up)
    up_tk = up * np.tile(t7, EZ)[None]
    mat["upt"] = np.concatenate([two(up_tk), two(up @ az7)], axis=1)
    gather = np.zeros((EZ, EZ * q))
    for e in range(EZ):
        for node in (0, 1):
            gather[(e + node) % EZ, e * q : (e + 1) * q] += j31[:, node] * c3
    b1 = two((fourier_rows(EZ) @ gather).T)
    b1 = np.tile(b1, (1, 4))
    mat["b12"] = np.concatenate([b1, az3 @ b1], axis=0)
    spread = np.zeros((EZ * q, EZ))
    for e in range(EZ):
        for node in (0, 1):
            spread[e * q : (e + 1) * q, (e + node) % EZ] += j31[:, node]
    back = two((spread @ fourier_rows(EZ).T).T)
    back = np.tile(back, (4, 1))
    mat["back"] = np.concatenate([back, back @ az3], axis=1)
    mode, here = np.arange(MODES)[:, None], np.arange(32)[None, :]
    s0 = np.where(here < ny, sine_rows(mode, here, ny), 0.0)
    s1 = np.where(here < ny, sine_rows(mode, here + 1, ny), 0.0)
    mat["sin"] = np.concatenate([s0, s1], axis=0)
    where, tiles, at = {}, [], 0
    for name in EARLY + LATE + tuple(row):
        value = tile[name] if name in tile else row[name].reshape(-1, 8, LANES)
        where[name] = (at, value.shape[0])
        tiles.append(value.astype(np.float32))
        at += value.shape[0]
    blocks, at = [], 0
    for name in MATS:
        value = mat[name].astype(np.float32)
        top = value.astype(ml_dtypes.bfloat16)
        rest = (value - top.astype(np.float32)).astype(ml_dtypes.bfloat16)
        parts = [top, top] if name == "pick" else [top, rest, top]
        value = np.concatenate(parts, axis=0 if name in RIGHT else 1)
        height, width = value.shape
        count = -(-width // LANES)
        value = np.pad(value, ((0, 0), (0, count * LANES - width)))
        where[name] = (at, height, width)
        blocks += [value[:, LANES * n : LANES * n + LANES] for n in range(count)]
        at += height * count
    return np.concatenate(tiles), np.concatenate(blocks), where


EARLY = ("e7", "kx", "kyl", "kyf", "ti", "ky", "tij")
LATE = ("cj", "ci", "jx", "green", "sine")
RIGHT = ("az7", "down", "az3", "b12", "back", "up", "upt")
MATS = ("az7", "down", "pick", "lown", "az3", "b12", "sin", "back", "kt", "tt", "lxy", "up", "upt",
        "fine", "pfine")
LINKS = 20 + 4 + 20 + 4 + 12 + 4 + 24


def reach(n):
    base = max(n // 8, 1)
    known, hops = base, []
    while known < n // 2:
        hops.append(known)
        known *= 2
    return range(1, base + 1), hops


def mean_hops(d, size):
    def ring(a, b):
        return min((a - b) % 4, (b - a) % 4)

    total = 0
    for p in range(size):
        t = (p + d) % size
        total += ring(p // 8, t // 8) + ring(p // 2 % 4, t // 2 % 4) + 0.5 * (p % 2 != t % 2)
    return total


def kernel(nx, ny, where, *refs):
    hbm, out_ref, vmem = refs[:3], refs[3], refs[4:7]
    (pair_send, pair_recv, edge_send, corner_recv, twice_recv, knight_send, knight_recv, g3_all,
     edge3_send, corner3_recv, twice3_recv, knight3_send, knight3_recv, line7_send, line7_recv,
     fine_send, fine_recv, mid_send, mid_recv, line_send, line_recv, mode_send, mode_recv,
     rest3_all, x3_all, load_sem, send_sem, recv_sem, known) = refs[7:]
    sx, cx = lax.axis_index("stream"), lax.axis_index("cross")
    tile_ref, block_ref = vmem[1:]

    def at(dx, dy):
        return {"stream": lax.rem(sx + (nx + dx), nx), "cross": lax.rem(cx + (ny + dy), ny)}

    def tab(name):
        start, size = where[name]
        return tile_ref[start : start + size]

    def rtab(name):
        return tab(name).reshape(-1, 16, LANES)

    def mat(name):
        start, height, width = where[name]
        parts = [block_ref[start + n * height : start + (n + 1) * height]
                 for n in range(-(-width // LANES))]
        return (parts[0] if len(parts) == 1 else jnp.concatenate(parts, axis=1))[:, :width]

    bar = pltpu.get_barrier_semaphore()
    faces = FACES
    near_x, hops_x = reach(nx)
    near_y, hops_y = reach(ny)
    near = list(KNIGHTS + CORNERS)
    near += [(s * d, 0) for d in reversed(near_x) for s in (1, -1)]
    near += [(0, s * d) for d in reversed(near_y) for s in (1, -1)]
    for d in near:
        pl.semaphore_signal(bar, inc=1, device_id=at(*d), device_id_type=MESH_ID)
    late, last = where[LATE[0]][0], where["sin"][0]
    spans = {"x": (0, 0, 128), "early": (1, 0, late), "late": (1, late, hbm[1].shape[0]),
             "first": (2, 0, last), "last": (2, last, hbm[2].shape[0])}
    loads = {}

    def load(*wanted):
        for name in wanted:
            operand, start, end = spans[name]
            part = pl.ds(start, end - start)
            loads[name] = pltpu.make_async_copy(
                hbm[operand].at[part], vmem[operand].at[part], load_sem.at[list(spans).index(name)])
            loads[name].start()

    load("x", "early")

    def need(*wanted):
        for name in wanted:
            if name in loads:
                loads.pop(name).wait()

    def tell(step):
        for n, hops in enumerate((hops_x, hops_y)):
            if step < len(hops):
                for s in (1, -1):
                    d = (s * hops[step], 0) if n == 0 else (0, s * hops[step])
                    pl.semaphore_signal(
                        known.at[step, n], inc=1, device_id=at(*d), device_id_type=MESH_ID)

    def told(step):
        for n, hops in enumerate((hops_x, hops_y)):
            if step < len(hops):
                pl.semaphore_wait(known.at[step, n], 2)

    used = [0]

    class Group:
        def __init__(self, size):
            self.base, self.copies = used[0], []
            used[0] += size

        def make(self, n, src, dst, device):
            return pltpu.make_async_remote_copy(
                src, dst, send_sem.at[self.base + n], recv_sem.at[self.base + n],
                device_id=device, device_id_type=MESH_ID)

        def start(self, src, dst, to):
            copy = self.make(len(self.copies), src, dst, at(*to))
            copy.start()
            self.copies.append(copy)

        def arrived(self):
            for copy in self.copies:
                copy.wait_recv()

        def left(self):
            for copy in self.copies:
                copy.wait_send()

    jrow = lax.broadcasted_iota(jnp.int32, (8, LANES), 0)
    lane = lax.broadcasted_iota(jnp.int32, (8, LANES), 1)
    low_wall = jnp.where(cx == 0, 0, -1)
    high_wall = jnp.where(cx == ny - 1, ORDER, -1)
    keep7 = jnp.where((jrow == low_wall) | (jrow == high_wall), 0.0, 1.0)
    mrow = lax.broadcasted_iota(jnp.int32, (16, LANES), 0)
    brow = lax.rem(mrow, 4)
    high_wall3 = jnp.where(cx == ny - 1, MID_ORDER, -1)
    keep3 = jnp.where((brow == low_wall) | (brow == high_wall3), 0.0, 1.0)
    _, keep_f, gain_f = smoother(ORDER)
    _, keep_m, gain_m = smoother(MID_ORDER)

    def halves(a):
        top = a.astype(jnp.bfloat16)
        return top, (a - top.astype(jnp.float32)).astype(jnp.bfloat16)

    def rdot(a, name):
        top, rest = halves(a)
        return jnp.dot(jnp.concatenate([top, top, rest], axis=1), mat(name),
                       preferred_element_type=jnp.float32)

    def ldot(name, b):
        top, rest = halves(b)
        parts = [top, rest] if name == "pick" else [top, top, rest]
        return jnp.dot(mat(name), jnp.concatenate(parts, axis=0),
                       preferred_element_type=jnp.float32)

    def fine_xy(u):
        kx = tab("kx").reshape(8, 8, 8, LANES)
        ax = kx[0][None] * u[:, 0:1]
        for a in range(1, 8):
            ax = ax + kx[a][None] * u[:, a : a + 1]
        ky = tab("ky")
        flat = u.reshape(16, 8, LANES)
        ay = ky[0][None] * flat
        for s in range(1, 8):
            ay = ay + ky[s][None] * pltpu.roll(flat, s, 1)
        return ax, ay.reshape(2, 8, 8, LANES) * tab("ti")[None]

    def fine_z(u):
        az = rdot(u.reshape(128, LANES), "az7")
        return az.reshape(2, 8, 8, LANES) * tab("tij")[None]

    def fine_send_faces(ax, ay):
        fine_send[0] = ax[:, 7].reshape(16, LANES)
        fine_send[1] = ax[:, 0].reshape(16, LANES)
        flat = ay.reshape(16, 8, LANES)
        fine_send[2] = flat[:, 7, :]
        fine_send[3] = flat[:, 0, :]
        group = Group(4)
        for d in range(4):
            group.start(fine_send.at[d], fine_recv.at[d], faces[d])
        return group

    def add_x(field, low, high):
        return jnp.concatenate(
            [field[:, 0:1] + low.reshape(2, 1, 8, LANES), field[:, 1:7],
             field[:, 7:8] + high.reshape(2, 1, 8, LANES)], axis=1)

    def add_y(field, low, high):
        flat = field.reshape(16, 8, LANES)
        flat = flat + jnp.where(jrow[None] == 0, low[:, None, :], 0.0)
        flat = flat + jnp.where(jrow[None] == 7, high[:, None, :], 0.0)
        return flat.reshape(2, 8, 8, LANES)

    def fine_join(group, field):
        group.arrived()
        field = add_x(field, fine_recv[0], fine_recv[1])
        return add_y(field, fine_recv[2], fine_recv[3])

    def left(name, v):
        start_row, size = where[name]
        acc = 0.0
        for c in range(size // 2):
            both = tile_ref[start_row + 2 * c : start_row + 2 * c + 2].reshape(16, LANES)
            acc = acc + both * v[c : c + 1]
        return acc

    def mid_start(ax, ay):
        mid_send[0] = ax
        mid_send[1] = ay
        group = Group(4)
        for d in range(4):
            group.start(mid_send.at[d // 2], mid_recv.at[d], faces[d])
        return group

    def shifted(v, shift, mask):
        return jnp.where(mask, pltpu.roll(v, shift, 0), 0.0)

    def mid_join(group, field):
        group.arrived()
        field = field + shifted(mid_recv[0], 4, mrow < 4)
        field = field + shifted(mid_recv[1], 12, mrow >= 12)
        field = field + shifted(mid_recv[2], 13, brow == 0)
        return field + shifted(mid_recv[3], 3, brow == 3)

    def masked(dy, table, top, index):
        low = jnp.where(cx + dy == 0, 0, -1)
        high = jnp.where(cx + dy == ny - 1, top, -1)
        return table * jnp.where((index == low) | (index == high), 0.0, 1.0)

    def along_x(u, row):
        acc = kx[0][row][None] * u[:, 0]
        for a in range(1, 8):
            acc = acc + kx[a][row][None] * u[:, a]
        return acc.reshape(16, LANES)

    def along_y(u, table):
        weighted = jnp.sum(table[None] * u, axis=2)
        return (tab("ti")[:, 0][None] * weighted).reshape(16, LANES)

    need("x")
    src = vmem[0][...].reshape(16, 8, LANES)
    knode = lax.rem(lane, 8)
    src = (src + jnp.where(knode[None] == 7, pltpu.roll(src, LANES - 1, 2), 0.0)
           + jnp.where(knode[None] == 0, pltpu.roll(src, 1, 2), 0.0))
    y7, y0 = src[:, 7, :], src[:, 0, :]
    src = src.reshape(2, 8, 8, LANES)
    x7, x0 = src[:, 7].reshape(16, LANES), src[:, 0].reshape(16, LANES)
    for n, edge in enumerate((x7, y7, x0, y0, x7)):
        edge_send[n] = edge
    for i, row in ((1, 7), (0, 0)):
        for j, line in ((1, y7), (0, y0)):
            knight_send[2 * i + j] = line.reshape(2, 8, LANES)[:, row : row + 1]
    need("early")
    e7 = masked(0, tab("e7"), ORDER, jrow[None])
    kx = tab("kx").reshape(8, 8, 8, LANES)
    ky_last, ky_first = tab("kyl"), tab("kyf")
    scaled = e7[None] * src
    pairs = ((x0, along_x(scaled, 0)), (x7, along_x(scaled, 7)),
             (y0, along_y(scaled, ky_first)), (y7, along_y(scaled, ky_last)))
    for n, (raw, contracted) in enumerate(pairs):
        pair_send[n, 0] = raw
        pair_send[n, 1] = contracted
    pl.semaphore_wait(bar, len(near))
    tell(0)
    first = [Group(size) for size in (8, 4, 4, 4)]
    for n, (dx, dy) in enumerate(KNIGHTS):
        first[0].start(knight_send.at[2 * (dx < 0) + (dy < 0)], knight_recv.at[n], (-dx, -dy))
    pick_edge = {(1, 1): 2, (1, -1): 1, (-1, 1): 3, (-1, -1): 0}
    for n, d in enumerate(CORNERS):
        first[1].start(edge_send.at[pick_edge[d] : pick_edge[d] + 2], corner_recv.at[n],
                       (-d[0], -d[1]))
    for n, (dx, dy) in enumerate(TWICE):
        first[2].start(edge_send.at[(2, 0, 3, 1)[n]], twice_recv.at[n], (-dx, -dy))
    for n, (dx, dy) in enumerate(FACES):
        first[3].start(pair_send.at[n], pair_recv.at[n], (-dx, -dy))
    load("first", "late", "last")
    need("first")
    for group in first:
        group.arrived()
    told(0)
    tell(1)
    irow = jrow[None]

    def lines_of(value):
        return value.reshape(2, 8, LANES)

    def row_of(value, row):
        return lines_of(value)[:, row : row + 1]

    def with_ends(line, first, last):
        line = lines_of(line) + jnp.where(irow == 0, first, 0.0) + jnp.where(irow == 7, last, 0.0)
        return line.reshape(16, LANES)

    knight = {d: knight_recv[n] for n, d in enumerate(KNIGHTS)}
    twice = {d: twice_recv[n] for n, d in enumerate(TWICE)}
    raw = {d: pair_recv[n, 0] for n, d in enumerate(FACES)}
    corner_x = {d: corner_recv[n, 0 if d[0] == d[1] else 1] for n, d in enumerate(CORNERS)}
    corner_y = {d: corner_recv[n, 1 if d[0] == d[1] else 0] for n, d in enumerate(CORNERS)}

    def joined(center, low_x, high_x, low_y, high_y):
        return add_y(add_x(center, low_x, high_x), low_y, high_y)

    b7 = joined(
        src, raw[-1, 0], raw[1, 0],
        with_ends(raw[0, -1], row_of(corner_y[-1, -1], 7), row_of(corner_y[1, -1], 0)),
        with_ends(raw[0, 1], row_of(corner_y[-1, 1], 7), row_of(corner_y[1, 1], 0)))
    zero = jnp.zeros_like(src)
    extra = {
        (1, 0): joined(
            zero, x7, twice[2, 0],
            with_ends(corner_y[1, -1], row_of(raw[0, -1], 7), knight[2, -1]),
            with_ends(corner_y[1, 1], row_of(raw[0, 1], 7), knight[2, 1])),
        (-1, 0): joined(
            zero, twice[-2, 0], x0,
            with_ends(corner_y[-1, -1], knight[-2, -1], row_of(raw[0, -1], 0)),
            with_ends(corner_y[-1, 1], knight[-2, 1], row_of(raw[0, 1], 0))),
        (0, 1): joined(
            zero, corner_x[-1, 1], corner_x[1, 1],
            with_ends(y7, row_of(raw[-1, 0], 7), row_of(raw[1, 0], 7)),
            with_ends(twice[0, 2], knight[-1, 2], knight[1, 2])),
        (0, -1): joined(
            zero, corner_x[-1, -1], corner_x[1, -1],
            with_ends(twice[0, -2], knight[-1, -2], knight[1, -2]),
            with_ends(y0, row_of(raw[-1, 0], 0), row_of(raw[1, 0], 0))),
    }
    e7_of = {0: e7}
    for dy in (1, -1):
        e7_of[dy] = masked(dy, tab("e7"), ORDER, jrow[None])
    extra = {d: e7_of[d[1]][None] * v for d, v in extra.items()}

    u1 = e7[None] * b7
    ax, ay = fine_xy(u1)
    au = add_x(ax + ay + fine_z(u1), pair_recv[1, 1] + along_x(extra[-1, 0], 7),
               pair_recv[0, 1] + along_x(extra[1, 0], 0))
    au = add_y(au, pair_recv[3, 1] + along_y(extra[0, -1], ky_last),
               pair_recv[2, 1] + along_y(extra[0, 1], ky_first))
    r1 = b7 - au
    x7 = (1.0 + keep_f) * u1 + gain_f * (e7[None] * r1)
    ax, ay = fine_xy(x7)
    side7 = fine_send_faces(ax, ay)
    az = fine_z(x7)
    local7 = ax + ay + az
    need("late")
    ci = tab("ci")[None]
    rest7 = (src - tab("cj")[None] * (ax + ci * az) - ci * ay) * keep7[None, None]
    jx = tab("jx").reshape(8, 4, 8, LANES)
    g = jx[0][None] * rest7[:, 0:1]
    for i in range(1, 8):
        g = g + jx[i][None] * rest7[:, i : i + 1]
    g = jnp.concatenate([g[0].reshape(32, LANES), g[1].reshape(32, LANES)], axis=1)
    g3 = left("jy", rdot(g, "down"))
    g3_all[0] = g3
    by_a = g3.reshape(4, 4, LANES)
    for n, edge in enumerate((by_a[3], by_a[:, 3], by_a[0], by_a[:, 0], by_a[3])):
        edge3_send[n] = edge
    for i, row in ((1, 12), (0, 0)):
        for j in (0, 1):
            knight3_send[2 * i + j] = g3[row + 3 * j : row + 3 * j + 1]
    wide = Group(len(AROUND) - 1)
    for n, (dx, dy) in enumerate(KNIGHTS):
        wide.start(knight3_send.at[2 * (dx < 0) + (dy < 0)], knight3_recv.at[n], (-dx, -dy))
    for n, d in enumerate(CORNERS):
        wide.start(edge3_send.at[pick_edge[d] : pick_edge[d] + 2], corner3_recv.at[n],
                   (-d[0], -d[1]))
    for n, (dx, dy) in enumerate(TWICE):
        wide.start(edge3_send.at[(2, 0, 3, 1)[n]], twice3_recv.at[n], (-dx, -dy))
    for n, (dx, dy) in enumerate(FACES):
        wide.start(g3_all.at[0], g3_all.at[n + 1], (-dx, -dy))
    rest7 = b7 - fine_join(side7, local7)
    scaled = e7[None] * rest7
    line7_send[0] = along_x(scaled, 0)
    line7_send[1] = along_x(scaled, 7)
    line7_send[2] = along_y(scaled, ky_first)
    line7_send[3] = along_y(scaled, ky_last)
    told(1)
    ring1, ring2, ring3 = offsets(1), offsets(2), offsets(3)
    e3 = {dy: masked(dy, rtab("e3")[0], MID_ORDER, brow) for dy in range(-3, 4)}
    e3_all = jnp.concatenate([e3[dy] for _, dy in ring3], axis=0)
    tc, tab3 = rtab("tc")[0], rtab("tab")[0]
    n1, n2, n3 = 16 * len(ring1), 16 * len(ring2), 16 * len(ring3)

    def mid_z(v):
        return tab3 * rdot(v, "az3")

    wide.arrived()

    b3 = ldot("pick", jnp.concatenate(
        [g3_all[...].reshape(80, LANES), corner3_recv[...].reshape(32, LANES),
         twice3_recv[...].reshape(16, LANES), knight3_recv[:, 0, :],
         jnp.zeros((8, LANES), jnp.float32)], axis=0))
    v1 = e3_all[:n1] * b3
    b3, e3 = b3[:16], e3[0]
    r1 = b3 - tc * ldot("lown", v1) - mid_z(v1[:16])
    x3 = (1.0 + keep_m) * v1[:16] + gain_m * (e3 * r1)
    ax, ay = left("lx", x3), left("ly", x3)
    ca, cb = rtab("ca")[0], rtab("cb")[0]
    part = keep3 * (g3 - cb * ax - ca * ay)
    other = keep3 * (ca * cb * tab3) * x3
    line = rdot(jnp.concatenate([part, -other], axis=1), "b12")
    line = jnp.sum(rtab("jj")[0] * line, axis=0, keepdims=True)
    line_send[0] = line

    lines = Group(ny)

    def line_copy(d, slot, to):
        return lines.make(d, line_send.at[0], line_recv.at[slot], {"cross": to})

    def far_first(n, size):
        step = lax.div(n + 1, 2)
        return size // 2 + step * (1 - 2 * lax.rem(n, 2))

    def line_left(d, carry):
        line_copy(d, cx, cx).wait_send()
        return carry

    def line_arrived(n, carry):
        d = far_first(ny - 2 - n, ny)
        line_copy(d, lax.rem(cx + ny - d, ny), cx).wait_recv()
        return carry

    for n in range(ny - 1):
        d = ny // 2 + (n + 1) // 2 * (1 - 2 * (n % 2))
        line_copy(d, cx, lax.rem(cx + d, ny)).start()
    line_recv[cx] = line
    side3 = mid_start(ax, ay)
    x3_all[0] = x3
    side = [Group(len(ring) - 1) for ring in (ring2, ring1, ring3)]
    for n, (dx, dy) in enumerate(ring2):
        if n:
            side[0].start(x3_all.at[0], x3_all.at[n], (-dx, -dy))
    for n, (dx, dy) in enumerate(FACES):
        side[1].start(line7_send.at[n], line7_recv.at[n], (-dx, -dy))
    if ny < 32:
        line_recv[ny:] = jnp.zeros((32 - ny, 1, LANES), jnp.float32)
    rest3_all[0] = b3 - mid_join(side3, ax + ay + mid_z(x3))
    for n, (dx, dy) in enumerate(ring3):
        if n:
            side[2].start(rest3_all.at[0], rest3_all.at[n], (-dx, -dy))
    need("last")
    for group in first + [wide, side7]:
        group.left()
    lax.fori_loop(1, ny, line_left, 0)
    lax.fori_loop(0, ny - 1, line_arrived, 0)
    spectrum = ldot("sin", line_recv[:, 0, :])
    group = lax.div(lane, 32)
    for alpha in range(2):
        total = jnp.zeros((8, LANES), jnp.float32)
        for hi in range(4):
            for beta in range(2):
                piece = spectrum[(beta * 4 + hi) * 8 : (beta * 4 + hi + 1) * 8]
                shift = 32 * (hi - 2 * alpha - beta) % LANES
                if shift:
                    piece = pltpu.roll(piece, shift, 1)
                total = total + jnp.where(group == hi, piece, 0.0)
        mode_send[alpha] = total

    modes = Group(nx)

    def mode_copy(d, to):
        return modes.make(d, mode_send, mode_recv.at[d], {"stream": to})

    def mode_left(d, carry):
        mode_copy(d, sx).wait_send()
        return carry

    by_hops = sorted(range(1, nx), key=lambda d: mean_hops(d, nx))
    for d in reversed(by_hops):
        mode_copy(d, lax.rem(sx + d, nx)).start()
    mode_recv[0] = mode_send[...]
    for group in side:
        group.arrived()
    for group in [side3] + side:
        group.left()
    lax.fori_loop(1, nx, mode_left, 0)
    for d in by_hops:
        mode_copy(d, sx).wait_recv()
    first = mode_recv[:, 0]
    second = mode_recv[:, 1]
    nodes = first + jnp.concatenate([second[1:], second[:1]], axis=0)
    start_g = where["green"][0]
    solved = [jnp.sum(tile_ref[start_g + n : start_g + n + nx] * nodes, axis=0)
              for n in range(SPAN)]
    sine = tile_ref[pl.ds(where["sine"][0] + cx, SPAN)]
    blank = jnp.zeros((PAD - SPAN, LANES), jnp.float32)
    window = []
    for s in solved:
        window += [jnp.sum(sine * s[None], axis=1), blank]
    window = jnp.concatenate(window, axis=0)
    window = rdot(window, "back")
    zval, zstiff = window[:, :LANES], window[:, LANES:]

    def per(table, count):
        return jnp.concatenate([table] * count, axis=0)

    from_low = ldot("kt", zval)
    r0 = rest3_all[...].reshape(n3, LANES) - per(tc, len(ring3)) * from_low[:n3]
    r0 = r0 - ldot("tt", zstiff)
    w1 = e3_all * r0
    aw = per(tc, len(ring2)) * ldot("lxy", w1)
    aw = aw + per(tab3, len(ring2)) * rdot(w1[:n2], "az3")
    x3 = x3_all[...].reshape(n2, LANES) + from_low[n3:]
    x3 = x3 + (1.0 + keep_m) * w1[:n2] + gain_m * (e3_all[:n2] * (r0[:n2] - aw))

    raised = rdot(x3, "upt")
    apx = ldot("fine", jnp.concatenate(
        [raised[:, : 2 * LANES], raised[:n1, 2 * LANES :]], axis=0))
    px = rdot(x3[:16], "up")
    px = jnp.stack([ldot("pfine", px[:, r * LANES : (r + 1) * LANES]) for r in range(2)])
    px = px.reshape(2, 8, 8, LANES)
    moved = []
    for n in range(len(ring1)):
        mine = apx[64 * n : 64 * n + 64]
        mine = jnp.stack([mine[:, r * LANES : (r + 1) * LANES] for r in range(2)])
        moved.append(mine.reshape(2, 8, 8, LANES))
    r0 = rest7 - moved[0]
    u1 = e7[None] * r0
    right, left_, above, below = [e7_of[dy][None] * moved[n + 1] for n, (_, dy) in enumerate(FACES)]
    ax, ay = fine_xy(u1)
    au = ax + ay + fine_z(u1)
    au = add_x(au, line7_recv[1] - along_x(left_, 7), line7_recv[0] - along_x(right, 0))
    au = add_y(au, line7_recv[3] - along_y(below, ky_last),
               line7_recv[2] - along_y(above, ky_first))
    x7 = x7 + px
    out = x7 + (1.0 + keep_f) * u1 + gain_f * (e7[None] * (r0 - au))
    out_ref[...] = out.reshape(128, LANES)


def solution(mesh):
    nx, ny = mesh.shape["stream"], mesh.shape["cross"]
    tiles, blocks, where = build_tables(nx, ny)

    def body(sources):
        flat = sources.reshape(128, LANES)
        operands = [flat, jnp.asarray(tiles), jnp.asarray(blocks)]
        links, f32 = pltpu.SemaphoreType.DMA, jnp.float32
        out = pl.pallas_call(
            functools.partial(kernel, nx, ny, where),
            out_shape=jax.ShapeDtypeStruct((128, LANES), jnp.float32),
            in_specs=[pl.BlockSpec(memory_space=pl.ANY)] * len(operands),
            out_specs=pl.BlockSpec(memory_space=pltpu.VMEM),
            scratch_shapes=[pltpu.VMEM(o.shape, o.dtype) for o in operands]
            + [
                pltpu.VMEM((4, 2, 16, LANES), f32),
                pltpu.VMEM((4, 2, 16, LANES), f32),
                pltpu.VMEM((5, 16, LANES), f32),
                pltpu.VMEM((4, 2, 16, LANES), f32),
                pltpu.VMEM((4, 16, LANES), f32),
                pltpu.VMEM((4, 2, 1, LANES), f32),
                pltpu.VMEM((8, 2, 1, LANES), f32),
                pltpu.VMEM((5, 16, LANES), f32),
                pltpu.VMEM((5, 4, LANES), f32),
                pltpu.VMEM((4, 2, 4, LANES), f32),
                pltpu.VMEM((4, 4, LANES), f32),
                pltpu.VMEM((4, 1, LANES), f32),
                pltpu.VMEM((8, 1, LANES), f32),
                pltpu.VMEM((4, 16, LANES), f32),
                pltpu.VMEM((4, 16, LANES), f32),
                pltpu.VMEM((4, 16, LANES), f32),
                pltpu.VMEM((4, 16, LANES), f32),
                pltpu.VMEM((2, 16, LANES), f32),
                pltpu.VMEM((4, 16, LANES), f32),
                pltpu.VMEM((1, 1, LANES), f32),
                pltpu.VMEM((32, 1, LANES), f32),
                pltpu.VMEM((2, 8, LANES), f32),
                pltpu.VMEM((nx, 2, 8, LANES), f32),
                pltpu.VMEM((len(offsets(3)), 16, LANES), f32),
                pltpu.VMEM((len(offsets(2)), 16, LANES), f32),
                links((5,)),
                links((LINKS + nx + ny,)),
                links((LINKS + nx + ny,)),
                pltpu.SemaphoreType.REGULAR((2, 2)),
            ],
            compiler_params=pltpu.CompilerParams(
                collective_id=0, has_side_effects=True, vmem_limit_bytes=VMEM_LIMIT),
            name="vcycle",
        )(*operands)
        return out.reshape(sources.shape)

    spec = P(None, "stream", "cross", None, None, None)
    return jax.shard_map(body, mesh=mesh, in_specs=(spec,), out_specs=spec, check_vma=False)
```

```python
import functools
import math

import jax
import jax.numpy as jnp
import ml_dtypes
import numpy as np
from jax import lax
from jax.experimental import pallas as pl
from jax.experimental.pallas import tpu as pltpu
from jax.sharding import PartitionSpec as P

ORDER = 7
MID_ORDER = 3
EZ = 16
LANES = 128
MODES = 32
MESH_ID = pl.DeviceIdType.MESH
FACES = ((1, 0), (-1, 0), (0, 1), (0, -1))
CORNERS = ((1, 1), (1, -1), (-1, 1), (-1, -1))
TWICE = ((2, 0), (-2, 0), (0, 2), (0, -2))
KNIGHTS = tuple((s * a, t * b) for a, b in ((1, 2), (2, 1)) for s in (1, -1) for t in (1, -1))
AROUND = ((0, 0),) + FACES + CORNERS + TWICE + KNIGHTS
VMEM_LIMIT = 55168 * 1024
WIDE, SPAN, PAD = 4, 10, 16


def legendre_pair(degree, points):
    below_poly = np.ones(points.shape)
    top_poly = points.copy()
    for step in range(2, degree + 1):
        below_poly, top_poly = (
            top_poly,
            ((2 * step - 1) * points * top_poly - (step - 1) * below_poly) / step,
        )
    return (below_poly, top_poly)


@functools.lru_cache(None)
def gll_tables(degree):
    nodes = -np.cos(np.pi * np.arange(degree + 1) / degree)
    for _ in range(100):
        below_poly, top_poly = legendre_pair(degree, nodes)
        nodes = nodes - (nodes * top_poly - below_poly) / ((degree + 1) * top_poly)
    at_nodes = legendre_pair(degree, nodes)[1]
    weights = 2.0 / (degree * (degree + 1) * at_nodes**2)
    count = degree + 1
    derivative = np.zeros((count, count))
    for target in range(count):
        for source in range(count):
            if target != source:
                derivative[target, source] = at_nodes[target] / (
                    at_nodes[source] * (nodes[target] - nodes[source])
                )
    derivative[0, 0] = -degree * (degree + 1) / 4.0
    derivative[degree, degree] = degree * (degree + 1) / 4.0
    stiffness = derivative.T @ (weights[:, None] * derivative)
    return (nodes, weights, stiffness)


def lagrange_matrix(fine_degree, coarse_degree):
    fine_nodes = gll_tables(fine_degree)[0]
    coarse_nodes = gll_tables(coarse_degree)[0]
    table = np.ones((fine_degree + 1, coarse_degree + 1))
    for column in range(coarse_degree + 1):
        for other in range(coarse_degree + 1):
            if other != column:
                table[:, column] *= (fine_nodes - coarse_nodes[other]) / (
                    coarse_nodes[column] - coarse_nodes[other]
                )
    return table


@functools.lru_cache(None)
def smoother(degree):
    stiffness = gll_tables(degree)[2]
    elements = 6
    size = elements * degree
    assembled = np.zeros((size, size))
    for element in range(elements):
        for row in range(degree + 1):
            for col in range(degree + 1):
                assembled[(element * degree + row) % size, (element * degree + col) % size] += (
                    stiffness[row, col]
                )
    diagonal = np.sqrt(np.diagonal(assembled))
    scaled = assembled / diagonal[:, None] / diagonal[None, :]
    positions = np.arange(size)
    vector = np.where(positions % 2 == 0, 1.0, -1.0) * (1.0 + positions / size)
    for _ in range(2000):
        vector = scaled @ vector
        vector = vector / np.sqrt(np.sum(vector * vector))
    high = float(np.sum(vector * (scaled @ vector)) / np.sum(vector * vector))
    low = 0.1 * high
    theta, delta = 0.5 * (high + low), 0.5 * (high - low)
    sigma = theta / delta
    rho1 = 1.0 / sigma
    rho2 = 1.0 / (2.0 * sigma - rho1)
    return theta, rho2 * rho1, 2.0 * rho2 / delta * theta


def level(degree):
    _, w, k = gll_tables(degree)
    t = w.copy()
    t[0] = t[-1] = w[0] + w[-1]
    s = np.diagonal(k).copy()
    s[0] = s[-1] = k[0, 0] + k[-1, -1]
    c = np.ones(degree + 1)
    c[0] = c[-1] = 0.5
    diag = (
        s[:, None, None] * t[None, :, None] * t[None, None, :]
        + t[:, None, None] * s[None, :, None] * t[None, None, :]
        + t[:, None, None] * t[None, :, None] * s[None, None, :]
    )
    return w, k, t, c, 1.0 / (diag * smoother(degree)[0])


def join_z(count):
    size = EZ * count
    m = np.eye(size)
    for e in range(EZ):
        a, b = e * count + count - 1, ((e + 1) % EZ) * count
        m[a, b] += 1.0
        m[b, a] += 1.0
    return m


def two(m):
    return np.kron(np.eye(2), m)


def lanes(values):
    return np.broadcast_to(values[None, :], (8, LANES))


def rows(values):
    return np.broadcast_to(np.asarray(values)[..., None], np.shape(values) + (LANES,))


def fourier_rows(total):
    k, n = np.meshgrid(np.arange(total), np.arange(total), indexing="ij")
    half = total // 2
    freq = np.where(k <= half, k, k - half)
    angle = 2.0 * np.pi * (freq * n % total) / total
    scale = np.where((k == 0) | (k == half), math.sqrt(1.0 / total), math.sqrt(2.0 / total))
    return scale * np.where(k <= half, np.cos(angle), np.sin(angle))


def sine_rows(mode, point, total):
    product = mode * point % (2 * total)
    inside = (mode > 0) & (mode < total) & (point > 0) & (point < total)
    return np.where(inside, math.sqrt(2.0 / total) * np.sin(np.pi * product / total), 0.0)


def green_table(nx, ny):
    mode = np.arange(MODES)
    wall_gap = 2.0 * np.sin(0.5 * np.pi * mode / ny) ** 2 + np.where(mode % ny == 0, 1.0, 0.0)
    freq = np.arange(EZ)
    freq = np.where(freq <= EZ // 2, freq, freq - EZ // 2)
    span_gap = 2.0 * np.sin(np.pi * freq / EZ) ** 2
    half_gap = wall_gap[:, None] + span_gap[None, :]
    root = np.sqrt(half_gap * (2.0 + half_gap))
    rate = np.log1p(half_gap + root)
    d = np.arange(nx)[:, None, None]
    top = np.exp(-rate * d) + np.exp(-rate * (nx - d))
    return top / (4.0 * root * -np.expm1(-rate * nx))


def modal(values):
    v = values.reshape(values.shape[:-2] + (MODES // 8, 8, EZ))
    v = np.stack([v, v], axis=-2)
    v = np.moveaxis(v, -4, -3)
    return v.reshape(v.shape[:-3] + (LANES,))


def offsets(radius):
    found = [(0, 0), *FACES]
    for ring in range(2, radius + 1):
        found += [
            (dx, dy)
            for dx in range(-ring, ring + 1)
            for dy in range(-ring, ring + 1)
            if abs(dx) + abs(dy) == ring
        ]
    return found


def assembled_1d(local_cols, window):
    count = local_cols.shape[0]
    out = np.zeros((count, window))
    out[:, 1:3] += local_cols
    out[0, 0:2] += local_cols[-1]
    out[-1, 2:4] += local_cols[0]
    return out


@functools.lru_cache(None)
def build_tables(nx, ny):
    f, q = ORDER + 1, MID_ORDER + 1
    w7, k7, t7, c7, e7 = level(ORDER)
    w3, k3, t3, c3, e3 = level(MID_ORDER)
    j73 = lagrange_matrix(ORDER, MID_ORDER)
    j31 = lagrange_matrix(MID_ORDER, 1)
    tile = {}
    tk = np.tile(t7, EZ)
    ones = np.ones((8, LANES))
    tile["kx"] = np.stack(
        [np.stack([k7[i, a] * t7[:, None] * tk[None, :] for i in range(f)]) for a in range(f)]
    ).reshape(f * f, 8, LANES)
    roll = np.stack([[k7[j, (j - s) % f] for j in range(f)] for s in range(f)])
    tile["ky"] = roll[:, :, None] * tk[None, None, :]
    tile["kyl"] = (k7[f - 1][:, None] * tk[None, :])[None]
    tile["kyf"] = (k7[0][:, None] * tk[None, :])[None]
    tile["e7"] = np.tile(e7, (1, 1, EZ))
    tile["ti"] = np.stack([t * ones for t in t7])
    tile["tij"] = np.stack([t * rows(t7) for t in t7])
    tile["cj"] = rows(c7)[None]
    tile["ci"] = np.stack([c * ones for c in c7])
    tile["jx"] = np.stack([j73[i, a] * ones for i in range(f) for a in range(q)])
    green = modal(green_table(nx, ny))
    tile["green"] = green[(np.arange(nx + SPAN - 1) - WIDE) % nx]
    point = np.arange(-WIDE, ny - WIDE + PAD)
    tile["sine"] = modal(
        np.broadcast_to(
            sine_rows(np.arange(MODES)[None, :], point[:, None], ny)[:, :, None],
            (len(point), MODES, EZ),
        )
    )
    row = {}
    mid = [(a, b) for a in range(q) for b in range(q)]
    tc = np.tile(np.tile(t3, EZ), 2)

    def left(matrix, scale=None):
        scale = np.ones(LANES) if scale is None else scale
        return matrix.T[:, :, None] * scale[None, None, :]

    row["jy"] = left(
        np.array([[(a == a2) * j73[j, b] for a2 in range(q) for j in range(f)] for a, b in mid])
    )
    row["lx"] = left(np.kron(k3, np.diag(t3)), tc)
    row["ly"] = left(np.kron(np.diag(t3), k3), tc)
    row["e3"] = np.stack([np.tile(np.tile(e3[a, b], EZ), 2) for a, b in mid])[None]
    row["tab"] = rows([t3[a] * t3[b] for a, b in mid])[None]
    row["ca"] = rows([c3[a] for a, b in mid])[None]
    row["cb"] = rows([c3[b] for a, b in mid])[None]
    groups = [np.array([j31[a, x] * j31[b, y] for a, b in mid]) for x in (0, 1) for y in (0, 1)]
    row["jj"] = np.repeat(np.stack(groups, axis=1), MODES, axis=1)[None]
    own = np.zeros((q, 4))
    own[:, 1:3] = j31
    stiff = assembled_1d(k3 @ j31, 4)
    mass = t3[:, None] * own

    ring1, ring2, ring3 = offsets(1), offsets(2), offsets(3)

    def placed(first, second, elements):
        out = np.zeros((len(elements), q, q, SPAN, PAD))
        for n, (dx, dy) in enumerate(elements):
            x0, y0 = dx - 1 + WIDE, dy - 1 + WIDE
            out[n, :, :, x0 : x0 + 4, y0 : y0 + 4] = np.einsum("at,bq->abtq", first, second)
        return out.reshape(len(elements) * q * q, SPAN * PAD)

    mat = {}
    mat["kt"] = np.concatenate(
        [placed(stiff, mass, ring3) + placed(mass, stiff, ring3), placed(own, own, ring2)])
    mat["tt"] = placed(mass, mass, ring3)
    cross = np.zeros((len(ring2), q, q, len(ring3), q, q))
    ends = {(1, 0): (3, 0), (-1, 0): (0, 3), (0, 1): (3, 0), (0, -1): (0, 3)}
    diag3 = np.diag(t3)
    for n, (dx, dy) in enumerate(ring2):
        cross[n, :, :, n] += np.einsum("ac,bd->abcd", k3, diag3)
        cross[n, :, :, n] += np.einsum("ac,bd->abcd", diag3, k3)
        for (fx, fy), (mine, theirs) in ends.items():
            m = ring3.index((dx + fx, dy + fy))
            line = np.zeros((q, q))
            line[mine] = k3[theirs]
            if fx:
                cross[n, :, :, m] += np.einsum("ac,bd->abcd", line, diag3)
            else:
                cross[n, :, :, m] += np.einsum("ac,bd->abcd", diag3, line)
    pick = np.zeros((len(ring1), q, q, 144))
    for n, (dx, dy) in enumerate(ring1):
        for gx, gy in AROUND:
            sx, sy = gx - dx, gy - dy
            if max(abs(sx), abs(sy)) > 1:
                continue
            span_x = [(a, a) for a in range(q)] if sx == 0 else [(q - 1, 0) if sx > 0 else (0, q - 1)]
            span_y = [(b, b) for b in range(q)] if sy == 0 else [(q - 1, 0) if sy > 0 else (0, q - 1)]
            for a, a2 in span_x:
                for b, b2 in span_y:
                    d = (gx, gy)
                    if d in ring1:
                        column = 16 * ring1.index(d) + 4 * a2 + b2
                    elif d in CORNERS:
                        part = (d[0] != d[1]) if sx else (d[0] == d[1])
                        column = 80 + 8 * CORNERS.index(d) + 4 * part + (b2 if sx else a2)
                    elif d in TWICE:
                        column = 112 + 4 * TWICE.index(d) + (b2 if sx else a2)
                    else:
                        column = 128 + KNIGHTS.index(d)
                    pick[n, a, b, column] = 1.0
    mat["pick"] = pick.reshape(len(ring1) * 16, 144)
    mat["lxy"] = cross.reshape(len(ring2) * 16, len(ring3) * 16)
    k7j = k7 @ j73
    t7j = t7[:, None] * j73
    fine = np.zeros((len(ring1), f, f, len(ring2), q, q))
    own_z = np.zeros((len(ring1), f, f, len(ring1), q, q))
    for n, (dx, dy) in enumerate(ring1):
        fine[n, :, :, n] += np.einsum("ia,jb->ijab", k7j, t7j) + np.einsum("ia,jb->ijab", t7j, k7j)
        own_z[n, :, :, n] = np.einsum("ia,jb->ijab", t7j, t7j)
        for (fx, fy), (mine, theirs) in ends.items():
            mine, theirs = (f - 1 if mine else 0), (f - 1 if theirs else 0)
            m = ring2.index((dx + fx, dy + fy))
            if fx:
                fine[n, mine, :, m] += np.einsum("a,jb->jab", k7j[theirs], t7j)
            else:
                fine[n, :, mine, m] += np.einsum("ia,b->iab", t7j, k7j[theirs])
    count = len(ring1) * f * f
    mat["fine"] = np.concatenate([fine.reshape(count, -1), own_z.reshape(count, -1)], axis=1)
    mat["lown"] = mat["lxy"][:16, : 16 * len(ring1)]
    mat["pfine"] = np.einsum("ia,jb->ijab", j73, j73).reshape(f * f, 16)
    row["tc"] = np.broadcast_to(tc, (1, 16, LANES))
    az7 = (join_z(f) @ np.kron(np.eye(EZ), k7)).T
    az3 = two((join_z(q) @ np.kron(np.eye(EZ), k3)).T)
    down = (join_z(q) @ np.kron(np.eye(EZ), j73.T) @ np.diag(np.tile(c7, EZ))).T
    zero = np.zeros_like(down)
    mat["az7"] = az7
    mat["down"] = np.concatenate(
        [np.concatenate([down, zero], axis=1), np.concatenate([zero, down], axis=1)], axis=0
    )
    mat["az3"] = az3
    up = np.kron(np.eye(EZ), j73).T
    mat["up"] = two(up)
    up_tk = up * np.tile(t7, EZ)[None]
    mat["upt"] = np.concatenate([two(up_tk), two(up @ az7)], axis=1)
    gather = np.zeros((EZ, EZ * q))
    for e in range(EZ):
        for node in (0, 1):
            gather[(e + node) % EZ, e * q : (e + 1) * q] += j31[:, node] * c3
    b1 = two((fourier_rows(EZ) @ gather).T)
    b1 = np.tile(b1, (1, 4))
    mat["b12"] = np.concatenate([b1, az3 @ b1], axis=0)
    spread = np.zeros((EZ * q, EZ))
    for e in range(EZ):
        for node in (0, 1):
            spread[e * q : (e + 1) * q, (e + node) % EZ] += j31[:, node]
    back = two((spread @ fourier_rows(EZ).T).T)
    back = np.tile(back, (4, 1))
    mat["back"] = np.concatenate([back, back @ az3], axis=1)
    mode, here = np.arange(MODES)[:, None], np.arange(32)[None, :]
    s0 = np.where(here < ny, sine_rows(mode, here, ny), 0.0)
    s1 = np.where(here < ny, sine_rows(mode, here + 1, ny), 0.0)
    mat["sin"] = np.concatenate([s0, s1], axis=0)
    where, tiles, at = {}, [], 0
    for name in EARLY + LATE + tuple(row):
        value = tile[name] if name in tile else row[name].reshape(-1, 8, LANES)
        where[name] = (at, value.shape[0])
        tiles.append(value.astype(np.float32))
        at += value.shape[0]
    blocks, at = [], 0
    for name in MATS:
        value = mat[name].astype(np.float32)
        top = value.astype(ml_dtypes.bfloat16)
        rest = (value - top.astype(np.float32)).astype(ml_dtypes.bfloat16)
        parts = [top, top] if name == "pick" else [top, rest, top]
        value = np.concatenate(parts, axis=0 if name in RIGHT else 1)
        height, width = value.shape
        count = -(-width // LANES)
        value = np.pad(value, ((0, 0), (0, count * LANES - width)))
        where[name] = (at, height, width)
        blocks += [value[:, LANES * n : LANES * n + LANES] for n in range(count)]
        at += height * count
    return np.concatenate(tiles), np.concatenate(blocks), where


EARLY = ("e7", "kx", "kyl", "kyf", "ti", "ky", "tij")
LATE = ("cj", "ci", "jx", "green", "sine")
RIGHT = ("az7", "down", "az3", "b12", "back", "up", "upt")
MATS = ("az7", "down", "pick", "lown", "az3", "b12", "sin", "back", "kt", "tt", "lxy", "up", "upt",
        "fine", "pfine")
LINKS = 20 + 4 + 20 + 4 + 12 + 4 + 24


def reach(n):
    base = max(n // 8, 1)
    known, hops = base, []
    while known < n // 2:
        hops.append(known)
        known *= 2
    return range(1, base + 1), hops


def mean_hops(d, size):
    def ring(a, b):
        return min((a - b) % 4, (b - a) % 4)

    total = 0
    for p in range(size):
        t = (p + d) % size
        total += ring(p // 8, t // 8) + ring(p // 2 % 4, t // 2 % 4) + 0.5 * (p % 2 != t % 2)
    return total


def kernel(nx, ny, where, *refs):
    hbm, out_ref, vmem = refs[:3], refs[3], refs[4:7]
    (pair_send, pair_recv, edge_send, corner_recv, twice_recv, knight_send, knight_recv, g3_all,
     edge3_send, corner3_recv, twice3_recv, knight3_send, knight3_recv, line7_send, line7_recv,
     fine_send, fine_recv, mid_send, mid_recv, line_send, line_recv, mode_send, mode_recv,
     rest3_all, x3_all, load_sem, send_sem, recv_sem, known) = refs[7:]
    sx, cx = lax.axis_index("stream"), lax.axis_index("cross")
    tile_ref, block_ref = vmem[1:]

    def at(dx, dy):
        return {"stream": lax.rem(sx + (nx + dx), nx), "cross": lax.rem(cx + (ny + dy), ny)}

    def tab(name):
        start, size = where[name]
        return tile_ref[start : start + size]

    def rtab(name):
        return tab(name).reshape(-1, 16, LANES)

    def mat(name):
        start, height, width = where[name]
        parts = [block_ref[start + n * height : start + (n + 1) * height]
                 for n in range(-(-width // LANES))]
        return (parts[0] if len(parts) == 1 else jnp.concatenate(parts, axis=1))[:, :width]

    bar = pltpu.get_barrier_semaphore()
    faces = FACES
    near_x, hops_x = reach(nx)
    near_y, hops_y = reach(ny)
    near = list(KNIGHTS + CORNERS)
    near += [(s * d, 0) for d in reversed(near_x) for s in (1, -1)]
    near += [(0, s * d) for d in reversed(near_y) for s in (1, -1)]
    for d in near:
        pl.semaphore_signal(bar, inc=1, device_id=at(*d), device_id_type=MESH_ID)
    late, last = where[LATE[0]][0], where["sin"][0]
    spans = {"x": (0, 0, 128), "early": (1, 0, late), "late": (1, late, hbm[1].shape[0]),
             "first": (2, 0, last), "last": (2, last, hbm[2].shape[0])}
    loads = {}

    def load(*wanted):
        for name in wanted:
            operand, start, end = spans[name]
            part = pl.ds(start, end - start)
            loads[name] = pltpu.make_async_copy(
                hbm[operand].at[part], vmem[operand].at[part], load_sem.at[list(spans).index(name)])
            loads[name].start()

    load("x", "early")

    def need(*wanted):
        for name in wanted:
            if name in loads:
                loads.pop(name).wait()

    def tell(step):
        for n, hops in enumerate((hops_x, hops_y)):
            if step < len(hops):
                for s in (1, -1):
                    d = (s * hops[step], 0) if n == 0 else (0, s * hops[step])
                    pl.semaphore_signal(
                        known.at[step, n], inc=1, device_id=at(*d), device_id_type=MESH_ID)

    def told(step):
        for n, hops in enumerate((hops_x, hops_y)):
            if step < len(hops):
                pl.semaphore_wait(known.at[step, n], 2)

    used = [0]

    class Group:
        def __init__(self, size):
            self.base, self.copies = used[0], []
            used[0] += size

        def make(self, n, src, dst, device):
            return pltpu.make_async_remote_copy(
                src, dst, send_sem.at[self.base + n], recv_sem.at[self.base + n],
                device_id=device, device_id_type=MESH_ID)

        def start(self, src, dst, to):
            copy = self.make(len(self.copies), src, dst, at(*to))
            copy.start()
            self.copies.append(copy)

        def arrived(self):
            for copy in self.copies:
                copy.wait_recv()

        def left(self):
            for copy in self.copies:
                copy.wait_send()

    jrow = lax.broadcasted_iota(jnp.int32, (8, LANES), 0)
    lane = lax.broadcasted_iota(jnp.int32, (8, LANES), 1)
    low_wall = jnp.where(cx == 0, 0, -1)
    high_wall = jnp.where(cx == ny - 1, ORDER, -1)
    keep7 = jnp.where((jrow == low_wall) | (jrow == high_wall), 0.0, 1.0)
    mrow = lax.broadcasted_iota(jnp.int32, (16, LANES), 0)
    brow = lax.rem(mrow, 4)
    high_wall3 = jnp.where(cx == ny - 1, MID_ORDER, -1)
    keep3 = jnp.where((brow == low_wall) | (brow == high_wall3), 0.0, 1.0)
    _, keep_f, gain_f = smoother(ORDER)
    _, keep_m, gain_m = smoother(MID_ORDER)

    def halves(a):
        top = a.astype(jnp.bfloat16)
        return top, (a - top.astype(jnp.float32)).astype(jnp.bfloat16)

    def rdot(a, name):
        top, rest = halves(a)
        return jnp.dot(jnp.concatenate([top, top, rest], axis=1), mat(name),
                       preferred_element_type=jnp.float32)

    def ldot(name, b):
        top, rest = halves(b)
        parts = [top, rest] if name == "pick" else [top, top, rest]
        return jnp.dot(mat(name), jnp.concatenate(parts, axis=0),
                       preferred_element_type=jnp.float32)

    def fine_xy(u):
        kx = tab("kx").reshape(8, 8, 8, LANES)
        ax = kx[0][None] * u[:, 0:1]
        for a in range(1, 8):
            ax = ax + kx[a][None] * u[:, a : a + 1]
        ky = tab("ky")
        flat = u.reshape(16, 8, LANES)
        ay = ky[0][None] * flat
        for s in range(1, 8):
            ay = ay + ky[s][None] * pltpu.roll(flat, s, 1)
        return ax, ay.reshape(2, 8, 8, LANES) * tab("ti")[None]

    def fine_z(u):
        az = rdot(u.reshape(128, LANES), "az7")
        return az.reshape(2, 8, 8, LANES) * tab("tij")[None]

    def fine_send_faces(ax, ay):
        fine_send[0] = ax[:, 7].reshape(16, LANES)
        fine_send[1] = ax[:, 0].reshape(16, LANES)
        flat = ay.reshape(16, 8, LANES)
        fine_send[2] = flat[:, 7, :]
        fine_send[3] = flat[:, 0, :]
        group = Group(4)
        for d in range(4):
            group.start(fine_send.at[d], fine_recv.at[d], faces[d])
        return group

    def add_x(field, low, high):
        return jnp.concatenate(
            [field[:, 0:1] + low.reshape(2, 1, 8, LANES), field[:, 1:7],
             field[:, 7:8] + high.reshape(2, 1, 8, LANES)], axis=1)

    def add_y(field, low, high):
        flat = field.reshape(16, 8, LANES)
        flat = flat + jnp.where(jrow[None] == 0, low[:, None, :], 0.0)
        flat = flat + jnp.where(jrow[None] == 7, high[:, None, :], 0.0)
        return flat.reshape(2, 8, 8, LANES)

    def fine_join(group, field):
        group.arrived()
        field = add_x(field, fine_recv[0], fine_recv[1])
        return add_y(field, fine_recv[2], fine_recv[3])

    def left(name, v):
        start_row, size = where[name]
        acc = 0.0
        for c in range(size // 2):
            both = tile_ref[start_row + 2 * c : start_row + 2 * c + 2].reshape(16, LANES)
            acc = acc + both * v[c : c + 1]
        return acc

    def mid_start(ax, ay):
        mid_send[0] = ax
        mid_send[1] = ay
        group = Group(4)
        for d in range(4):
            group.start(mid_send.at[d // 2], mid_recv.at[d], faces[d])
        return group

    def shifted(v, shift, mask):
        return jnp.where(mask, pltpu.roll(v, shift, 0), 0.0)

    def mid_join(group, field):
        group.arrived()
        field = field + shifted(mid_recv[0], 4, mrow < 4)
        field = field + shifted(mid_recv[1], 12, mrow >= 12)
        field = field + shifted(mid_recv[2], 13, brow == 0)
        return field + shifted(mid_recv[3], 3, brow == 3)

    def masked(dy, table, top, index):
        low = jnp.where(cx + dy == 0, 0, -1)
        high = jnp.where(cx + dy == ny - 1, top, -1)
        return table * jnp.where((index == low) | (index == high), 0.0, 1.0)

    def along_x(u, row):
        acc = kx[0][row][None] * u[:, 0]
        for a in range(1, 8):
            acc = acc + kx[a][row][None] * u[:, a]
        return acc.reshape(16, LANES)

    def along_y(u, table):
        weighted = jnp.sum(table[None] * u, axis=2)
        return (tab("ti")[:, 0][None] * weighted).reshape(16, LANES)

    need("x")
    src = vmem[0][...].reshape(16, 8, LANES)
    knode = lax.rem(lane, 8)
    src = (src + jnp.where(knode[None] == 7, pltpu.roll(src, LANES - 1, 2), 0.0)
           + jnp.where(knode[None] == 0, pltpu.roll(src, 1, 2), 0.0))
    y7, y0 = src[:, 7, :], src[:, 0, :]
    src = src.reshape(2, 8, 8, LANES)
    x7, x0 = src[:, 7].reshape(16, LANES), src[:, 0].reshape(16, LANES)
    for n, edge in enumerate((x7, y7, x0, y0, x7)):
        edge_send[n] = edge
    for i, row in ((1, 7), (0, 0)):
        for j, line in ((1, y7), (0, y0)):
            knight_send[2 * i + j] = line.reshape(2, 8, LANES)[:, row : row + 1]
    need("early")
    e7 = masked(0, tab("e7"), ORDER, jrow[None])
    kx = tab("kx").reshape(8, 8, 8, LANES)
    ky_last, ky_first = tab("kyl"), tab("kyf")
    scaled = e7[None] * src
    pairs = ((x0, along_x(scaled, 0)), (x7, along_x(scaled, 7)),
             (y0, along_y(scaled, ky_first)), (y7, along_y(scaled, ky_last)))
    for n, (raw, contracted) in enumerate(pairs):
        pair_send[n, 0] = raw
        pair_send[n, 1] = contracted
    pl.semaphore_wait(bar, len(near))
    tell(0)
    first = [Group(size) for size in (8, 4, 4, 4)]
    for n, (dx, dy) in enumerate(KNIGHTS):
        first[0].start(knight_send.at[2 * (dx < 0) + (dy < 0)], knight_recv.at[n], (-dx, -dy))
    pick_edge = {(1, 1): 2, (1, -1): 1, (-1, 1): 3, (-1, -1): 0}
    for n, d in enumerate(CORNERS):
        first[1].start(edge_send.at[pick_edge[d] : pick_edge[d] + 2], corner_recv.at[n],
                       (-d[0], -d[1]))
    for n, (dx, dy) in enumerate(TWICE):
        first[2].start(edge_send.at[(2, 0, 3, 1)[n]], twice_recv.at[n], (-dx, -dy))
    for n, (dx, dy) in enumerate(FACES):
        first[3].start(pair_send.at[n], pair_recv.at[n], (-dx, -dy))
    load("first", "late")
    need("first")
    for group in first:
        group.arrived()
    told(0)
    tell(1)
    irow = jrow[None]

    def lines_of(value):
        return value.reshape(2, 8, LANES)

    def row_of(value, row):
        return lines_of(value)[:, row : row + 1]

    def with_ends(line, first, last):
        line = lines_of(line) + jnp.where(irow == 0, first, 0.0) + jnp.where(irow == 7, last, 0.0)
        return line.reshape(16, LANES)

    knight = {d: knight_recv[n] for n, d in enumerate(KNIGHTS)}
    twice = {d: twice_recv[n] for n, d in enumerate(TWICE)}
    raw = {d: pair_recv[n, 0] for n, d in enumerate(FACES)}
    corner_x = {d: corner_recv[n, 0 if d[0] == d[1] else 1] for n, d in enumerate(CORNERS)}
    corner_y = {d: corner_recv[n, 1 if d[0] == d[1] else 0] for n, d in enumerate(CORNERS)}

    def joined(center, low_x, high_x, low_y, high_y):
        return add_y(add_x(center, low_x, high_x), low_y, high_y)

    b7 = joined(
        src, raw[-1, 0], raw[1, 0],
        with_ends(raw[0, -1], row_of(corner_y[-1, -1], 7), row_of(corner_y[1, -1], 0)),
        with_ends(raw[0, 1], row_of(corner_y[-1, 1], 7), row_of(corner_y[1, 1], 0)))
    zero = jnp.zeros_like(src)
    extra = {
        (1, 0): joined(
            zero, x7, twice[2, 0],
            with_ends(corner_y[1, -1], row_of(raw[0, -1], 7), knight[2, -1]),
            with_ends(corner_y[1, 1], row_of(raw[0, 1], 7), knight[2, 1])),
        (-1, 0): joined(
            zero, twice[-2, 0], x0,
            with_ends(corner_y[-1, -1], knight[-2, -1], row_of(raw[0, -1], 0)),
            with_ends(corner_y[-1, 1], knight[-2, 1], row_of(raw[0, 1], 0))),
        (0, 1): joined(
            zero, corner_x[-1, 1], corner_x[1, 1],
            with_ends(y7, row_of(raw[-1, 0], 7), row_of(raw[1, 0], 7)),
            with_ends(twice[0, 2], knight[-1, 2], knight[1, 2])),
        (0, -1): joined(
            zero, corner_x[-1, -1], corner_x[1, -1],
            with_ends(twice[0, -2], knight[-1, -2], knight[1, -2]),
            with_ends(y0, row_of(raw[-1, 0], 0), row_of(raw[1, 0], 0))),
    }
    e7_of = {0: e7}
    for dy in (1, -1):
        e7_of[dy] = masked(dy, tab("e7"), ORDER, jrow[None])
    extra = {d: e7_of[d[1]][None] * v for d, v in extra.items()}

    u1 = e7[None] * b7
    ax, ay = fine_xy(u1)
    au = add_x(ax + ay + fine_z(u1), pair_recv[1, 1] + along_x(extra[-1, 0], 7),
               pair_recv[0, 1] + along_x(extra[1, 0], 0))
    au = add_y(au, pair_recv[3, 1] + along_y(extra[0, -1], ky_last),
               pair_recv[2, 1] + along_y(extra[0, 1], ky_first))
    r1 = b7 - au
    x7 = (1.0 + keep_f) * u1 + gain_f * (e7[None] * r1)
    ax, ay = fine_xy(x7)
    side7 = fine_send_faces(ax, ay)
    az = fine_z(x7)
    local7 = ax + ay + az
    need("late")
    ci = tab("ci")[None]
    rest7 = (src - tab("cj")[None] * (ax + ci * az) - ci * ay) * keep7[None, None]
    jx = tab("jx").reshape(8, 4, 8, LANES)
    g = jx[0][None] * rest7[:, 0:1]
    for i in range(1, 8):
        g = g + jx[i][None] * rest7[:, i : i + 1]
    g = jnp.concatenate([g[0].reshape(32, LANES), g[1].reshape(32, LANES)], axis=1)
    g3 = left("jy", rdot(g, "down"))
    g3_all[0] = g3
    by_a = g3.reshape(4, 4, LANES)
    for n, edge in enumerate((by_a[3], by_a[:, 3], by_a[0], by_a[:, 0], by_a[3])):
        edge3_send[n] = edge
    for i, row in ((1, 12), (0, 0)):
        for j in (0, 1):
            knight3_send[2 * i + j] = g3[row + 3 * j : row + 3 * j + 1]
    wide = Group(len(AROUND) - 1)
    for n, (dx, dy) in enumerate(KNIGHTS):
        wide.start(knight3_send.at[2 * (dx < 0) + (dy < 0)], knight3_recv.at[n], (-dx, -dy))
    for n, d in enumerate(CORNERS):
        wide.start(edge3_send.at[pick_edge[d] : pick_edge[d] + 2], corner3_recv.at[n],
                   (-d[0], -d[1]))
    for n, (dx, dy) in enumerate(TWICE):
        wide.start(edge3_send.at[(2, 0, 3, 1)[n]], twice3_recv.at[n], (-dx, -dy))
    for n, (dx, dy) in enumerate(FACES):
        wide.start(g3_all.at[0], g3_all.at[n + 1], (-dx, -dy))
    load("last")
    rest7 = b7 - fine_join(side7, local7)
    scaled = e7[None] * rest7
    line7_send[0] = along_x(scaled, 0)
    line7_send[1] = along_x(scaled, 7)
    line7_send[2] = along_y(scaled, ky_first)
    line7_send[3] = along_y(scaled, ky_last)
    told(1)
    ring1, ring2, ring3 = offsets(1), offsets(2), offsets(3)
    e3 = {dy: masked(dy, rtab("e3")[0], MID_ORDER, brow) for dy in range(-3, 4)}
    e3_all = jnp.concatenate([e3[dy] for _, dy in ring3], axis=0)
    tc, tab3 = rtab("tc")[0], rtab("tab")[0]
    n1, n2, n3 = 16 * len(ring1), 16 * len(ring2), 16 * len(ring3)

    def mid_z(v):
        return tab3 * rdot(v, "az3")

    wide.arrived()

    b3 = ldot("pick", jnp.concatenate(
        [g3_all[...].reshape(80, LANES), corner3_recv[...].reshape(32, LANES),
         twice3_recv[...].reshape(16, LANES), knight3_recv[:, 0, :],
         jnp.zeros((8, LANES), jnp.float32)], axis=0))
    v1 = e3_all[:n1] * b3
    b3, e3 = b3[:16], e3[0]
    r1 = b3 - tc * ldot("lown", v1) - mid_z(v1[:16])
    x3 = (1.0 + keep_m) * v1[:16] + gain_m * (e3 * r1)
    ax, ay = left("lx", x3), left("ly", x3)
    ca, cb = rtab("ca")[0], rtab("cb")[0]
    part = keep3 * (g3 - cb * ax - ca * ay)
    other = keep3 * (ca * cb * tab3) * x3
    line = rdot(jnp.concatenate([part, -other], axis=1), "b12")
    line = jnp.sum(rtab("jj")[0] * line, axis=0, keepdims=True)
    line_send[0] = line

    lines = Group(ny)

    def line_copy(d, slot, to):
        return lines.make(d, line_send.at[0], line_recv.at[slot], {"cross": to})

    def far_first(n, size):
        step = lax.div(n + 1, 2)
        return size // 2 + step * (1 - 2 * lax.rem(n, 2))

    def line_left(d, carry):
        line_copy(d, cx, cx).wait_send()
        return carry

    def line_arrived(n, carry):
        d = far_first(ny - 2 - n, ny)
        line_copy(d, lax.rem(cx + ny - d, ny), cx).wait_recv()
        return carry

    for n in range(ny - 1):
        d = ny // 2 + (n + 1) // 2 * (1 - 2 * (n % 2))
        line_copy(d, cx, lax.rem(cx + d, ny)).start()
    line_recv[cx] = line
    side3 = mid_start(ax, ay)
    x3_all[0] = x3
    side = [Group(len(ring) - 1) for ring in (ring2, ring1, ring3)]
    for n, (dx, dy) in enumerate(ring2):
        if n:
            side[0].start(x3_all.at[0], x3_all.at[n], (-dx, -dy))
    for n, (dx, dy) in enumerate(FACES):
        side[1].start(line7_send.at[n], line7_recv.at[n], (-dx, -dy))
    if ny < 32:
        line_recv[ny:] = jnp.zeros((32 - ny, 1, LANES), jnp.float32)
    rest3_all[0] = b3 - mid_join(side3, ax + ay + mid_z(x3))
    for n, (dx, dy) in enumerate(ring3):
        if n:
            side[2].start(rest3_all.at[0], rest3_all.at[n], (-dx, -dy))
    need("last")
    for group in first + [wide, side7]:
        group.left()
    lax.fori_loop(1, ny, line_left, 0)
    lax.fori_loop(0, ny - 1, line_arrived, 0)
    spectrum = ldot("sin", line_recv[:, 0, :])
    group = lax.div(lane, 32)
    for alpha in range(2):
        total = jnp.zeros((8, LANES), jnp.float32)
        for hi in range(4):
            for beta in range(2):
                piece = spectrum[(beta * 4 + hi) * 8 : (beta * 4 + hi + 1) * 8]
                shift = 32 * (hi - 2 * alpha - beta) % LANES
                if shift:
                    piece = pltpu.roll(piece, shift, 1)
                total = total + jnp.where(group == hi, piece, 0.0)
        mode_send[alpha] = total

    modes = Group(nx)

    def mode_copy(d, to):
        return modes.make(d, mode_send, mode_recv.at[d], {"stream": to})

    def mode_left(d, carry):
        mode_copy(d, sx).wait_send()
        return carry

    by_hops = sorted(range(1, nx), key=lambda d: mean_hops(d, nx))
    for d in reversed(by_hops):
        mode_copy(d, lax.rem(sx + d, nx)).start()
    mode_recv[0] = mode_send[...]
    for group in side:
        group.arrived()
    for group in [side3] + side:
        group.left()
    lax.fori_loop(1, nx, mode_left, 0)
    for d in by_hops:
        mode_copy(d, sx).wait_recv()
    first = mode_recv[:, 0]
    second = mode_recv[:, 1]
    nodes = first + jnp.concatenate([second[1:], second[:1]], axis=0)
    start_g = where["green"][0]
    solved = [jnp.sum(tile_ref[start_g + n : start_g + n + nx] * nodes, axis=0)
              for n in range(SPAN)]
    sine = tile_ref[pl.ds(where["sine"][0] + cx, SPAN)]
    blank = jnp.zeros((PAD - SPAN, LANES), jnp.float32)
    window = []
    for s in solved:
        window += [jnp.sum(sine * s[None], axis=1), blank]
    window = jnp.concatenate(window, axis=0)
    window = rdot(window, "back")
    zval, zstiff = window[:, :LANES], window[:, LANES:]

    def per(table, count):
        return jnp.concatenate([table] * count, axis=0)

    from_low = ldot("kt", zval)
    r0 = rest3_all[...].reshape(n3, LANES) - per(tc, len(ring3)) * from_low[:n3]
    r0 = r0 - ldot("tt", zstiff)
    w1 = e3_all * r0
    aw = per(tc, len(ring2)) * ldot("lxy", w1)
    aw = aw + per(tab3, len(ring2)) * rdot(w1[:n2], "az3")
    x3 = x3_all[...].reshape(n2, LANES) + from_low[n3:]
    x3 = x3 + (1.0 + keep_m) * w1[:n2] + gain_m * (e3_all[:n2] * (r0[:n2] - aw))

    raised = rdot(x3, "upt")
    apx = ldot("fine", jnp.concatenate(
        [raised[:, : 2 * LANES], raised[:n1, 2 * LANES :]], axis=0))
    px = rdot(x3[:16], "up")
    px = jnp.stack([ldot("pfine", px[:, r * LANES : (r + 1) * LANES]) for r in range(2)])
    px = px.reshape(2, 8, 8, LANES)
    moved = []
    for n in range(len(ring1)):
        mine = apx[64 * n : 64 * n + 64]
        mine = jnp.stack([mine[:, r * LANES : (r + 1) * LANES] for r in range(2)])
        moved.append(mine.reshape(2, 8, 8, LANES))
    r0 = rest7 - moved[0]
    u1 = e7[None] * r0
    right, left_, above, below = [e7_of[dy][None] * moved[n + 1] for n, (_, dy) in enumerate(FACES)]
    ax, ay = fine_xy(u1)
    au = ax + ay + fine_z(u1)
    au = add_x(au, line7_recv[1] - along_x(left_, 7), line7_recv[0] - along_x(right, 0))
    au = add_y(au, line7_recv[3] - along_y(below, ky_last),
               line7_recv[2] - along_y(above, ky_first))
    x7 = x7 + px
    out = x7 + (1.0 + keep_f) * u1 + gain_f * (e7[None] * (r0 - au))
    out_ref[...] = out.reshape(128, LANES)


def solution(mesh):
    nx, ny = mesh.shape["stream"], mesh.shape["cross"]
    tiles, blocks, where = build_tables(nx, ny)

    def body(sources):
        flat = sources.reshape(128, LANES)
        operands = [flat, jnp.asarray(tiles), jnp.asarray(blocks)]
        links, f32 = pltpu.SemaphoreType.DMA, jnp.float32
        out = pl.pallas_call(
            functools.partial(kernel, nx, ny, where),
            out_shape=jax.ShapeDtypeStruct((128, LANES), jnp.float32),
            in_specs=[pl.BlockSpec(memory_space=pl.ANY)] * len(operands),
            out_specs=pl.BlockSpec(memory_space=pltpu.VMEM),
            scratch_shapes=[pltpu.VMEM(o.shape, o.dtype) for o in operands]
            + [
                pltpu.VMEM((4, 2, 16, LANES), f32),
                pltpu.VMEM((4, 2, 16, LANES), f32),
                pltpu.VMEM((5, 16, LANES), f32),
                pltpu.VMEM((4, 2, 16, LANES), f32),
                pltpu.VMEM((4, 16, LANES), f32),
                pltpu.VMEM((4, 2, 1, LANES), f32),
                pltpu.VMEM((8, 2, 1, LANES), f32),
                pltpu.VMEM((5, 16, LANES), f32),
                pltpu.VMEM((5, 4, LANES), f32),
                pltpu.VMEM((4, 2, 4, LANES), f32),
                pltpu.VMEM((4, 4, LANES), f32),
                pltpu.VMEM((4, 1, LANES), f32),
                pltpu.VMEM((8, 1, LANES), f32),
                pltpu.VMEM((4, 16, LANES), f32),
                pltpu.VMEM((4, 16, LANES), f32),
                pltpu.VMEM((4, 16, LANES), f32),
                pltpu.VMEM((4, 16, LANES), f32),
                pltpu.VMEM((2, 16, LANES), f32),
                pltpu.VMEM((4, 16, LANES), f32),
                pltpu.VMEM((1, 1, LANES), f32),
                pltpu.VMEM((32, 1, LANES), f32),
                pltpu.VMEM((2, 8, LANES), f32),
                pltpu.VMEM((nx, 2, 8, LANES), f32),
                pltpu.VMEM((len(offsets(3)), 16, LANES), f32),
                pltpu.VMEM((len(offsets(2)), 16, LANES), f32),
                links((5,)),
                links((LINKS + nx + ny,)),
                links((LINKS + nx + ny,)),
                pltpu.SemaphoreType.REGULAR((2, 2)),
            ],
            compiler_params=pltpu.CompilerParams(
                collective_id=0, has_side_effects=True, vmem_limit_bytes=VMEM_LIMIT),
            name="vcycle",
        )(*operands)
        return out.reshape(sources.shape)

    spec = P(None, "stream", "cross", None, None, None)
    return jax.shard_map(body, mesh=mesh, in_specs=(spec,), out_specs=spec, check_vma=False)
```
